32 devices in a mesh: lon: 8 (over z, y), lat: 4 (over x, core).
Axes of the slice: x: 2, y: 2, z: 4, core: 2. Of those that a mesh axis runs over, the one named last changes fastest.
Arguments:
- features: bfloat16 [8, 4, 16, 16, 128], P('lon', 'lat'), may hold values from -12 to 12
- conv_first: bfloat16 [3, 3, 128, 256], replicated, may hold values from -0.1875 to 0.1875
- conv_second: bfloat16 [3, 3, 256, 256], replicated, may hold values from -0.125 to 0.125
- cotangent: bfloat16 [8, 4, 8, 8, 256], P('lon', 'lat'), may hold values from -60 to 60
- edge_pick: int32 [8, 4, 2], P('lon', 'lat'), may hold values from 0 to 3
- edge_flip: int32 [8, 4, 2], P('lon', 'lat'), may hold values from 0 to 1
- corner_rule: int32 [8, 4, 4], P('lon', 'lat'), may hold values from 0 to 1
Outputs:
- pooled: bfloat16 [8, 4, 8, 8, 256], P('lon', 'lat')
- input_grad: bfloat16 [8, 4, 16, 16, 128], P('lon', 'lat')
- scaled_first: bfloat16 [3, 3, 128, 256], replicated
- scaled_second: bfloat16 [3, 3, 256, 256], replicated
The draws below stay inside these ranges and needn't reach their ends.
All inputs are finite; a program needn't handle non-finite values.
Results may differ from the reference program's by a relative error of at most 0.015.
Values may be sent and summed in bfloat16 or wider, within the bound.
No kernel may reach another device: no remote copies, remote signals or barrier semaphores. Data moves between devices by JAX's collectives and lax.ppermute only.
A program may use at most 64 MiB of HBM per device.

```python
import math
import jax
import jax.numpy as jnp
from jax import lax

C_IN = 128
C_OUT = 256
TILE = 16
TILES_LON = 8
TILES_LAT = 4
HALF = 8


def draw_features(key, part):
    scale_key, value_key = jax.random.split(key, 2)
    full_shape = (TILES_LON, TILES_LAT, TILE, TILE, C_IN)
    channel_scale = jnp.exp(jax.random.uniform(scale_key, (C_IN,), jnp.float32, math.log(0.3), math.log(3.0)))
    values = jax.random.truncated_normal(value_key, -4.0, 4.0, full_shape, jnp.float32)
    return (values * channel_scale).astype(jnp.bfloat16)


def draw_cotangent(key, part):
    scale_key, value_key = jax.random.split(key, 2)
    full_shape = (TILES_LON, TILES_LAT, HALF, HALF, C_OUT)
    channel_scale = jnp.exp(jax.random.uniform(scale_key, (C_OUT,), jnp.float32, math.log(0.3), math.log(3.0)))
    position = jnp.arange(TILES_LON).astype(jnp.float32) / (TILES_LON - 1)
    ramp_up = 1.0 + 2.0 * position
    values = jax.random.truncated_normal(value_key, -4.0, 4.0, full_shape, jnp.float32)
    values = values * channel_scale * ramp_up[:, None, None, None, None]
    return values.astype(jnp.bfloat16)


def set_ends(result, stream_key, smallest, top_value):
    extent = result.shape
    index_at = [jax.random.randint(jax.random.fold_in(stream_key, axis), (), 0, extent[axis]) for axis in range(len(extent))]
    result = result.at[tuple(index_at)].set(smallest)
    longest = extent.index(max(extent))
    index_at[longest] = (index_at[longest] + 1) % extent[longest]
    return result.at[tuple(index_at)].set(top_value)


def scatter_about(rng, dims, scale, reach, kind=jnp.bfloat16):
    values = scale * jax.random.normal(rng, dims, jnp.float32)
    return jnp.clip(values, min=-reach, max=reach).astype(kind)


def setup_inputs(seed: int = 0) -> dict:
    streams_of = jax.random.split(jax.random.key(seed), 8)
    return {
        "features": draw_features(jax.random.fold_in(streams_of[7], 71), 0),
        "conv_first": scatter_about(streams_of[1], (3, 3, C_IN, C_OUT), (9 * C_IN) ** -0.5, 0.1875),
        "conv_second": scatter_about(streams_of[2], (3, 3, C_OUT, C_OUT), (9 * C_OUT) ** -0.5, 0.125),
        "cotangent": draw_cotangent(jax.random.fold_in(streams_of[7], 71), 0),
        "edge_pick": set_ends(jax.random.randint(streams_of[4], (TILES_LON, TILES_LAT, 2), 0, 4), jax.random.fold_in(streams_of[4], 1), 0, 3).astype(jnp.int32),
        "edge_flip": set_ends(jax.random.randint(streams_of[5], (TILES_LON, TILES_LAT, 2), 0, 2), jax.random.fold_in(streams_of[5], 1), 0, 1).astype(jnp.int32),
        "corner_rule": set_ends(jax.random.randint(streams_of[6], (TILES_LON, TILES_LAT, 4), 0, 2), jax.random.fold_in(streams_of[6], 1), 0, 1).astype(jnp.int32),
    }


def normal_cdf(values):
    return 0.5 * (1.0 + lax.erf(values * (1.0 / math.sqrt(2.0))))

def gelu_value(values):
    return values * normal_cdf(values)

def gelu_slope(values):
    return normal_cdf(values) + values * jnp.exp(-0.5 * values * values) * (1.0 / math.sqrt(2.0 * math.pi))

def edge_pack(square):
    return jnp.stack([square[0], square[-1], square[:, 0], square[:, -1]])

def pick_row(bundle, choose_edge, reverse_flag):
    chosen = jnp.zeros_like(bundle[0])
    for edge_id in range(4):
        chosen = jnp.where(choose_edge == edge_id, bundle[edge_id], chosen)
    return jnp.where(reverse_flag == 1, chosen[::-1], chosen)

def extend_rows(square, from_north, from_south, edge_picks, edge_flips):
    south_row = pick_row(from_south, edge_picks[0], edge_flips[0])
    north_row = pick_row(from_north, edge_picks[1], edge_flips[1])
    return jnp.concatenate([south_row[None], square, north_row[None]], axis=0)

def extend_cols(extended, west_column, east_column, corner_rules):
    padded = jnp.concatenate([west_column[:, None], extended, east_column[:, None]], axis=1)
    far_edge = padded.shape[0] - 1
    corner_spots = ((0, 0, 0, 1, 1, 0), (0, far_edge, 0, far_edge - 1, 1, far_edge), (far_edge, 0, far_edge, 1, far_edge - 1, 0), (far_edge, far_edge, far_edge, far_edge - 1, far_edge - 1, far_edge))
    for corner_id, corner_spot in enumerate(corner_spots):
        row_at, col_at, first_row, first_col, second_row, second_col = corner_spot
        blended = 0.5 * (padded[first_row, first_col] + padded[second_row, second_col])
        padded = padded.at[row_at, col_at].set(jnp.where(corner_rules[corner_id] == 1, blended, padded[row_at, col_at]))
    return padded

def twice_mapped(func):
    return jax.vmap(jax.vmap(func))

def halo_field(values, edge_pick, edge_flip, corner_rule):
    lon_count, lat_count = (values.shape[0], values.shape[1])
    bundles = twice_mapped(edge_pack)(values)
    blank_rows = jnp.zeros_like(bundles[:, :1])
    north_band = jnp.concatenate([bundles[:, 1:], blank_rows], axis=1)
    south_band = jnp.concatenate([blank_rows, bundles[:, :-1]], axis=1)
    across_pole = jnp.roll(bundles, lon_count // 2, axis=0)
    band_index = jnp.arange(lat_count)[None, :, None, None, None]
    from_north = jnp.where(band_index == lat_count - 1, across_pole, north_band)
    from_south = jnp.where(band_index == 0, across_pole, south_band)
    extended = twice_mapped(extend_rows)(values, from_north, from_south, edge_pick, edge_flip)
    west_column = jnp.roll(extended[:, :, :, -1], 1, axis=0)
    east_column = jnp.roll(extended[:, :, :, 0], -1, axis=0)
    return twice_mapped(extend_cols)(extended, west_column, east_column, corner_rule)

def halo_back(grad_pad, edge_pick, edge_flip, corner_rule):
    lon_count, lat_count, side_cells = (grad_pad.shape[0], grad_pad.shape[1], grad_pad.shape[2] - 2)
    blank_field = jnp.zeros((lon_count, lat_count, side_cells, side_cells, grad_pad.shape[4]), jnp.float32)
    _, pullback = jax.vjp(lambda field_in: halo_field(field_in, edge_pick, edge_flip, corner_rule), blank_field)
    return pullback(grad_pad)[0]

def convolve(padded, weight):
    tile_count, tile_width = (padded.shape[0], padded.shape[1] - 2)
    summed = jnp.zeros((tile_count * tile_width * tile_width, weight.shape[3]), jnp.float32)
    for shift_row in range(3):
        for shift_col in range(3):
            window = padded[:, shift_row:shift_row + tile_width, shift_col:shift_col + tile_width].reshape(tile_count * tile_width * tile_width, -1)
            summed = summed + jnp.dot(window, weight[shift_row, shift_col], preferred_element_type=jnp.float32)
    return summed.reshape(tile_count, tile_width, tile_width, -1)

def weight_grad(padded, gradient):
    tile_count, tile_width = (gradient.shape[0], gradient.shape[1])
    flat_grad = gradient.reshape(tile_count * tile_width * tile_width, -1)
    blocks = []
    for shift_row in range(3):
        for shift_col in range(3):
            window = padded[:, shift_row:shift_row + tile_width, shift_col:shift_col + tile_width].reshape(tile_count * tile_width * tile_width, -1)
            blocks.append(lax.dot_general(window, flat_grad, (((0,), (0,)), ((), ())), preferred_element_type=jnp.float32))
    return jnp.stack(blocks).reshape(3, 3, padded.shape[3], gradient.shape[3])

def input_side_grad(gradient, weight):
    tile_count, tile_width = (gradient.shape[0], gradient.shape[1])
    flat_grad = gradient.reshape(tile_count * tile_width * tile_width, -1)
    summed = jnp.zeros((tile_count, tile_width + 2, tile_width + 2, weight.shape[2]), jnp.float32)
    for shift_row in range(3):
        for shift_col in range(3):
            product = lax.dot_general(flat_grad, weight[shift_row, shift_col], (((1,), (1,)), ((), ())), preferred_element_type=jnp.float32)
            product = product.reshape(tile_count, tile_width, tile_width, -1)
            summed = summed + jnp.pad(product, ((0, 0), (shift_row, 2 - shift_row), (shift_col, 2 - shift_col), (0, 0)))
    return summed

def pool_cells(values):
    tile_count, tile_width, channels = (values.shape[0], values.shape[1], values.shape[3])
    grouped = values.reshape(tile_count, tile_width // 2, 2, tile_width // 2, 2, channels)
    return lax.optimization_barrier(jnp.sum(grouped, axis=(2, 4))) * 0.25

def expand_grad(values):
    tile_count, half_width, channels = (values.shape[0], values.shape[1], values.shape[3])
    spread = jnp.broadcast_to(values[:, :, None, :, None, :], (tile_count, half_width, 2, half_width, 2, channels))
    return spread.reshape(tile_count, 2 * half_width, 2 * half_width, channels) * 0.25

def reference(features, conv_first, conv_second, cotangent, edge_pick, edge_flip, corner_rule):
    features_pad = halo_field(features, edge_pick, edge_flip, corner_rule)
    first_pre = lax.map(lambda padded: convolve(padded, conv_first), features_pad)
    first_act = gelu_value(first_pre).astype(jnp.bfloat16)
    first_pad = halo_field(first_act, edge_pick, edge_flip, corner_rule)

    def second_step(running, inputs):
        padded, cot_rows = inputs
        second_pre = convolve(padded, conv_second)
        pooled_rows = pool_cells(gelu_value(second_pre)).astype(jnp.bfloat16)
        second_grad = (expand_grad(cot_rows.astype(jnp.float32)) * gelu_slope(second_pre)).astype(jnp.bfloat16)
        running = running + weight_grad(padded, second_grad)
        pad_grad = input_side_grad(second_grad, conv_second).astype(jnp.bfloat16)
        return (running, (pooled_rows, pad_grad))
    grad_second, (pooled, first_pad_grad) = lax.scan(second_step, jnp.zeros(conv_second.shape, jnp.float32), (first_pad, cotangent))
    first_grad = halo_back(first_pad_grad.astype(jnp.float32), edge_pick, edge_flip, corner_rule)

    def first_step(running, inputs):
        padded, upstream, pre_act = inputs
        pre_grad = (upstream * gelu_slope(pre_act)).astype(jnp.bfloat16)
        running = running + weight_grad(padded, pre_grad)
        return (running, input_side_grad(pre_grad, conv_first).astype(jnp.bfloat16))
    grad_first, features_pad_grad = lax.scan(first_step, jnp.zeros(conv_first.shape, jnp.float32), (features_pad, first_grad, first_pre))
    input_grad = halo_back(features_pad_grad.astype(jnp.float32), edge_pick, edge_flip, corner_rule).astype(jnp.bfloat16)
    squared = jnp.sum(grad_first * grad_first) + jnp.sum(grad_second * grad_second)
    norm_target = math.sqrt(9.0 * (conv_first.shape[2] + conv_first.shape[3]) * conv_first.shape[3])
    grad_norm = jnp.sqrt(squared + 1e-06)
    norm_scale = norm_target / grad_norm
    return (pooled, input_grad, (grad_first * norm_scale).astype(jnp.bfloat16), (grad_second * norm_scale).astype(jnp.bfloat16))
```

```python
import functools
import math

import jax
import jax.numpy as jnp
from jax import lax
from jax.experimental import pallas as pl
from jax.experimental.pallas import tpu as pltpu
from jax.sharding import PartitionSpec as P


BF = jnp.bfloat16
F32 = jnp.float32
ROWS_PER_STEP = 4


def normal_parts(z):
    cdf = 0.5 * (1.0 + lax.erf(z * (1.0 / math.sqrt(2.0))))
    pdf = jnp.exp(-0.5 * z * z) * (1.0 / math.sqrt(2.0 * math.pi))
    return cdf, pdf


class Ring:
    def __init__(self, slots, channels, table, info):
        self.slots, self.band = slots, slots // 2
        self.channels, self.info = channels, info
        place = lax.broadcasted_iota(jnp.int32, (slots, channels), 0)
        self.top = lax.rem(place, self.band) == self.band - 1
        self.bottom = lax.rem(place, self.band) == 0
        self.table = table

    def flag(self, column):
        return jnp.broadcast_to(self.table[:, column : column + 1], (self.slots, self.channels))

    def up(self, x):
        return pltpu.roll(x, self.slots - 1, 0)

    def down(self, x):
        return pltpu.roll(x, 1, 0)

    def across(self, x):
        return pltpu.roll(x, self.band, 0)

    def take(self, edges, side, to_source, to_slot):
        pick, flip = to_source(self.flag(side)), to_source(self.flag(2 + side))
        count = len(edges[0])
        chosen = [
            jnp.where(
                pick == 0.0,
                edges[0][j],
                jnp.where(
                    pick == 1.0, edges[1][j], jnp.where(pick == 2.0, edges[2][j], edges[3][j])
                ),
            )
            for j in range(count)
        ]
        return [
            to_slot(jnp.where(flip == 1.0, chosen[count - 1 - j], chosen[j])) for j in range(count)
        ]

    def halo_rows(self, edges):
        same = self.take(edges, 0, self.up, self.down)
        pole = self.take(edges, 0, self.across, self.across)
        south = [jnp.where(self.bottom, b, a) for a, b in zip(same, pole)]
        same = self.take(edges, 1, self.down, self.up)
        pole = self.take(edges, 1, self.across, self.across)
        north = [jnp.where(self.top, b, a) for a, b in zip(same, pole)]
        return south, north

    def give(self, totals, rows, side, to_source):
        pick, flip = to_source(self.flag(side)), to_source(self.flag(2 + side))
        count = len(rows)
        moved = [to_source(row) for row in rows]
        for j in range(count):
            value = jnp.where(flip == 1.0, moved[count - 1 - j], moved[j])
            for edge in range(4):
                share = jnp.where(pick == float(edge), value, 0.0)
                totals[edge][j] = share if totals[edge][j] is None else totals[edge][j] + share

    def halo_rows_back(self, south, north):
        totals = [[None] * len(south) for _ in range(4)]
        self.give(totals, [jnp.where(self.bottom, 0.0, x) for x in south], 0, self.up)
        self.give(totals, [jnp.where(self.bottom, x, 0.0) for x in south], 0, self.across)
        self.give(totals, [jnp.where(self.top, 0.0, x) for x in north], 1, self.down)
        self.give(totals, [jnp.where(self.top, x, 0.0) for x in north], 1, self.across)
        return totals

    def arrived(self, near_ref, far_ref):
        slots = self.slots
        near, far = near_ref[...].astype(F32), far_ref[...].astype(F32)
        to_east = self.info[3] == 1
        east, west = jnp.where(to_east, near, far), jnp.where(to_east, far, near)
        count = near.shape[0] // slots
        east = [east[i * slots : (i + 1) * slots] for i in range(count)]
        west = [west[i * slots : (i + 1) * slots] for i in range(count)]
        east = [jnp.where(self.info[1] == 1, self.across(x), x) for x in east]
        west = [jnp.where(self.info[2] == 1, self.across(x), x) for x in west]
        return east, west

    def packed(self, east_list, west_list, out_ref):
        east, west = jnp.concatenate(east_list, axis=0), jnp.concatenate(west_list, axis=0)
        out_ref[...] = jnp.where(self.info[3] == 1, east, west).astype(BF)


def split_cells(row, slots):
    return [row[j * slots : (j + 1) * slots] for j in range(row.shape[0] // slots)]


def extend_and_send(ring, side, ext_ref, send_ref):
    slots = ring.slots
    width = side * slots
    pair = 2 * slots
    first_col, last_col = [], []
    for i in range(side):
        first_col.append(ext_ref[1 + i, 0:pair].astype(F32)[:slots])
        last_col.append(ext_ref[1 + i, width - pair : width].astype(F32)[slots:])
    edges = [
        split_cells(ext_ref[1].astype(F32), slots),
        split_cells(ext_ref[side].astype(F32), slots),
        first_col,
        last_col,
    ]
    south, north = ring.halo_rows(edges)
    ext_ref[0] = jnp.concatenate(south, axis=0).astype(BF)
    ext_ref[side + 1] = jnp.concatenate(north, axis=0).astype(BF)
    ring.packed(
        [south[-1]] + last_col + [north[-1]], [south[0]] + first_col + [north[0]], send_ref
    )


def pad_columns(ring, side, ext_ref, near_ref, far_ref, pad_ref):
    slots = ring.slots
    width = side * slots
    east, west = ring.arrived(near_ref, far_ref)
    low, high = ext_ref[0].astype(F32), ext_ref[side + 1].astype(F32)
    blends = (
        (0, west, 0, 1, low[:slots]),
        (1, east, 0, 1, low[width - slots :]),
        (2, west, side + 1, side, high[:slots]),
        (3, east, side + 1, side, high[width - slots :]),
    )
    for corner, column, at, beside, along in blends:
        blended = (0.5 * (along + column[beside])).astype(BF).astype(F32)
        column[at] = jnp.where(ring.flag(4 + corner) == 1.0, blended, column[at])
    for i in range(side + 2):
        pad_ref[i] = jnp.concatenate([west[i], ext_ref[i].astype(F32), east[i]], axis=0).astype(BF)


def windows(pad_ref, ext_ref, start, rows, width, slots, channels):
    left = pad_ref[pl.ds(start, rows), 0:width, :]
    middle = ext_ref[pl.ds(start, rows), :, :]
    right = pad_ref[pl.ds(start, rows), 2 * slots : 2 * slots + width, :]
    return jnp.concatenate([left, middle, right], axis=-1).reshape(rows * width, 3 * channels)


def convolved(pad_ref, ext_ref, weight_ref, start, rows, width, slots, channels):
    total = None
    for dh in range(3):
        window = windows(pad_ref, ext_ref, start + dh, rows, width, slots, channels)
        part = jnp.dot(window, weight_ref[dh], preferred_element_type=F32)
        total = part if total is None else total + part
    return total


def clear_edges(wide_ref, shifted_ref, side, slots):
    width = side * slots
    for row in (0, 1, side + 2, side + 3):
        wide_ref[row] = jnp.zeros_like(wide_ref[row])
        shifted_ref[row] = jnp.zeros_like(shifted_ref[row])
    blank = jnp.zeros((side, 2 * slots, wide_ref.shape[2]), BF)
    wide_ref[2 : side + 2, 0 : 2 * slots] = blank
    wide_ref[2 : side + 2, width + 2 * slots :] = blank


def put_gradient(wide_ref, shifted_ref, row, value, slots):
    width = value.shape[0]
    wide_ref[row, 2 * slots : 2 * slots + width] = value.astype(BF)
    blank = jnp.zeros((slots, value.shape[1]), F32)
    shifted_ref[row] = jnp.concatenate([blank, value, blank], axis=0).astype(BF)


def convolved_back(
    ring, side, wide_ref, shifted_ref, weight_ref, out_ref, send_ref, west_ref, east_ref
):
    slots, channels = ring.slots, ring.channels
    width, padded = side * slots, (side + 2) * slots
    depth = wide_ref.shape[2]
    rows = 3

    def step(index, carry):
        start = index * rows
        total = None
        for dh in range(3):
            at = pl.ds(start + 2 - dh, rows)
            window = jnp.concatenate(
                [
                    wide_ref[at, 2 * slots : 2 * slots + padded, :],
                    shifted_ref[at, :, :],
                    wide_ref[at, 0:padded, :],
                ],
                axis=-1,
            ).reshape(rows * padded, 3 * depth)
            part = jnp.dot(window, weight_ref[dh], preferred_element_type=F32)
            total = part if total is None else total + part
        total = total.reshape(rows, padded, channels)
        out_ref[pl.ds(start, rows)] = total[:, slots : slots + width].astype(BF)
        west_ref[pl.ds(start, rows)] = total[:, :slots].astype(BF).astype(F32)
        east_ref[pl.ds(start, rows)] = total[:, slots + width :].astype(BF).astype(F32)
        return carry

    lax.fori_loop(0, (side + 2) // rows, step, 0)
    pair = 2 * slots
    for corner, column_ref, at, beside, is_east in (
        (0, west_ref, 0, 1, False),
        (1, east_ref, 0, 1, True),
        (2, west_ref, side + 1, side, False),
        (3, east_ref, side + 1, side, True),
    ):
        value = column_ref[at]
        blended = ring.flag(4 + corner) == 1.0
        half = jnp.where(blended, 0.5 * value, 0.0)
        column_ref[beside] = column_ref[beside] + half
        column_ref[at] = jnp.where(blended, 0.0, value)
        if is_east:
            old = out_ref[at, width - pair : width].astype(F32)
            new = jnp.concatenate([old[:slots], old[slots:] + half], axis=0)
            out_ref[at, width - pair : width] = new.astype(BF)
        else:
            old = out_ref[at, 0:pair].astype(F32)
            new = jnp.concatenate([old[:slots] + half, old[slots:]], axis=0)
            out_ref[at, 0:pair] = new.astype(BF)
    ring.packed(
        [east_ref[i] for i in range(side + 2)], [west_ref[i] for i in range(side + 2)], send_ref
    )


def halo_back(ring, side, ext_ref, near_ref, far_ref, field_ref):
    slots = ring.slots
    width = side * slots
    east, west = ring.arrived(near_ref, far_ref)
    for i in range(side):
        field_ref[i] = ext_ref[1 + i].astype(F32)
    south = split_cells(ext_ref[0].astype(F32), slots)
    north = split_cells(ext_ref[side + 1].astype(F32), slots)
    south[0], south[-1] = south[0] + west[0], south[-1] + east[0]
    north[0], north[-1] = north[0] + west[-1], north[-1] + east[-1]
    low, high, first, last = ring.halo_rows_back(south, north)
    field_ref[0] += jnp.concatenate(low, axis=0)
    field_ref[side - 1] += jnp.concatenate(high, axis=0)
    for i in range(side):
        field_ref[i, 0:slots] += first[i] + west[1 + i]
        field_ref[i, width - slots : width] += last[i] + east[1 + i]


def collect_kernel(side, half, slots, info, *refs):
    parts, (ext_ref, cot_ref, table_ref, send_ref), scratch = (
        refs[:slots],
        refs[slots : slots + 4],
        refs[slots + 4 :],
    )
    cells, cot_cells = side * side, half * half
    channels = ext_ref.shape[2]
    field_ref, low_ref, high_ref = scratch
    for index, part in enumerate(parts):
        slot = info[0] ^ index
        field_ref[pl.ds(slot, cells, stride=slots), :] = part[0:cells].astype(F32)
        low_ref[pl.ds(slot, cot_cells, stride=slots), :] = part[
            cells : cells + cot_cells
        ].astype(F32)
        high_ref[pl.ds(slot, cot_cells, stride=slots), :] = part[
            cells + cot_cells : cells + 2 * cot_cells
        ].astype(F32)
        flags = part[cells + 2 * cot_cells : cells + 2 * cot_cells + 16].astype(F32)
        table_ref[pl.ds(slot, 1), :] = flags[0:1]
    width = side * slots
    for i in range(side):
        ext_ref[1 + i] = field_ref[i * width : (i + 1) * width].astype(BF)
    cot_ref[:, 0:channels] = low_ref[...].astype(BF)
    cot_ref[:, channels : 2 * channels] = high_ref[...].astype(BF)
    ring = Ring(slots, channels, table_ref[...], info)
    extend_and_send(ring, side, ext_ref, send_ref)


def first_kernel(
    side, slots, info, ext_in, near_ref, far_ref, table_ref, weight_ref,
    pad_ref, ext_ref, slope_ref, send_ref,
):
    channels, width = ext_in.shape[2], side * slots
    ring = Ring(slots, channels, table_ref[...], info)
    pad_columns(ring, side, ext_in, near_ref, far_ref, pad_ref)
    rows = ROWS_PER_STEP

    def step(index, carry):
        start = index * rows
        z = convolved(pad_ref, ext_in, weight_ref, start, rows, width, slots, channels)
        cdf, pdf = normal_parts(z)
        shape = (rows, width, z.shape[1])
        ext_ref[pl.ds(start + 1, rows)] = (z * cdf).astype(BF).reshape(shape)
        slope_ref[pl.ds(start, rows)] = (cdf + z * pdf).astype(BF).reshape(shape)
        return carry

    lax.fori_loop(0, side // rows, step, 0)
    ring = Ring(slots, ext_ref.shape[2], table_ref[...], info)
    extend_and_send(ring, side, ext_ref, send_ref)


def second_kernel(
    side, slots, info, ext_in, near_ref, far_ref, table_ref, cot_ref, weight_ref, back_ref,
    pad_ref, grad_ref, pooled_ref, ext_ref, send_ref,
    wide_ref, shifted_ref, mean_ref, west_ref, east_ref,
):
    channels, width = ext_in.shape[2], side * slots
    ring = Ring(slots, channels, table_ref[...], info)
    pad_columns(ring, side, ext_in, near_ref, far_ref, pad_ref)
    clear_edges(wide_ref, shifted_ref, side, slots)
    rows = ROWS_PER_STEP
    half = side // 2
    step_cells = (rows // 2) * half * slots

    def step(index, carry):
        start = index * rows
        z = convolved(pad_ref, ext_in, weight_ref, start, rows, width, slots, channels)
        cdf, pdf = normal_parts(z)
        paired = (rows // 2, 2, half, 2, slots, channels)
        value = (z * cdf).reshape(paired)
        cells = pl.ds(pl.multiple_of(index * step_cells, step_cells), step_cells)
        mean = (value[:, 0, :, 0] + value[:, 0, :, 1]) + (value[:, 1, :, 0] + value[:, 1, :, 1])
        mean = mean.reshape(step_cells, channels) * 0.25
        for block in range(channels // 128):
            mean_ref[block, cells, :] = mean[:, block * 128 : (block + 1) * 128]
        cot = cot_ref[cells, :].astype(F32) * 0.25
        cot = cot.reshape(rows // 2, 1, half, 1, slots, channels)
        slope = (cdf + z * pdf).reshape(paired)
        grad = (jnp.broadcast_to(cot, paired) * slope).reshape(rows, width, channels)
        grad_ref[pl.ds(start, rows)] = grad.astype(BF)
        for row in range(rows):
            put_gradient(wide_ref, shifted_ref, start + 2 + row, grad[row], slots)
        return carry

    lax.fori_loop(0, side // rows, step, 0)
    for block in range(channels // 128):
        pooled_ref[:, block * 128 : (block + 1) * 128] = mean_ref[
            block, pl.ds(info[0], half * half, stride=slots), :
        ].astype(BF)
    convolved_back(
        ring, side, wide_ref, shifted_ref, back_ref, ext_ref, send_ref, west_ref, east_ref
    )


def third_kernel(
    side, slots, info, ext_in, near_ref, far_ref, table_ref, slope_ref, back_ref,
    grad_ref, ext_ref, send_ref,
    field_ref, wide_ref, shifted_ref, west_ref, east_ref,
):
    ring = Ring(slots, ext_in.shape[2], table_ref[...], info)
    halo_back(ring, side, ext_in, near_ref, far_ref, field_ref)
    clear_edges(wide_ref, shifted_ref, side, slots)

    def step(index, carry):
        grad = field_ref[index] * slope_ref[index].astype(F32)
        grad_ref[index] = grad.astype(BF)
        put_gradient(wide_ref, shifted_ref, index + 2, grad, slots)
        return carry

    lax.fori_loop(0, side, step, 0)
    ring = Ring(slots, ext_ref.shape[2], table_ref[...], info)
    convolved_back(
        ring, side, wide_ref, shifted_ref, back_ref, ext_ref, send_ref, west_ref, east_ref
    )


def last_kernel(side, slots, info, ext_in, near_ref, far_ref, table_ref, out_ref, field_ref, flat_ref):
    width = side * slots
    ring = Ring(slots, ext_in.shape[2], table_ref[...], info)
    halo_back(ring, side, ext_in, near_ref, far_ref, field_ref)
    for i in range(side):
        flat_ref[i * width : (i + 1) * width] = field_ref[i]
    out_ref[...] = flat_ref[pl.ds(info[0], side * side, stride=slots), :].astype(BF)


def weight_kernel(side, slots, info, pad_ref, ext_ref, grad_ref, out_ref):
    width, channels = side * slots, pad_ref.shape[2]
    columns = out_ref.shape[2]
    start = pl.multiple_of(info[4] * columns, columns)
    grad = grad_ref[:, :, pl.ds(start, columns)].reshape(side * width, columns)

    def step(dh, carry):
        views = (
            pad_ref[pl.ds(dh, side), 0:width, :],
            ext_ref[pl.ds(dh, side), :, :],
            pad_ref[pl.ds(dh, side), 2 * slots : 2 * slots + width, :],
        )
        for dw, view in enumerate(views):
            product = lax.dot_general(
                view.reshape(side * width, channels),
                grad,
                (((0,), (0,)), ((), ())),
                preferred_element_type=F32,
            )
            out_ref[dh * 3 + dw] = product.astype(BF)
        return carry

    lax.fori_loop(0, 3, step, 0)


def scale_kernel(target, info, first_a, first_b, second_a, second_b, first_out, second_out):
    squared = jnp.zeros((1, 1), F32)
    for ref in (first_a, first_b, second_a, second_b):
        value = ref[...].astype(F32)
        rows = jnp.sum(value * value, axis=0, keepdims=True)
        squared = squared + jnp.sum(rows, axis=1, keepdims=True)
    scale = target / jnp.sqrt(squared + 1e-06)
    for mine, other, out in ((first_a, first_b, first_out), (second_a, second_b, second_out)):
        columns = mine.shape[1]
        low = jnp.where(info[4] == 0, mine[...].astype(F32), other[...].astype(F32))
        high = jnp.where(info[4] == 0, other[...].astype(F32), mine[...].astype(F32))
        out[:, 0:columns] = (low * scale).astype(BF)
        out[:, columns : 2 * columns] = (high * scale).astype(BF)


def run(kernel, outs, args, scratch=(), flops=0, transcendentals=0):
    vmem = pl.BlockSpec(memory_space=pltpu.VMEM)
    smem = pl.BlockSpec(memory_space=pltpu.SMEM)
    moved = sum(math.prod(x.shape) * x.dtype.itemsize for x in list(args) + list(outs))
    return pl.pallas_call(
        kernel,
        out_shape=tuple(outs),
        in_specs=[smem] + [vmem] * (len(args) - 1),
        out_specs=tuple(vmem for _ in outs),
        scratch_shapes=list(scratch),
        compiler_params=pltpu.CompilerParams(vmem_limit_bytes=44 * 1024 * 1024),
        cost_estimate=pl.CostEstimate(
            flops=flops, bytes_accessed=moved, transcendentals=transcendentals
        ),
    )(*args)


def on_device(lon, lat, features, conv_first, conv_second, cotangent, edge_pick, edge_flip, corner_rule):
    side, c_in = features.shape[2], features.shape[4]
    half, c_out = cotangent.shape[2], cotangent.shape[4]
    slots, rings = 2 * lat, lon // 2
    width, padded = side * slots, (side + 2) * slots
    axes = ("lon", "lat")
    lon_at, lat_at = lax.axis_index("lon"), lax.axis_index("lat")
    ring_at, hemisphere = lon_at % rings, lon_at // rings
    core = lat_at % 2
    send_east = ((ring_at + core) % 2 == 0).astype(jnp.int32)
    info = jnp.stack(
        [
            hemisphere * lat + lat_at,
            (ring_at == rings - 1).astype(jnp.int32),
            (ring_at == 0).astype(jnp.int32),
            send_east,
            core,
        ]
    ).astype(jnp.int32)

    def spec(shape, dtype=BF):
        return jax.ShapeDtypeStruct(shape, dtype)

    def permuted(value, partner):
        pairs = []
        for place in range(lon):
            for band in range(lat):
                there = partner(place, band)
                pairs.append((place * lat + band, there[0] * lat + there[1]))
        return lax.ppermute(value, axes, pairs)

    def core_swap(value):
        return permuted(value, lambda place, band: (place, band ^ 1))

    def beside(place, band):
        ring, upper = place % rings, place // rings
        east = (ring + band) % 2 == 0
        return ((ring + (1 if east else -1)) % rings + upper * rings, band)

    def exchange(value):
        near = permuted(value, beside)
        return near, core_swap(near)

    flags = jnp.concatenate(
        [edge_pick.reshape(-1), edge_flip.reshape(-1), corner_rule.reshape(-1)]
    ).astype(BF)
    flags = jnp.broadcast_to(jnp.pad(flags, (0, c_in - flags.shape[0])), (16, c_in))
    cot = cotangent.reshape(half * half, c_out)
    own = jnp.concatenate(
        [features.reshape(side * side, c_in), cot[:, :c_in], cot[:, c_in:], flags], axis=0
    )
    parts = [None] * slots
    parts[0] = own
    for index in range(2, slots, 2):
        parts[index] = permuted(
            own,
            lambda place, band, index=index: (
                (place + rings * (index // lat)) % lon,
                band ^ (index % lat),
            ),
        )
    for index in range(0, slots, 2):
        parts[index + 1] = core_swap(parts[index])

    first_weight = conv_first.reshape(3, 3 * c_in, c_out)
    second_weight = conv_second.reshape(3, 3 * c_out, c_out)
    first_back = conv_first.transpose(0, 1, 3, 2).reshape(3, 3 * c_out, c_in)
    second_back = conv_second.transpose(0, 1, 3, 2).reshape(3, 3 * c_out, c_out)

    def vmem(shape, dtype):
        return pltpu.VMEM(shape, dtype)

    features_ext, cot_ring, table, columns = run(
        functools.partial(collect_kernel, side, half, slots),
        [
            spec((side + 2, width, c_in)),
            spec((half * half * slots, c_out)),
            spec((slots, c_in), F32),
            spec((padded, c_in)),
        ],
        [info] + parts,
        [
            vmem((side * width, c_in), F32),
            vmem((half * half * slots, c_in), F32),
            vmem((half * half * slots, c_in), F32),
        ],
    )
    near, far = exchange(columns)
    work = 2 * side * width * 9 * c_in * c_out
    features_pad, act_ext, slope, columns = run(
        functools.partial(first_kernel, side, slots),
        [
            spec((side + 2, padded, c_in)),
            spec((side + 2, width, c_out)),
            spec((side, width, c_out)),
            spec((padded, c_out)),
        ],
        [info, features_ext, near, far, table, first_weight],
        flops=work,
    )
    near, far = exchange(columns)
    back_scratch = [
        vmem((side + 4, (side + 4) * slots, c_out), BF),
        vmem((side + 4, padded, c_out), BF),
    ]
    act_pad, second_grad, pooled, act_grad, columns = run(
        functools.partial(second_kernel, side, slots),
        [
            spec((side + 2, padded, c_out)),
            spec((side, width, c_out)),
            spec((half * half, c_out)),
            spec((side + 2, width, c_out)),
            spec((padded, c_out)),
        ],
        [info, act_ext, near, far, table, cot_ring, second_weight, second_back],
        back_scratch
        + [
            vmem((c_out // 128, half * half * slots, 128), F32),
            vmem((side + 2, slots, c_out), F32),
            vmem((side + 2, slots, c_out), F32),
        ],
        flops=4 * work,
    )
    near, far = exchange(columns)
    columns_each = c_out // 2
    second_sum = run(
        functools.partial(weight_kernel, side, slots),
        [spec((9, c_out, columns_each))],
        [info, act_pad, act_ext, second_grad],
        flops=2 * work,
    )[0]
    pre_grad, features_grad, columns = run(
        functools.partial(third_kernel, side, slots),
        [
            spec((side, width, c_out)),
            spec((side + 2, width, c_in)),
            spec((padded, c_in)),
        ],
        [info, act_grad, near, far, table, slope, first_back],
        [vmem((side, width, c_out), F32)]
        + back_scratch
        + [vmem((side + 2, slots, c_in), F32), vmem((side + 2, slots, c_in), F32)],
        flops=work,
    )
    near, far = exchange(columns)
    first_sum = run(
        functools.partial(weight_kernel, side, slots),
        [spec((9, c_in, columns_each))],
        [info, features_pad, features_ext, pre_grad],
        flops=work,
    )[0]
    input_grad = run(
        functools.partial(last_kernel, side, slots),
        [spec((side * side, c_in))],
        [info, features_grad, near, far, table],
        [vmem((side, width, c_in), F32), vmem((side * width, c_in), F32)],
    )[0]

    def over_rings(value):
        if rings & (rings - 1):
            total = lax.psum(value.astype(F32), "lon") * (0.5 if lon % 2 == 0 else 1.0)
            return total.astype(BF)
        step = 1
        while step < rings:
            other = permuted(
                value,
                lambda place, band: (((place % rings) ^ step) + (place // rings) * rings, band),
            )
            value = (value.astype(F32) + other.astype(F32)).astype(BF)
            step *= 2
        return value

    second_half = over_rings(second_sum.reshape(9 * c_out, columns_each))
    first_half = over_rings(first_sum.reshape(9 * c_in, columns_each))
    target = math.sqrt(9.0 * (c_in + c_out) * c_out)
    scaled_first, scaled_second = run(
        functools.partial(scale_kernel, target),
        [spec((9 * c_in, c_out)), spec((9 * c_out, c_out))],
        [info, first_half, core_swap(first_half), second_half, core_swap(second_half)],
    )
    return (
        pooled.reshape(1, 1, half, half, c_out),
        input_grad.reshape(1, 1, side, side, c_in),
        scaled_first.reshape(3, 3, c_in, c_out),
        scaled_second.reshape(3, 3, c_out, c_out),
    )


def solution(mesh):
    return jax.shard_map(
        functools.partial(on_device, mesh.shape["lon"], mesh.shape["lat"]),
        mesh=mesh,
        in_specs=(
            P("lon", "lat", None, None, None),
            P(),
            P(),
            P("lon", "lat", None, None, None),
            P("lon", "lat", None),
            P("lon", "lat", None),
            P("lon", "lat", None),
        ),
        out_specs=(P("lon", "lat", None, None, None), P("lon", "lat", None, None, None), P(), P()),
        check_vma=False,
    )
```

```python
import functools
import math

import jax
import jax.numpy as jnp
from jax import lax
from jax.experimental import pallas as pl
from jax.experimental.pallas import tpu as pltpu
from jax.sharding import PartitionSpec as P


BF = jnp.bfloat16
F32 = jnp.float32
ROWS_PER_STEP = 4


def normal_parts(z):
    cdf = 0.5 * (1.0 + lax.erf(z * (1.0 / math.sqrt(2.0))))
    pdf = jnp.exp(-0.5 * z * z) * (1.0 / math.sqrt(2.0 * math.pi))
    return cdf, pdf


class Ring:
    def __init__(self, slots, channels, table, info):
        self.slots, self.band = slots, slots // 2
        self.channels, self.info = channels, info
        place = lax.broadcasted_iota(jnp.int32, (slots, channels), 0)
        self.top = lax.rem(place, self.band) == self.band - 1
        self.bottom = lax.rem(place, self.band) == 0
        self.table = table

    def flag(self, column):
        return jnp.broadcast_to(self.table[:, column : column + 1], (self.slots, self.channels))

    def up(self, x):
        return pltpu.roll(x, self.slots - 1, 0)

    def down(self, x):
        return pltpu.roll(x, 1, 0)

    def across(self, x):
        return pltpu.roll(x, self.band, 0)

    def take(self, edges, side, to_source, to_slot):
        pick, flip = to_source(self.flag(side)), to_source(self.flag(2 + side))
        count = len(edges[0])
        chosen = [
            jnp.where(
                pick == 0.0,
                edges[0][j],
                jnp.where(
                    pick == 1.0, edges[1][j], jnp.where(pick == 2.0, edges[2][j], edges[3][j])
                ),
            )
            for j in range(count)
        ]
        return [
            to_slot(jnp.where(flip == 1.0, chosen[count - 1 - j], chosen[j])) for j in range(count)
        ]

    def halo_rows(self, edges):
        same = self.take(edges, 0, self.up, self.down)
        pole = self.take(edges, 0, self.across, self.across)
        south = [jnp.where(self.bottom, b, a) for a, b in zip(same, pole)]
        same = self.take(edges, 1, self.down, self.up)
        pole = self.take(edges, 1, self.across, self.across)
        north = [jnp.where(self.top, b, a) for a, b in zip(same, pole)]
        return south, north

    def give(self, totals, rows, side, to_source):
        pick, flip = to_source(self.flag(side)), to_source(self.flag(2 + side))
        count = len(rows)
        moved = [to_source(row) for row in rows]
        for j in range(count):
            value = jnp.where(flip == 1.0, moved[count - 1 - j], moved[j])
            for edge in range(4):
                share = jnp.where(pick == float(edge), value, 0.0)
                totals[edge][j] = share if totals[edge][j] is None else totals[edge][j] + share

    def halo_rows_back(self, south, north):
        totals = [[None] * len(south) for _ in range(4)]
        self.give(totals, [jnp.where(self.bottom, 0.0, x) for x in south], 0, self.up)
        self.give(totals, [jnp.where(self.bottom, x, 0.0) for x in south], 0, self.across)
        self.give(totals, [jnp.where(self.top, 0.0, x) for x in north], 1, self.down)
        self.give(totals, [jnp.where(self.top, x, 0.0) for x in north], 1, self.across)
        return totals

    def arrived(self, near_ref, far_ref):
        slots = self.slots
        near, far = near_ref[...].astype(F32), far_ref[...].astype(F32)
        to_east = self.info[3] == 1
        east, west = jnp.where(to_east, near, far), jnp.where(to_east, far, near)
        count = near.shape[0] // slots
        east = [east[i * slots : (i + 1) * slots] for i in range(count)]
        west = [west[i * slots : (i + 1) * slots] for i in range(count)]
        east = [jnp.where(self.info[1] == 1, self.across(x), x) for x in east]
        west = [jnp.where(self.info[2] == 1, self.across(x), x) for x in west]
        return east, west

    def packed(self, east_list, west_list, out_ref):
        east, west = jnp.concatenate(east_list, axis=0), jnp.concatenate(west_list, axis=0)
        out_ref[...] = jnp.where(self.info[3] == 1, east, west).astype(BF)


def place_of(slots):
    lat, rings = slots // 2, lax.axis_size("lon") // 2
    lon_at, lat_at = lax.axis_index("lon"), lax.axis_index("lat")
    ring_at, hemisphere = lax.rem(lon_at, rings), lax.div(lon_at, rings)
    core = lax.rem(lat_at, 2)
    return (
        hemisphere * lat + lat_at,
        (ring_at == rings - 1).astype(jnp.int32),
        (ring_at == 0).astype(jnp.int32),
        1 - lax.rem(ring_at + core, 2),
        core,
        lax.rem(lax.div(lat_at, 2), 2),
    )


def split_cells(row, slots):
    return [row[j * slots : (j + 1) * slots] for j in range(row.shape[0] // slots)]


def extend_and_send(ring, side, ext_ref, send_ref):
    slots = ring.slots
    width = side * slots
    pair = 2 * slots
    first_col, last_col = [], []
    for i in range(side):
        first_col.append(ext_ref[1 + i, 0:pair].astype(F32)[:slots])
        last_col.append(ext_ref[1 + i, width - pair : width].astype(F32)[slots:])
    edges = [
        split_cells(ext_ref[1].astype(F32), slots),
        split_cells(ext_ref[side].astype(F32), slots),
        first_col,
        last_col,
    ]
    south, north = ring.halo_rows(edges)
    ext_ref[0] = jnp.concatenate(south, axis=0).astype(BF)
    ext_ref[side + 1] = jnp.concatenate(north, axis=0).astype(BF)
    ring.packed(
        [south[-1]] + last_col + [north[-1]], [south[0]] + first_col + [north[0]], send_ref
    )


def pad_columns(ring, side, ext_ref, near_ref, far_ref, pad_ref):
    slots = ring.slots
    width = side * slots
    east, west = ring.arrived(near_ref, far_ref)
    low, high = ext_ref[0].astype(F32), ext_ref[side + 1].astype(F32)
    blends = (
        (0, west, 0, 1, low[:slots]),
        (1, east, 0, 1, low[width - slots :]),
        (2, west, side + 1, side, high[:slots]),
        (3, east, side + 1, side, high[width - slots :]),
    )
    for corner, column, at, beside, along in blends:
        blended = (0.5 * (along + column[beside])).astype(BF).astype(F32)
        column[at] = jnp.where(ring.flag(4 + corner) == 1.0, blended, column[at])
    for i in range(side + 2):
        pad_ref[i] = jnp.concatenate([west[i], ext_ref[i].astype(F32), east[i]], axis=0).astype(BF)


def windows(pad_ref, ext_ref, start, rows, width, slots, channels):
    left = pad_ref[pl.ds(start, rows), 0:width, :]
    middle = ext_ref[pl.ds(start, rows), :, :]
    right = pad_ref[pl.ds(start, rows), 2 * slots : 2 * slots + width, :]
    return jnp.concatenate([left, middle, right], axis=-1).reshape(rows * width, 3 * channels)


def convolved(pad_ref, ext_ref, weight_ref, start, rows, width, slots, channels):
    total = None
    for dh in range(3):
        window = windows(pad_ref, ext_ref, start + dh, rows, width, slots, channels)
        part = jnp.dot(window, weight_ref[dh], preferred_element_type=F32)
        total = part if total is None else total + part
    return total


def clear_edges(wide_ref, shifted_ref, side, slots):
    width = side * slots
    for row in (0, 1, side + 2, side + 3):
        wide_ref[row] = jnp.zeros_like(wide_ref[row])
        shifted_ref[row] = jnp.zeros_like(shifted_ref[row])
    blank = jnp.zeros((side, 2 * slots, wide_ref.shape[2]), BF)
    wide_ref[2 : side + 2, 0 : 2 * slots] = blank
    wide_ref[2 : side + 2, width + 2 * slots :] = blank


def put_gradient(wide_ref, shifted_ref, row, value, slots):
    width = value.shape[0]
    wide_ref[row, 2 * slots : 2 * slots + width] = value.astype(BF)
    blank = jnp.zeros((slots, value.shape[1]), F32)
    shifted_ref[row] = jnp.concatenate([blank, value, blank], axis=0).astype(BF)


def convolved_back(
    ring, side, wide_ref, shifted_ref, weight_ref, out_ref, send_ref, west_ref, east_ref
):
    slots, channels = ring.slots, ring.channels
    width, padded = side * slots, (side + 2) * slots
    depth = wide_ref.shape[2]
    rows = 3

    def step(index, carry):
        start = index * rows
        total = None
        for dh in range(3):
            at = pl.ds(start + 2 - dh, rows)
            window = jnp.concatenate(
                [
                    wide_ref[at, 2 * slots : 2 * slots + padded, :],
                    shifted_ref[at, :, :],
                    wide_ref[at, 0:padded, :],
                ],
                axis=-1,
            ).reshape(rows * padded, 3 * depth)
            part = jnp.dot(window, weight_ref[dh], preferred_element_type=F32)
            total = part if total is None else total + part
        total = total.reshape(rows, padded, channels)
        out_ref[pl.ds(start, rows)] = total[:, slots : slots + width].astype(BF)
        west_ref[pl.ds(start, rows)] = total[:, :slots].astype(BF).astype(F32)
        east_ref[pl.ds(start, rows)] = total[:, slots + width :].astype(BF).astype(F32)
        return carry

    lax.fori_loop(0, (side + 2) // rows, step, 0)
    pair = 2 * slots
    for corner, column_ref, at, beside, is_east in (
        (0, west_ref, 0, 1, False),
        (1, east_ref, 0, 1, True),
        (2, west_ref, side + 1, side, False),
        (3, east_ref, side + 1, side, True),
    ):
        value = column_ref[at]
        blended = ring.flag(4 + corner) == 1.0
        half = jnp.where(blended, 0.5 * value, 0.0)
        column_ref[beside] = column_ref[beside] + half
        column_ref[at] = jnp.where(blended, 0.0, value)
        if is_east:
            old = out_ref[at, width - pair : width].astype(F32)
            new = jnp.concatenate([old[:slots], old[slots:] + half], axis=0)
            out_ref[at, width - pair : width] = new.astype(BF)
        else:
            old = out_ref[at, 0:pair].astype(F32)
            new = jnp.concatenate([old[:slots] + half, old[slots:]], axis=0)
            out_ref[at, 0:pair] = new.astype(BF)
    ring.packed(
        [east_ref[i] for i in range(side + 2)], [west_ref[i] for i in range(side + 2)], send_ref
    )


def halo_back(ring, side, ext_ref, near_ref, far_ref, field_ref):
    slots = ring.slots
    width = side * slots
    east, west = ring.arrived(near_ref, far_ref)
    for i in range(side):
        field_ref[i] = ext_ref[1 + i].astype(F32)
    south = split_cells(ext_ref[0].astype(F32), slots)
    north = split_cells(ext_ref[side + 1].astype(F32), slots)
    south[0], south[-1] = south[0] + west[0], south[-1] + east[0]
    north[0], north[-1] = north[0] + west[-1], north[-1] + east[-1]
    low, high, first, last = ring.halo_rows_back(south, north)
    field_ref[0] += jnp.concatenate(low, axis=0)
    field_ref[side - 1] += jnp.concatenate(high, axis=0)
    for i in range(side):
        field_ref[i, 0:slots] += first[i] + west[1 + i]
        field_ref[i, width - slots : width] += last[i] + east[1 + i]


def collect_kernel(side, half, slots, *refs):
    info = place_of(slots)
    parts, (ext_ref, cot_ref, table_ref, send_ref), scratch = (
        refs[:slots],
        refs[slots : slots + 4],
        refs[slots + 4 :],
    )
    cells, cot_cells = side * side, half * half
    channels = ext_ref.shape[2]
    field_ref, low_ref, high_ref = scratch
    for index, part in enumerate(parts):
        slot = info[0] ^ index
        field_ref[pl.ds(slot, cells, stride=slots), :] = part[0:cells].astype(F32)
        low_ref[pl.ds(slot, cot_cells, stride=slots), :] = part[
            cells : cells + cot_cells
        ].astype(F32)
        high_ref[pl.ds(slot, cot_cells, stride=slots), :] = part[
            cells + cot_cells : cells + 2 * cot_cells
        ].astype(F32)
        flags = part[cells + 2 * cot_cells : cells + 2 * cot_cells + 16].astype(F32)
        table_ref[pl.ds(slot, 1), :] = flags[0:1]
    width = side * slots
    for i in range(side):
        ext_ref[1 + i] = field_ref[i * width : (i + 1) * width].astype(BF)
    cot_ref[:, 0:channels] = low_ref[...].astype(BF)
    cot_ref[:, channels : 2 * channels] = high_ref[...].astype(BF)
    ring = Ring(slots, channels, table_ref[...], info)
    extend_and_send(ring, side, ext_ref, send_ref)


def first_kernel(
    side, slots, ext_in, near_ref, far_ref, table_ref, weight_ref,
    pad_ref, ext_ref, slope_ref, send_ref,
):
    info = place_of(slots)
    channels, width = ext_in.shape[2], side * slots
    ring = Ring(slots, channels, table_ref[...], info)
    pad_columns(ring, side, ext_in, near_ref, far_ref, pad_ref)
    rows = ROWS_PER_STEP

    def step(index, carry):
        start = index * rows
        z = convolved(pad_ref, ext_in, weight_ref, start, rows, width, slots, channels)
        cdf, pdf = normal_parts(z)
        shape = (rows, width, z.shape[1])
        ext_ref[pl.ds(start + 1, rows)] = (z * cdf).astype(BF).reshape(shape)
        slope_ref[pl.ds(start, rows)] = (cdf + z * pdf).astype(BF).reshape(shape)
        return carry

    lax.fori_loop(0, side // rows, step, 0)
    ring = Ring(slots, ext_ref.shape[2], table_ref[...], info)
    extend_and_send(ring, side, ext_ref, send_ref)


def second_kernel(
    side, slots, ext_in, near_ref, far_ref, table_ref, cot_ref, weight_ref, back_ref,
    pad_ref, grad_ref, pooled_ref, ext_ref, send_ref,
    wide_ref, shifted_ref, mean_ref, west_ref, east_ref,
):
    info = place_of(slots)
    channels, width = ext_in.shape[2], side * slots
    ring = Ring(slots, channels, table_ref[...], info)
    pad_columns(ring, side, ext_in, near_ref, far_ref, pad_ref)
    clear_edges(wide_ref, shifted_ref, side, slots)
    rows = ROWS_PER_STEP
    half = side // 2
    step_cells = (rows // 2) * half * slots

    def step(index, carry):
        start = index * rows
        z = convolved(pad_ref, ext_in, weight_ref, start, rows, width, slots, channels)
        cdf, pdf = normal_parts(z)
        paired = (rows // 2, 2, half, 2, slots, channels)
        value = (z * cdf).reshape(paired)
        cells = pl.ds(pl.multiple_of(index * step_cells, step_cells), step_cells)
        mean = (value[:, 0, :, 0] + value[:, 0, :, 1]) + (value[:, 1, :, 0] + value[:, 1, :, 1])
        mean = mean.reshape(step_cells, channels) * 0.25
        for block in range(channels // 128):
            mean_ref[block, cells, :] = mean[:, block * 128 : (block + 1) * 128]
        cot = cot_ref[cells, :].astype(F32) * 0.25
        cot = cot.reshape(rows // 2, 1, half, 1, slots, channels)
        slope = (cdf + z * pdf).reshape(paired)
        grad = (jnp.broadcast_to(cot, paired) * slope).reshape(rows, width, channels)
        grad_ref[pl.ds(start, rows)] = grad.astype(BF)
        for row in range(rows):
            put_gradient(wide_ref, shifted_ref, start + 2 + row, grad[row], slots)
        return carry

    lax.fori_loop(0, side // rows, step, 0)
    for block in range(channels // 128):
        pooled_ref[:, block * 128 : (block + 1) * 128] = mean_ref[
            block, pl.ds(info[0], half * half, stride=slots), :
        ].astype(BF)
    convolved_back(
        ring, side, wide_ref, shifted_ref, back_ref, ext_ref, send_ref, west_ref, east_ref
    )


def third_kernel(
    side, slots, ext_in, near_ref, far_ref, table_ref, slope_ref, pad_ref, features_ref,
    grad_ref, low_ref, high_ref,
    field_ref,
):
    info = place_of(slots)
    ring = Ring(slots, ext_in.shape[2], table_ref[...], info)
    halo_back(ring, side, ext_in, near_ref, far_ref, field_ref)
    for i in range(side):
        grad_ref[i] = (field_ref[i] * slope_ref[i].astype(F32)).astype(BF)
    columns = low_ref.shape[2]
    start = pl.multiple_of(info[4] * columns, columns)
    grad = grad_ref[:, :, pl.ds(start, columns)].reshape(side * side * slots, columns)

    def put(tap, product):
        rows = product.shape[0] // 2
        low_ref[tap] = product[:rows]
        high_ref[tap] = product[rows:]

    weight_products(side, slots, pad_ref, features_ref, grad, 0, pad_ref.shape[2], put)


def fourth_kernel(
    side, slots, grad_ref, table_ref, back_ref,
    ext_ref, send_ref,
    wide_ref, shifted_ref, west_ref, east_ref,
):
    info = place_of(slots)
    clear_edges(wide_ref, shifted_ref, side, slots)
    for i in range(side):
        put_gradient(wide_ref, shifted_ref, i + 2, grad_ref[i].astype(F32), slots)
    ring = Ring(slots, ext_ref.shape[2], table_ref[...], info)
    convolved_back(
        ring, side, wide_ref, shifted_ref, back_ref, ext_ref, send_ref, west_ref, east_ref
    )


def last_kernel(
    side, slots, ext_in, near_ref, far_ref, table_ref, out_ref, field_ref, flat_ref
):
    info = place_of(slots)
    width = side * slots
    ring = Ring(slots, ext_in.shape[2], table_ref[...], info)
    halo_back(ring, side, ext_in, near_ref, far_ref, field_ref)
    for i in range(side):
        flat_ref[i * width : (i + 1) * width] = field_ref[i]
    out_ref[...] = flat_ref[pl.ds(info[0], side * side, stride=slots), :].astype(BF)


def weight_products(side, slots, pad_ref, ext_ref, grad, first, channels, put):
    width = side * slots
    lanes = pl.ds(first, channels)

    def step(dh, carry):
        rows = pl.ds(dh, side)
        window = jnp.concatenate(
            [
                pad_ref[rows, 0:width, lanes],
                ext_ref[rows, :, lanes],
                pad_ref[rows, 2 * slots : 2 * slots + width, lanes],
            ],
            axis=-1,
        ).reshape(side * width, 3 * channels)
        product = lax.dot_general(
            window, grad, (((0,), (0,)), ((), ())), preferred_element_type=F32
        ).astype(BF)
        for dw in range(3):
            put(dh * 3 + dw, product[dw * channels : (dw + 1) * channels])
        return carry

    lax.fori_loop(0, 3, step, 0)


def weight_kernel(side, slots, pad_ref, ext_ref, grad_ref, out_ref):
    info = place_of(slots)
    rows, columns = out_ref.shape[1:]
    start = pl.multiple_of(info[4] * columns, columns)
    grad = grad_ref[:, :, pl.ds(start, columns)].reshape(side * side * slots, columns)

    def put(tap, product):
        out_ref[tap] = product

    first = pl.multiple_of(info[5] * rows, rows)
    weight_products(side, slots, pad_ref, ext_ref, grad, first, rows, put)


def pack_kernel(features_ref, cot_ref, pick_ref, flip_ref, rule_ref, out_ref):
    cells, channels = features_ref.shape
    cot_cells = cot_ref.shape[0]
    out_ref[0:cells] = features_ref[...]
    out_ref[cells : cells + cot_cells] = cot_ref[:, 0:channels]
    out_ref[cells + cot_cells : cells + 2 * cot_cells] = cot_ref[:, channels : 2 * channels]
    lane = lax.broadcasted_iota(jnp.int32, (16, channels), 1)
    flags = jnp.zeros((16, channels), jnp.int32)
    values = [pick_ref[0, 0, k] for k in range(2)] + [flip_ref[0, 0, k] for k in range(2)]
    values = values + [rule_ref[0, 0, k] for k in range(4)]
    for column, value in enumerate(values):
        flags = jnp.where(lane == column, value, flags)
    out_ref[cells + 2 * cot_cells :] = flags.astype(F32).astype(BF)


def scale_kernel(slots, target, *refs):
    info = place_of(slots)
    blocks, (first_out, second_out) = refs[:-2], refs[-2:]
    squared = jnp.zeros((1, 1), F32)
    for ref in blocks:
        value = ref[...].astype(F32)
        lanes = jnp.sum(jnp.sum(value * value, axis=0), axis=0, keepdims=True)
        squared = squared + jnp.sum(lanes, axis=1, keepdims=True)
    scale = target / jnp.sqrt(squared + 1e-06)
    for index, ref in enumerate(blocks):
        core = info[4] if index % 2 == 0 else 1 - info[4]
        rows, columns = ref.shape[1:]
        lanes = pl.ds(pl.multiple_of(core * columns, columns), columns)
        value = (ref[...].astype(F32) * scale).astype(BF)
        if index < 4:
            part = index // 2 * rows
            first_out[:, part : part + rows, lanes] = value
        else:
            half = info[5] if index < 6 else 1 - info[5]
            second_out[:, pl.ds(pl.multiple_of(half * rows, rows), rows), lanes] = value


def run(kernel, outs, args, scratch=(), flops=0, scalars=0, vmem_mib=16):
    vmem = pl.BlockSpec(memory_space=pltpu.VMEM)
    smem = pl.BlockSpec(memory_space=pltpu.SMEM)
    moved = sum(math.prod(x.shape) * x.dtype.itemsize for x in list(args) + list(outs))
    return pl.pallas_call(
        kernel,
        out_shape=tuple(outs),
        in_specs=[vmem] * (len(args) - scalars) + [smem] * scalars,
        out_specs=tuple(vmem for _ in outs),
        scratch_shapes=list(scratch),
        compiler_params=pltpu.CompilerParams(vmem_limit_bytes=vmem_mib * 1024 * 1024),
        cost_estimate=pl.CostEstimate(flops=flops, bytes_accessed=moved, transcendentals=0),
    )(*args)


def on_device(lon, lat, features, conv_first, conv_second, cotangent, edge_pick, edge_flip, corner_rule):
    side, c_in = features.shape[2], features.shape[4]
    half, c_out = cotangent.shape[2], cotangent.shape[4]
    slots, rings = 2 * lat, lon // 2
    width, padded = side * slots, (side + 2) * slots
    axes = ("lon", "lat")

    def spec(shape, dtype=BF):
        return jax.ShapeDtypeStruct(shape, dtype)

    def vmem(shape, dtype):
        return pltpu.VMEM(shape, dtype)

    def permuted(value, partner):
        pairs = []
        for place in range(lon):
            for band in range(lat):
                there = partner(place, band)
                pairs.append((place * lat + band, there[0] * lat + there[1]))
        return lax.ppermute(value, axes, pairs)

    def core_swap(value):
        return permuted(value, lambda place, band: (place, band ^ 1))

    def x_swap(value):
        return permuted(value, lambda place, band: (place, band ^ 2))

    def ring_swap(value, step):
        return permuted(
            value, lambda place, band: (((place % rings) ^ step) + place // rings * rings, band)
        )

    def beside(place, band):
        ring, upper = place % rings, place // rings
        east = (ring + band) % 2 == 0
        return ((ring + (1 if east else -1)) % rings + upper * rings, band)

    def exchange(value):
        near = permuted(value, beside)
        return near, core_swap(near)

    own = run(
        pack_kernel,
        [spec((side * side + 2 * half * half + 16, c_in))],
        [
            features.reshape(side * side, c_in),
            cotangent.reshape(half * half, c_out),
            edge_pick,
            edge_flip,
            corner_rule,
        ],
        scalars=3,
    )[0]
    parts = [None] * slots
    parts[0] = own
    for index in [*range(lat, slots, 2), *range(2, lat, 2)]:
        parts[index] = permuted(
            own,
            lambda place, band, index=index: (
                (place + rings * (index // lat)) % lon,
                band ^ (index % lat),
            ),
        )
    for index in range(0, slots, 2):
        parts[index + 1] = core_swap(parts[index])

    first_weight = conv_first.reshape(3, 3 * c_in, c_out)
    second_weight = conv_second.reshape(3, 3 * c_out, c_out)
    first_back = conv_first.transpose(0, 1, 3, 2).reshape(3, 3 * c_out, c_in)
    second_back = conv_second.transpose(0, 1, 3, 2).reshape(3, 3 * c_out, c_out)

    features_ext, cot_ring, table, columns = run(
        functools.partial(collect_kernel, side, half, slots),
        [
            spec((side + 2, width, c_in)),
            spec((half * half * slots, c_out)),
            spec((slots, c_in), F32),
            spec((padded, c_in)),
        ],
        parts,
        [
            vmem((side * width, c_in), F32),
            vmem((half * half * slots, c_in), F32),
            vmem((half * half * slots, c_in), F32),
        ],
    )
    near, far = exchange(columns)
    work = 2 * side * width * 9 * c_in * c_out
    features_pad, act_ext, slope, columns = run(
        functools.partial(first_kernel, side, slots),
        [
            spec((side + 2, padded, c_in)),
            spec((side + 2, width, c_out)),
            spec((side, width, c_out)),
            spec((padded, c_out)),
        ],
        [features_ext, near, far, table, first_weight],
        flops=work,
    )
    near, far = exchange(columns)
    back_scratch = [
        vmem((side + 4, (side + 4) * slots, c_out), BF),
        vmem((side + 4, padded, c_out), BF),
    ]
    act_pad, second_grad, pooled, act_grad, columns = run(
        functools.partial(second_kernel, side, slots),
        [
            spec((side + 2, padded, c_out)),
            spec((side, width, c_out)),
            spec((half * half, c_out)),
            spec((side + 2, width, c_out)),
            spec((padded, c_out)),
        ],
        [act_ext, near, far, table, cot_ring, second_weight, second_back],
        back_scratch
        + [
            vmem((c_out // 128, half * half * slots, 128), F32),
            vmem((side + 2, slots, c_out), F32),
            vmem((side + 2, slots, c_out), F32),
        ],
        flops=4 * work,
    )
    near, far = exchange(columns)
    part = c_out // 2
    second_sum = run(
        functools.partial(weight_kernel, side, slots),
        [spec((9, part, part))],
        [act_pad, act_ext, second_grad],
        flops=work,
    )[0]
    near, far, second_sum = lax.optimization_barrier((near, far, second_sum))
    pre_grad, first_low, first_high = run(
        functools.partial(third_kernel, side, slots),
        [
            spec((side, width, c_out)),
            spec((9, c_in // 2, part)),
            spec((9, c_in // 2, part)),
        ],
        [act_grad, near, far, table, slope, features_pad, features_ext],
        [vmem((side, width, c_out), F32)],
        flops=work,
    )
    features_grad, columns = run(
        functools.partial(fourth_kernel, side, slots),
        [spec((side + 2, width, c_in)), spec((padded, c_in))],
        [pre_grad, table, first_back],
        back_scratch + [vmem((side + 2, slots, c_in), F32), vmem((side + 2, slots, c_in), F32)],
        flops=work,
    )
    near, far = exchange(columns)
    input_grad = run(
        functools.partial(last_kernel, side, slots),
        [spec((side * side, c_in))],
        [features_grad, near, far, table],
        [vmem((side, width, c_in), F32), vmem((side * width, c_in), F32)],
    )[0]

    def over_rings(value, backwards):
        if rings & (rings - 1):
            total = lax.psum(value.astype(F32), "lon") * (0.5 if lon % 2 == 0 else 1.0)
            return total.astype(BF)
        steps = [1 << k for k in range(rings.bit_length() - 1)]
        for step in reversed(steps) if backwards else steps:
            value = (value.astype(F32) + ring_swap(value, step).astype(F32)).astype(BF)
        return value

    second_sum = over_rings(second_sum, False)
    second_other = x_swap(second_sum)
    first_low = over_rings(first_low, False)
    first_high = over_rings(first_high, True)
    blocks = []
    for block in (first_low, first_high, second_sum, second_other):
        blocks += [block, core_swap(block)]
    target = math.sqrt(9.0 * (c_in + c_out) * c_out)
    scaled_first, scaled_second = run(
        functools.partial(scale_kernel, slots, target),
        [spec((9, c_in, c_out)), spec((9, c_out, c_out))],
        blocks,
    )
    return (
        pooled.reshape(1, 1, half, half, c_out),
        input_grad.reshape(1, 1, side, side, c_in),
        scaled_first.reshape(3, 3, c_in, c_out),
        scaled_second.reshape(3, 3, c_out, c_out),
    )


def solution(mesh):
    return jax.shard_map(
        functools.partial(on_device, mesh.shape["lon"], mesh.shape["lat"]),
        mesh=mesh,
        in_specs=(
            P("lon", "lat", None, None, None),
            P(),
            P(),
            P("lon", "lat", None, None, None),
            P("lon", "lat", None),
            P("lon", "lat", None),
            P("lon", "lat", None),
        ),
        out_specs=(P("lon", "lat", None, None, None), P("lon", "lat", None, None, None), P(), P()),
        check_vma=False,
    )
```

```python
import functools
import math

import jax
import jax.numpy as jnp
from jax import lax
from jax.experimental import pallas as pl
from jax.experimental.pallas import tpu as pltpu
from jax.sharding import PartitionSpec as P


BF = jnp.bfloat16
F32 = jnp.float32
ROWS_PER_STEP = 4


def normal_parts(z):
    cdf = 0.5 * (1.0 + lax.erf(z * (1.0 / math.sqrt(2.0))))
    pdf = jnp.exp(-0.5 * z * z) * (1.0 / math.sqrt(2.0 * math.pi))
    return cdf, pdf


class Ring:
    def __init__(self, slots, channels, table, info):
        self.slots, self.band = slots, slots // 2
        self.channels, self.info = channels, info
        place = lax.broadcasted_iota(jnp.int32, (slots, channels), 0)
        self.top = lax.rem(place, self.band) == self.band - 1
        self.bottom = lax.rem(place, self.band) == 0
        self.table = table

    def flag(self, column):
        return jnp.broadcast_to(self.table[:, column : column + 1], (self.slots, self.channels))

    def up(self, x):
        return pltpu.roll(x, self.slots - 1, 0)

    def down(self, x):
        return pltpu.roll(x, 1, 0)

    def across(self, x):
        return pltpu.roll(x, self.band, 0)

    def take(self, edges, side, to_source, to_slot):
        pick, flip = to_source(self.flag(side)), to_source(self.flag(2 + side))
        count = len(edges[0])
        chosen = [
            jnp.where(
                pick == 0.0,
                edges[0][j],
                jnp.where(
                    pick == 1.0, edges[1][j], jnp.where(pick == 2.0, edges[2][j], edges[3][j])
                ),
            )
            for j in range(count)
        ]
        return [
            to_slot(jnp.where(flip == 1.0, chosen[count - 1 - j], chosen[j])) for j in range(count)
        ]

    def halo_rows(self, edges):
        same = self.take(edges, 0, self.up, self.down)
        pole = self.take(edges, 0, self.across, self.across)
        south = [jnp.where(self.bottom, b, a) for a, b in zip(same, pole)]
        same = self.take(edges, 1, self.down, self.up)
        pole = self.take(edges, 1, self.across, self.across)
        north = [jnp.where(self.top, b, a) for a, b in zip(same, pole)]
        return south, north

    def give(self, totals, rows, side, to_source):
        pick, flip = to_source(self.flag(side)), to_source(self.flag(2 + side))
        count = len(rows)
        moved = [to_source(row) for row in rows]
        for j in range(count):
            value = jnp.where(flip == 1.0, moved[count - 1 - j], moved[j])
            for edge in range(4):
                share = jnp.where(pick == float(edge), value, 0.0)
                totals[edge][j] = share if totals[edge][j] is None else totals[edge][j] + share

    def halo_rows_back(self, south, north):
        totals = [[None] * len(south) for _ in range(4)]
        self.give(totals, [jnp.where(self.bottom, 0.0, x) for x in south], 0, self.up)
        self.give(totals, [jnp.where(self.bottom, x, 0.0) for x in south], 0, self.across)
        self.give(totals, [jnp.where(self.top, 0.0, x) for x in north], 1, self.down)
        self.give(totals, [jnp.where(self.top, x, 0.0) for x in north], 1, self.across)
        return totals

    def arrived(self, near_ref, far_ref):
        slots = self.slots
        near, far = near_ref[...].astype(F32), far_ref[...].astype(F32)
        to_east = self.info[3] == 1
        east, west = jnp.where(to_east, near, far), jnp.where(to_east, far, near)
        count = near.shape[0] // slots
        east = [east[i * slots : (i + 1) * slots] for i in range(count)]
        west = [west[i * slots : (i + 1) * slots] for i in range(count)]
        east = [jnp.where(self.info[1] == 1, self.across(x), x) for x in east]
        west = [jnp.where(self.info[2] == 1, self.across(x), x) for x in west]
        return east, west

    def packed(self, east_list, west_list, out_ref):
        east, west = jnp.concatenate(east_list, axis=0), jnp.concatenate(west_list, axis=0)
        out_ref[...] = jnp.where(self.info[3] == 1, east, west).astype(BF)


def place_of(slots):
    lat, rings = slots // 2, lax.axis_size("lon") // 2
    lon_at, lat_at = lax.axis_index("lon"), lax.axis_index("lat")
    ring_at, hemisphere = lax.rem(lon_at, rings), lax.div(lon_at, rings)
    core = lax.rem(lat_at, 2)
    return (
        hemisphere * lat + lat_at,
        (ring_at == rings - 1).astype(jnp.int32),
        (ring_at == 0).astype(jnp.int32),
        1 - lax.rem(ring_at + core, 2),
        core,
        lax.rem(lax.div(lat_at, 2), 2),
    )


def split_cells(row, slots):
    return [row[j * slots : (j + 1) * slots] for j in range(row.shape[0] // slots)]


def extend_and_send(ring, side, ext_ref, send_ref):
    slots = ring.slots
    width = side * slots
    pair = 2 * slots
    first_col, last_col = [], []
    for i in range(side):
        first_col.append(ext_ref[1 + i, 0:pair].astype(F32)[:slots])
        last_col.append(ext_ref[1 + i, width - pair : width].astype(F32)[slots:])
    edges = [
        split_cells(ext_ref[1].astype(F32), slots),
        split_cells(ext_ref[side].astype(F32), slots),
        first_col,
        last_col,
    ]
    south, north = ring.halo_rows(edges)
    ext_ref[0] = jnp.concatenate(south, axis=0).astype(BF)
    ext_ref[side + 1] = jnp.concatenate(north, axis=0).astype(BF)
    ring.packed(
        [south[-1]] + last_col + [north[-1]], [south[0]] + first_col + [north[0]], send_ref
    )


def pad_columns(ring, side, ext_ref, near_ref, far_ref, pad_ref):
    slots = ring.slots
    width = side * slots
    east, west = ring.arrived(near_ref, far_ref)
    low, high = ext_ref[0].astype(F32), ext_ref[side + 1].astype(F32)
    blends = (
        (0, west, 0, 1, low[:slots]),
        (1, east, 0, 1, low[width - slots :]),
        (2, west, side + 1, side, high[:slots]),
        (3, east, side + 1, side, high[width - slots :]),
    )
    for corner, column, at, beside, along in blends:
        blended = (0.5 * (along + column[beside])).astype(BF).astype(F32)
        column[at] = jnp.where(ring.flag(4 + corner) == 1.0, blended, column[at])
    for i in range(side + 2):
        pad_ref[i] = jnp.concatenate([west[i], ext_ref[i].astype(F32), east[i]], axis=0).astype(BF)


def windows(pad_ref, ext_ref, start, rows, width, slots, channels):
    left = pad_ref[pl.ds(start, rows), 0:width, :]
    middle = ext_ref[pl.ds(start, rows), :, :]
    right = pad_ref[pl.ds(start, rows), 2 * slots : 2 * slots + width, :]
    return jnp.concatenate([left, middle, right], axis=-1).reshape(rows * width, 3 * channels)


def convolved(pad_ref, ext_ref, weight_ref, start, rows, width, slots, channels):
    total = None
    for dh in range(3):
        window = windows(pad_ref, ext_ref, start + dh, rows, width, slots, channels)
        part = jnp.dot(window, weight_ref[dh], preferred_element_type=F32)
        total = part if total is None else total + part
    return total


def clear_edges(wide_ref, side, slots):
    width = side * slots
    blank = jnp.zeros((side, 2 * slots, wide_ref.shape[2]), BF)
    wide_ref[:, 0 : 2 * slots] = blank
    wide_ref[:, width + 2 * slots :] = blank


def put_gradient(wide_ref, shifted_ref, row, value, slots):
    width = value.shape[0]
    wide_ref[row, 2 * slots : 2 * slots + width] = value.astype(BF)
    blank = jnp.zeros((slots, value.shape[1]), F32)
    shifted_ref[row] = jnp.concatenate([blank, value, blank], axis=0).astype(BF)


def convolved_back(
    ring, side, wide_ref, shifted_ref, weight_ref, out_ref, send_ref, west_ref, east_ref
):
    slots, channels = ring.slots, ring.channels
    width, padded = side * slots, (side + 2) * slots
    depth = wide_ref.shape[2]
    rows = ROWS_PER_STEP

    def finish(row, total):
        out_ref[row] = total[slots : slots + width].astype(BF)
        west_ref[row] = total[:slots].astype(BF).astype(F32)
        east_ref[row] = total[slots + width :].astype(BF).astype(F32)

    waiting = {}
    for start in range(0, side, rows):
        windows_back = (
            wide_ref[start : start + rows, 2 * slots : 2 * slots + padded, :],
            shifted_ref[start : start + rows, :, :],
            wide_ref[start : start + rows, 0:padded, :],
        )
        product = None
        for dw, window in enumerate(windows_back):
            part = lax.dot_general(
                window.reshape(rows * padded, depth),
                weight_ref[:, dw].reshape(3 * channels, depth),
                (((1,), (1,)), ((), ())),
                preferred_element_type=F32,
            )
            product = part if product is None else product + part
        for row in range(rows):
            for dh in range(3):
                part = product[
                    row * padded : (row + 1) * padded, dh * channels : (dh + 1) * channels
                ]
                at = start + row + dh
                waiting[at] = waiting[at] + part if at in waiting else part
        for at in sorted(waiting):
            if at < start + rows or start + rows == side:
                finish(at, waiting.pop(at))
    pair = 2 * slots
    for corner, column_ref, at, beside, is_east in (
        (0, west_ref, 0, 1, False),
        (1, east_ref, 0, 1, True),
        (2, west_ref, side + 1, side, False),
        (3, east_ref, side + 1, side, True),
    ):
        value = column_ref[at]
        blended = ring.flag(4 + corner) == 1.0
        half = jnp.where(blended, 0.5 * value, 0.0)
        column_ref[beside] = column_ref[beside] + half
        column_ref[at] = jnp.where(blended, 0.0, value)
        if is_east:
            old = out_ref[at, width - pair : width].astype(F32)
            new = jnp.concatenate([old[:slots], old[slots:] + half], axis=0)
            out_ref[at, width - pair : width] = new.astype(BF)
        else:
            old = out_ref[at, 0:pair].astype(F32)
            new = jnp.concatenate([old[:slots] + half, old[slots:]], axis=0)
            out_ref[at, 0:pair] = new.astype(BF)
    ring.packed(
        [east_ref[i] for i in range(side + 2)], [west_ref[i] for i in range(side + 2)], send_ref
    )


def halo_back(ring, side, ext_ref, near_ref, far_ref, field_ref):
    slots = ring.slots
    width = side * slots
    east, west = ring.arrived(near_ref, far_ref)
    for i in range(side):
        field_ref[i] = ext_ref[1 + i].astype(F32)
    south = split_cells(ext_ref[0].astype(F32), slots)
    north = split_cells(ext_ref[side + 1].astype(F32), slots)
    south[0], south[-1] = south[0] + west[0], south[-1] + east[0]
    north[0], north[-1] = north[0] + west[-1], north[-1] + east[-1]
    low, high, first, last = ring.halo_rows_back(south, north)
    field_ref[0] += jnp.concatenate(low, axis=0)
    field_ref[side - 1] += jnp.concatenate(high, axis=0)
    for i in range(side):
        field_ref[i, 0:slots] += first[i] + west[1 + i]
        field_ref[i, width - slots : width] += last[i] + east[1 + i]


def collect_kernel(side, half, slots, *refs):
    info = place_of(slots)
    parts, (ext_ref, cot_ref, table_ref, send_ref), scratch = (
        refs[:slots],
        refs[slots : slots + 4],
        refs[slots + 4 :],
    )
    cells, cot_cells = side * side, half * half
    channels = ext_ref.shape[2]
    field_ref, low_ref, high_ref = scratch
    for index, part in enumerate(parts):
        slot = info[0] ^ index
        field_ref[pl.ds(slot, cells, stride=slots), :] = part[0:cells].astype(F32)
        low_ref[pl.ds(slot, cot_cells, stride=slots), :] = part[
            cells : cells + cot_cells
        ].astype(F32)
        high_ref[pl.ds(slot, cot_cells, stride=slots), :] = part[
            cells + cot_cells : cells + 2 * cot_cells
        ].astype(F32)
        flags = part[cells + 2 * cot_cells : cells + 2 * cot_cells + 16].astype(F32)
        table_ref[pl.ds(slot, 1), :] = flags[0:1]
    width = side * slots
    for i in range(side):
        ext_ref[1 + i] = field_ref[i * width : (i + 1) * width].astype(BF)
    cot_ref[:, 0:channels] = low_ref[...].astype(BF)
    cot_ref[:, channels : 2 * channels] = high_ref[...].astype(BF)
    ring = Ring(slots, channels, table_ref[...], info)
    extend_and_send(ring, side, ext_ref, send_ref)


def first_kernel(
    side, slots, ext_in, near_ref, far_ref, table_ref, weight_ref,
    pad_ref, ext_ref, slope_ref, send_ref,
):
    info = place_of(slots)
    channels, width = ext_in.shape[2], side * slots
    ring = Ring(slots, channels, table_ref[...], info)
    pad_columns(ring, side, ext_in, near_ref, far_ref, pad_ref)
    rows = ROWS_PER_STEP

    def step(index, carry):
        start = index * rows
        z = convolved(pad_ref, ext_in, weight_ref, start, rows, width, slots, channels)
        cdf, pdf = normal_parts(z)
        shape = (rows, width, z.shape[1])
        ext_ref[pl.ds(start + 1, rows)] = (z * cdf).astype(BF).reshape(shape)
        slope_ref[pl.ds(start, rows)] = (cdf + z * pdf).astype(BF).reshape(shape)
        return carry

    for index in range(side // rows):
        step(index, 0)
    ring = Ring(slots, ext_ref.shape[2], table_ref[...], info)
    extend_and_send(ring, side, ext_ref, send_ref)


def second_kernel(
    side, slots, ext_in, near_ref, far_ref, table_ref, cot_ref, weight_ref, back_ref,
    pad_ref, grad_ref, pooled_ref, ext_ref, send_ref,
    wide_ref, shifted_ref, mean_ref, west_ref, east_ref,
):
    info = place_of(slots)
    channels, width = ext_in.shape[2], side * slots
    ring = Ring(slots, channels, table_ref[...], info)
    pad_columns(ring, side, ext_in, near_ref, far_ref, pad_ref)
    clear_edges(wide_ref, side, slots)
    rows = ROWS_PER_STEP
    half = side // 2
    step_cells = (rows // 2) * half * slots

    def step(index, carry):
        start = index * rows
        z = convolved(pad_ref, ext_in, weight_ref, start, rows, width, slots, channels)
        cdf, pdf = normal_parts(z)
        paired = (rows // 2, 2, half, 2, slots, channels)
        value = (z * cdf).reshape(paired)
        cells = pl.ds(index * step_cells, step_cells)
        mean = (value[:, 0, :, 0] + value[:, 0, :, 1]) + (value[:, 1, :, 0] + value[:, 1, :, 1])
        mean = mean.reshape(step_cells, channels) * 0.25
        for block in range(channels // 128):
            mean_ref[block, cells, :] = mean[:, block * 128 : (block + 1) * 128]
        cot = cot_ref[cells, :].astype(F32) * 0.25
        cot = cot.reshape(rows // 2, 1, half, 1, slots, channels)
        slope = (cdf + z * pdf).reshape(paired)
        grad = (jnp.broadcast_to(cot, paired) * slope).reshape(rows, width, channels)
        grad_ref[pl.ds(start, rows)] = grad.astype(BF)
        for row in range(rows):
            put_gradient(wide_ref, shifted_ref, start + row, grad[row], slots)
        return carry

    for index in range(side // rows):
        step(index, 0)
    for block in range(channels // 128):
        pooled_ref[:, block * 128 : (block + 1) * 128] = mean_ref[
            block, pl.ds(info[0], half * half, stride=slots), :
        ].astype(BF)
    convolved_back(
        ring, side, wide_ref, shifted_ref, back_ref, ext_ref, send_ref, west_ref, east_ref
    )


def third_kernel(
    side, slots, ext_in, near_ref, far_ref, table_ref, slope_ref, pad_ref, features_ref,
    grad_ref, low_ref, high_ref,
    field_ref,
):
    info = place_of(slots)
    ring = Ring(slots, ext_in.shape[2], table_ref[...], info)
    halo_back(ring, side, ext_in, near_ref, far_ref, field_ref)
    for i in range(side):
        grad_ref[i] = (field_ref[i] * slope_ref[i].astype(F32)).astype(BF)
    columns = low_ref.shape[2]
    start = pl.multiple_of(info[4] * columns, columns)
    grad = grad_ref[:, :, pl.ds(start, columns)].reshape(side * side * slots, columns)

    weight_products(side, slots, pad_ref, features_ref, grad, low_ref, high_ref)


def fourth_kernel(
    side, slots, grad_ref, table_ref, back_ref,
    ext_ref, send_ref,
    wide_ref, shifted_ref, west_ref, east_ref,
):
    info = place_of(slots)
    clear_edges(wide_ref, side, slots)
    for i in range(side):
        put_gradient(wide_ref, shifted_ref, i, grad_ref[i].astype(F32), slots)
    ring = Ring(slots, ext_ref.shape[2], table_ref[...], info)
    convolved_back(
        ring, side, wide_ref, shifted_ref, back_ref, ext_ref, send_ref, west_ref, east_ref
    )


def last_kernel(
    side, slots, ext_in, near_ref, far_ref, table_ref, out_ref, field_ref, flat_ref
):
    info = place_of(slots)
    width = side * slots
    ring = Ring(slots, ext_in.shape[2], table_ref[...], info)
    halo_back(ring, side, ext_in, near_ref, far_ref, field_ref)
    for i in range(side):
        flat_ref[i * width : (i + 1) * width] = field_ref[i]
    out_ref[...] = flat_ref[pl.ds(info[0], side * side, stride=slots), :].astype(BF)


def weight_products(side, slots, pad_ref, ext_ref, grad, low_ref, high_ref):
    width, channels = side * slots, pad_ref.shape[2]
    half = channels // 2

    def step(dh, carry):
        rows = pl.ds(dh, side)
        window = jnp.concatenate(
            [
                pad_ref[rows, 0:width, :],
                ext_ref[rows, :, :],
                pad_ref[rows, 2 * slots : 2 * slots + width, :],
            ],
            axis=-1,
        ).reshape(side * width, 3 * channels)
        product = lax.dot_general(
            window, grad, (((0,), (0,)), ((), ())), preferred_element_type=F32
        ).astype(BF)
        for dw in range(3):
            at = dw * channels
            low_ref[dh * 3 + dw] = product[at : at + half]
            high_ref[dh * 3 + dw] = product[at + half : at + channels]
        return carry

    lax.fori_loop(0, 3, step, 0)


def weight_kernel(side, slots, pad_ref, ext_ref, grad_ref, low_ref, high_ref):
    columns = low_ref.shape[2]
    start = pl.multiple_of(place_of(slots)[4] * columns, columns)
    grad = grad_ref[:, :, pl.ds(start, columns)].reshape(side * side * slots, columns)
    weight_products(side, slots, pad_ref, ext_ref, grad, low_ref, high_ref)


def scale_kernel(slots, target, *refs):
    info = place_of(slots)
    blocks, (first_out, second_out) = refs[:-2], refs[-2:]
    squared = jnp.zeros((1, 1), F32)
    for ref in blocks:
        value = ref[...].astype(F32)
        lanes = jnp.sum(jnp.sum(value * value, axis=0), axis=0, keepdims=True)
        squared = squared + jnp.sum(lanes, axis=1, keepdims=True)
    scale = target / jnp.sqrt(squared + 1e-06)
    for index, ref in enumerate(blocks):
        core = info[4] if index % 2 == 0 else 1 - info[4]
        rows, columns = ref.shape[1:]
        lanes = pl.ds(pl.multiple_of(core * columns, columns), columns)
        out, part = first_out if index < 4 else second_out, index % 4 // 2 * rows
        out[:, part : part + rows, lanes] = (ref[...].astype(F32) * scale).astype(BF)


class RingSums:
    def __init__(self, rings, swap, values):
        self.values, self.swap, self.at, self.arriving = list(values), swap, 0, []
        steps = [1 << k for k in range(rings.bit_length() - 1)]
        self.even = rings == 1 << len(steps)
        self.rounds = len(steps) if self.even else 1
        self.orders = (steps, steps[::-1])

    def send(self):
        if self.even:
            self.arriving = [
                self.swap(value, order[self.at]) for value, order in zip(self.values, self.orders)
            ]
        else:
            totals = [0.5 * lax.psum(value.astype(F32), "lon") for value in self.values]
            self.arriving = [total - value for total, value in zip(totals, self.values)]
        self.at += 1

    def add(self):
        self.values = [
            (value.astype(F32) + other.astype(F32)).astype(BF)
            for value, other in zip(self.values, self.arriving)
        ]


def run(kernel, outs, args, scratch=(), flops=0, vmem_mib=8):
    vmem = pl.BlockSpec(memory_space=pltpu.VMEM)
    moved = sum(math.prod(x.shape) * x.dtype.itemsize for x in list(args) + list(outs))
    return pl.pallas_call(
        kernel,
        out_shape=tuple(outs),
        in_specs=[vmem] * len(args),
        out_specs=tuple(vmem for _ in outs),
        scratch_shapes=list(scratch),
        compiler_params=pltpu.CompilerParams(vmem_limit_bytes=vmem_mib * 1024 * 1024),
        cost_estimate=pl.CostEstimate(flops=flops, bytes_accessed=moved, transcendentals=0),
    )(*args)


def on_device(lon, lat, features, conv_first, conv_second, cotangent, edge_pick, edge_flip, corner_rule):
    side, c_in = features.shape[2], features.shape[4]
    half, c_out = cotangent.shape[2], cotangent.shape[4]
    slots, rings = 2 * lat, lon // 2
    width, padded = side * slots, (side + 2) * slots
    axes = ("lon", "lat")

    def spec(shape, dtype=BF):
        return jax.ShapeDtypeStruct(shape, dtype)

    def vmem(shape, dtype):
        return pltpu.VMEM(shape, dtype)

    def permuted(value, partner):
        pairs = []
        for place in range(lon):
            for band in range(lat):
                there = partner(place, band)
                pairs.append((place * lat + band, there[0] * lat + there[1]))
        return lax.ppermute(value, axes, pairs)

    def core_swap(value):
        return permuted(value, lambda place, band: (place, band ^ 1))

    def x_swap(value):
        return permuted(value, lambda place, band: (place, band ^ 2))

    def ring_swap(value, step):
        return permuted(
            value, lambda place, band: (((place % rings) ^ step) + place // rings * rings, band)
        )

    def beside(place, band):
        ring, upper = place % rings, place // rings
        east = (ring + band) % 2 == 0
        return ((ring + (1 if east else -1)) % rings + upper * rings, band)

    def exchange(value):
        near = permuted(value, beside)
        return near, core_swap(near)

    flags = jnp.concatenate(
        [edge_pick.reshape(-1), edge_flip.reshape(-1), corner_rule.reshape(-1)]
    ).astype(BF)
    flags = jnp.broadcast_to(jnp.pad(flags, (0, c_in - flags.shape[0])), (16, c_in))
    cot = cotangent.reshape(half * half, c_out)
    own = jnp.concatenate(
        [features.reshape(side * side, c_in), cot[:, :c_in], cot[:, c_in:], flags], axis=0
    )
    parts = [None] * slots
    parts[0] = own
    for index in [*range(lat, slots, 2), *range(2, lat, 2)]:
        parts[index] = permuted(
            own,
            lambda place, band, index=index: (
                (place + rings * (index // lat)) % lon,
                band ^ (index % lat),
            ),
        )
    for index in range(0, slots, 2):
        parts[index + 1] = core_swap(parts[index])

    first_weight = conv_first.reshape(3, 3 * c_in, c_out)
    second_weight = conv_second.reshape(3, 3 * c_out, c_out)

    features_ext, cot_ring, table, columns = run(
        functools.partial(collect_kernel, side, half, slots),
        [
            spec((side + 2, width, c_in)),
            spec((half * half * slots, c_out)),
            spec((slots, c_in), F32),
            spec((padded, c_in)),
        ],
        parts,
        [
            vmem((side * width, c_in), F32),
            vmem((half * half * slots, c_in), F32),
            vmem((half * half * slots, c_in), F32),
        ],
    )
    near, far = exchange(columns)
    work = 2 * side * width * 9 * c_in * c_out
    features_pad, act_ext, slope, columns = run(
        functools.partial(first_kernel, side, slots),
        [
            spec((side + 2, padded, c_in)),
            spec((side + 2, width, c_out)),
            spec((side, width, c_out)),
            spec((padded, c_out)),
        ],
        [features_ext, near, far, table, first_weight],
        flops=work,
    )
    near, far = exchange(columns)
    back_scratch = [
        vmem((side, (side + 4) * slots, c_out), BF),
        vmem((side, padded, c_out), BF),
    ]
    act_pad, second_grad, pooled, act_grad, columns = run(
        functools.partial(second_kernel, side, slots),
        [
            spec((side + 2, padded, c_out)),
            spec((side, width, c_out)),
            spec((half * half, c_out)),
            spec((side + 2, width, c_out)),
            spec((padded, c_out)),
        ],
        [act_ext, near, far, table, cot_ring, second_weight, conv_second],
        back_scratch
        + [
            vmem((c_out // 128, half * half * slots, 128), F32),
            vmem((side + 2, slots, c_out), F32),
            vmem((side + 2, slots, c_out), F32),
        ],
        flops=4 * work,
    )
    near = permuted(columns, beside)
    part = c_out // 2
    second_low, second_high = run(
        functools.partial(weight_kernel, side, slots),
        [spec((9, part, part)), spec((9, part, part))],
        [act_pad, act_ext, second_grad],
        flops=2 * work,
    )
    near, second_low, second_high = lax.optimization_barrier((near, second_low, second_high))
    far = core_swap(near)
    second_sums = RingSums(rings, ring_swap, (second_low, second_high))
    second_sums.send()
    pre_grad, first_low, first_high = run(
        functools.partial(third_kernel, side, slots),
        [
            spec((side, width, c_out)),
            spec((9, c_in // 2, part)),
            spec((9, c_in // 2, part)),
        ],
        [act_grad, near, far, table, slope, features_pad, features_ext],
        [vmem((side, width, c_out), F32)],
        flops=work,
    )
    features_grad, columns = run(
        functools.partial(fourth_kernel, side, slots),
        [spec((side + 2, width, c_in)), spec((padded, c_in))],
        [pre_grad, table, conv_first],
        back_scratch + [vmem((side + 2, slots, c_in), F32), vmem((side + 2, slots, c_in), F32)],
        flops=work,
    )
    *second_sums.arriving, first_low, first_high = lax.optimization_barrier(
        (*second_sums.arriving, first_low, first_high)
    )
    first_sums = RingSums(rings, ring_swap, (first_low, first_high))
    first_sums.send()
    near = permuted(columns, beside)
    for _ in range(second_sums.rounds - 1):
        for sums in (second_sums, first_sums):
            sums.add()
            sums.send()
    *second_sums.arriving, near = lax.optimization_barrier((*second_sums.arriving, near))
    far = core_swap(near)
    input_grad = run(
        functools.partial(last_kernel, side, slots),
        [spec((side * side, c_in))],
        [features_grad, near, far, table],
        [vmem((side, width, c_in), F32), vmem((side * width, c_in), F32)],
    )[0]
    second_sums.add()
    first_sums.add()
    blocks = []
    for block in (*first_sums.values, *second_sums.values):
        blocks += [block, core_swap(block)]
    target = math.sqrt(9.0 * (c_in + c_out) * c_out)
    scaled_first, scaled_second = run(
        functools.partial(scale_kernel, slots, target),
        [spec((9, c_in, c_out)), spec((9, c_out, c_out))],
        blocks,
    )
    return (
        pooled.reshape(1, 1, half, half, c_out),
        input_grad.reshape(1, 1, side, side, c_in),
        scaled_first.reshape(3, 3, c_in, c_out),
        scaled_second.reshape(3, 3, c_out, c_out),
    )


def solution(mesh):
    return jax.shard_map(
        functools.partial(on_device, mesh.shape["lon"], mesh.shape["lat"]),
        mesh=mesh,
        in_specs=(
            P("lon", "lat", None, None, None),
            P(),
            P(),
            P("lon", "lat", None, None, None),
            P("lon", "lat", None),
            P("lon", "lat", None),
            P("lon", "lat", None),
        ),
        out_specs=(P("lon", "lat", None, None, None), P("lon", "lat", None, None, None), P(), P()),
        check_vma=False,
    )
```

```python
import functools
import math

import jax
import jax.numpy as jnp
from jax import lax
from jax.experimental import pallas as pl
from jax.experimental.pallas import tpu as pltpu
from jax.sharding import PartitionSpec as P


BF = jnp.bfloat16
F32 = jnp.float32
ROWS_PER_STEP = 4


def normal_parts(z):
    cdf = 0.5 * (1.0 + lax.erf(z * (1.0 / math.sqrt(2.0))))
    pdf = jnp.exp(-0.5 * z * z) * (1.0 / math.sqrt(2.0 * math.pi))
    return cdf, pdf


class Ring:
    def __init__(self, slots, channels, table, info):
        self.slots, self.band = slots, slots // 2
        self.channels, self.info = channels, info
        place = lax.broadcasted_iota(jnp.int32, (slots, channels), 0)
        self.top = lax.rem(place, self.band) == self.band - 1
        self.bottom = lax.rem(place, self.band) == 0
        self.table = table

    def flag(self, column):
        return jnp.broadcast_to(self.table[:, column : column + 1], (self.slots, self.channels))

    def up(self, x):
        return pltpu.roll(x, self.slots - 1, 0)

    def down(self, x):
        return pltpu.roll(x, 1, 0)

    def across(self, x):
        return pltpu.roll(x, self.band, 0)

    def take(self, edges, side, to_source, to_slot):
        pick, flip = to_source(self.flag(side)), to_source(self.flag(2 + side))
        count = len(edges[0])
        chosen = [
            jnp.where(
                pick == 0.0,
                edges[0][j],
                jnp.where(
                    pick == 1.0, edges[1][j], jnp.where(pick == 2.0, edges[2][j], edges[3][j])
                ),
            )
            for j in range(count)
        ]
        return [
            to_slot(jnp.where(flip == 1.0, chosen[count - 1 - j], chosen[j])) for j in range(count)
        ]

    def halo_rows(self, edges):
        same = self.take(edges, 0, self.up, self.down)
        pole = self.take(edges, 0, self.across, self.across)
        south = [jnp.where(self.bottom, b, a) for a, b in zip(same, pole)]
        same = self.take(edges, 1, self.down, self.up)
        pole = self.take(edges, 1, self.across, self.across)
        north = [jnp.where(self.top, b, a) for a, b in zip(same, pole)]
        return south, north

    def give(self, totals, rows, side, to_source):
        pick, flip = to_source(self.flag(side)), to_source(self.flag(2 + side))
        count = len(rows)
        moved = [to_source(row) for row in rows]
        for j in range(count):
            value = jnp.where(flip == 1.0, moved[count - 1 - j], moved[j])
            for edge in range(4):
                share = jnp.where(pick == float(edge), value, 0.0)
                totals[edge][j] = share if totals[edge][j] is None else totals[edge][j] + share

    def halo_rows_back(self, south, north):
        totals = [[None] * len(south) for _ in range(4)]
        self.give(totals, [jnp.where(self.bottom, 0.0, x) for x in south], 0, self.up)
        self.give(totals, [jnp.where(self.bottom, x, 0.0) for x in south], 0, self.across)
        self.give(totals, [jnp.where(self.top, 0.0, x) for x in north], 1, self.down)
        self.give(totals, [jnp.where(self.top, x, 0.0) for x in north], 1, self.across)
        return totals

    def arrived(self, near_ref, far_ref):
        slots = self.slots
        near, far = near_ref[...].astype(F32), far_ref[...].astype(F32)
        to_east = self.info[3] == 1
        east, west = jnp.where(to_east, near, far), jnp.where(to_east, far, near)
        count = near.shape[0] // slots
        east = [east[i * slots : (i + 1) * slots] for i in range(count)]
        west = [west[i * slots : (i + 1) * slots] for i in range(count)]
        east = [jnp.where(self.info[1] == 1, self.across(x), x) for x in east]
        west = [jnp.where(self.info[2] == 1, self.across(x), x) for x in west]
        return east, west

    def packed(self, east_list, west_list, out_ref):
        east, west = jnp.concatenate(east_list, axis=0), jnp.concatenate(west_list, axis=0)
        out_ref[...] = jnp.where(self.info[3] == 1, east, west).astype(BF)


def place_of(slots):
    lat, rings = slots // 2, lax.axis_size("lon") // 2
    lon_at, lat_at = lax.axis_index("lon"), lax.axis_index("lat")
    ring_at, hemisphere = lax.rem(lon_at, rings), lax.div(lon_at, rings)
    core = lax.rem(lat_at, 2)
    return (
        hemisphere * lat + lat_at,
        (ring_at == rings - 1).astype(jnp.int32),
        (ring_at == 0).astype(jnp.int32),
        1 - lax.rem(ring_at + core, 2),
        core,
        lax.rem(lax.div(lat_at, 2), 2),
    )


def split_cells(row, slots):
    return [row[j * slots : (j + 1) * slots] for j in range(row.shape[0] // slots)]


def extend_and_send(ring, side, ext_ref, send_ref):
    slots = ring.slots
    width = side * slots
    pair = 2 * slots
    first_col, last_col = [], []
    for i in range(side):
        first_col.append(ext_ref[1 + i, 0:pair].astype(F32)[:slots])
        last_col.append(ext_ref[1 + i, width - pair : width].astype(F32)[slots:])
    edges = [
        split_cells(ext_ref[1].astype(F32), slots),
        split_cells(ext_ref[side].astype(F32), slots),
        first_col,
        last_col,
    ]
    south, north = ring.halo_rows(edges)
    ext_ref[0] = jnp.concatenate(south, axis=0).astype(BF)
    ext_ref[side + 1] = jnp.concatenate(north, axis=0).astype(BF)
    ring.packed(
        [south[-1]] + last_col + [north[-1]], [south[0]] + first_col + [north[0]], send_ref
    )


def pad_columns(ring, side, ext_ref, near_ref, far_ref, pad_ref):
    slots = ring.slots
    width = side * slots
    east, west = ring.arrived(near_ref, far_ref)
    low, high = ext_ref[0].astype(F32), ext_ref[side + 1].astype(F32)
    blends = (
        (0, west, 0, 1, low[:slots]),
        (1, east, 0, 1, low[width - slots :]),
        (2, west, side + 1, side, high[:slots]),
        (3, east, side + 1, side, high[width - slots :]),
    )
    for corner, column, at, beside, along in blends:
        blended = (0.5 * (along + column[beside])).astype(BF).astype(F32)
        column[at] = jnp.where(ring.flag(4 + corner) == 1.0, blended, column[at])
    for i in range(side + 2):
        pad_ref[i] = jnp.concatenate([west[i], ext_ref[i].astype(F32), east[i]], axis=0).astype(BF)


def windows(pad_ref, ext_ref, start, rows, width, slots, channels):
    left = pad_ref[pl.ds(start, rows), 0:width, :]
    middle = ext_ref[pl.ds(start, rows), :, :]
    right = pad_ref[pl.ds(start, rows), 2 * slots : 2 * slots + width, :]
    return jnp.concatenate([left, middle, right], axis=-1).reshape(rows * width, 3 * channels)


def convolved(pad_ref, ext_ref, weight_ref, start, rows, width, slots, channels):
    total = None
    for dh in range(3):
        window = windows(pad_ref, ext_ref, start + dh, rows, width, slots, channels)
        part = jnp.dot(window, weight_ref[dh], preferred_element_type=F32)
        total = part if total is None else total + part
    return total


def clear_edges(wide_ref, side, slots):
    width = side * slots
    blank = jnp.zeros((side, 2 * slots, wide_ref.shape[2]), BF)
    wide_ref[:, 0 : 2 * slots] = blank
    wide_ref[:, width + 2 * slots :] = blank


def put_gradient(wide_ref, shifted_ref, row, value, slots):
    width = value.shape[0]
    wide_ref[row, 2 * slots : 2 * slots + width] = value.astype(BF)
    blank = jnp.zeros((slots, value.shape[1]), F32)
    shifted_ref[row] = jnp.concatenate([blank, value, blank], axis=0).astype(BF)


def convolved_back(
    ring, side, wide_ref, shifted_ref, weight_ref, out_ref, send_ref, west_ref, east_ref
):
    slots, channels = ring.slots, ring.channels
    width, padded = side * slots, (side + 2) * slots
    depth = wide_ref.shape[2]
    rows = ROWS_PER_STEP

    def finish(row, total):
        out_ref[row] = total[slots : slots + width].astype(BF)
        west_ref[row] = total[:slots].astype(BF).astype(F32)
        east_ref[row] = total[slots + width :].astype(BF).astype(F32)

    waiting = {}
    for start in range(0, side, rows):
        windows_back = (
            wide_ref[start : start + rows, 2 * slots : 2 * slots + padded, :],
            shifted_ref[start : start + rows, :, :],
            wide_ref[start : start + rows, 0:padded, :],
        )
        product = None
        for dw, window in enumerate(windows_back):
            part = lax.dot_general(
                window.reshape(rows * padded, depth),
                weight_ref[:, dw].reshape(3 * channels, depth),
                (((1,), (1,)), ((), ())),
                preferred_element_type=F32,
            )
            product = part if product is None else product + part
        for row in range(rows):
            for dh in range(3):
                part = product[
                    row * padded : (row + 1) * padded, dh * channels : (dh + 1) * channels
                ]
                at = start + row + dh
                waiting[at] = waiting[at] + part if at in waiting else part
        for at in sorted(waiting):
            if at < start + rows or start + rows == side:
                finish(at, waiting.pop(at))
    pair = 2 * slots
    for corner, column_ref, at, beside, is_east in (
        (0, west_ref, 0, 1, False),
        (1, east_ref, 0, 1, True),
        (2, west_ref, side + 1, side, False),
        (3, east_ref, side + 1, side, True),
    ):
        value = column_ref[at]
        blended = ring.flag(4 + corner) == 1.0
        half = jnp.where(blended, 0.5 * value, 0.0)
        column_ref[beside] = column_ref[beside] + half
        column_ref[at] = jnp.where(blended, 0.0, value)
        if is_east:
            old = out_ref[at, width - pair : width].astype(F32)
            new = jnp.concatenate([old[:slots], old[slots:] + half], axis=0)
            out_ref[at, width - pair : width] = new.astype(BF)
        else:
            old = out_ref[at, 0:pair].astype(F32)
            new = jnp.concatenate([old[:slots] + half, old[slots:]], axis=0)
            out_ref[at, 0:pair] = new.astype(BF)
    ring.packed(
        [east_ref[i] for i in range(side + 2)], [west_ref[i] for i in range(side + 2)], send_ref
    )


def halo_back(ring, side, ext_ref, near_ref, far_ref, field_ref):
    slots = ring.slots
    width = side * slots
    east, west = ring.arrived(near_ref, far_ref)
    for i in range(side):
        field_ref[i] = ext_ref[1 + i].astype(F32)
    south = split_cells(ext_ref[0].astype(F32), slots)
    north = split_cells(ext_ref[side + 1].astype(F32), slots)
    south[0], south[-1] = south[0] + west[0], south[-1] + east[0]
    north[0], north[-1] = north[0] + west[-1], north[-1] + east[-1]
    low, high, first, last = ring.halo_rows_back(south, north)
    field_ref[0] += jnp.concatenate(low, axis=0)
    field_ref[side - 1] += jnp.concatenate(high, axis=0)
    for i in range(side):
        field_ref[i, 0:slots] += first[i] + west[1 + i]
        field_ref[i, width - slots : width] += last[i] + east[1 + i]


def collect_kernel(side, half, slots, *refs):
    info = place_of(slots)
    parts, (ext_ref, cot_ref, table_ref, send_ref), scratch = (
        refs[:slots],
        refs[slots : slots + 4],
        refs[slots + 4 :],
    )
    cells, cot_cells = side * side, half * half
    channels = ext_ref.shape[2]
    field_ref, low_ref, high_ref = scratch
    for index, part in enumerate(parts):
        slot = info[0] ^ index
        field_ref[pl.ds(slot, cells, stride=slots), :] = part[0:cells].astype(F32)
        low_ref[pl.ds(slot, cot_cells, stride=slots), :] = part[
            cells : cells + cot_cells
        ].astype(F32)
        high_ref[pl.ds(slot, cot_cells, stride=slots), :] = part[
            cells + cot_cells : cells + 2 * cot_cells
        ].astype(F32)
        flags = part[cells + 2 * cot_cells : cells + 2 * cot_cells + 16].astype(F32)
        table_ref[pl.ds(slot, 1), :] = flags[0:1]
    width = side * slots
    for i in range(side):
        ext_ref[1 + i] = field_ref[i * width : (i + 1) * width].astype(BF)
    cot_ref[:, 0:channels] = low_ref[...].astype(BF)
    cot_ref[:, channels : 2 * channels] = high_ref[...].astype(BF)
    ring = Ring(slots, channels, table_ref[...], info)
    extend_and_send(ring, side, ext_ref, send_ref)


def first_kernel(
    side, slots, ext_in, near_ref, far_ref, table_ref, weight_ref,
    pad_ref, ext_ref, slope_ref, send_ref,
):
    info = place_of(slots)
    channels, width = ext_in.shape[2], side * slots
    ring = Ring(slots, channels, table_ref[...], info)
    pad_columns(ring, side, ext_in, near_ref, far_ref, pad_ref)
    rows = ROWS_PER_STEP

    def step(index, carry):
        start = index * rows
        z = convolved(pad_ref, ext_in, weight_ref, start, rows, width, slots, channels)
        cdf, pdf = normal_parts(z)
        shape = (rows, width, z.shape[1])
        ext_ref[pl.ds(start + 1, rows)] = (z * cdf).astype(BF).reshape(shape)
        slope_ref[pl.ds(start, rows)] = (cdf + z * pdf).astype(BF).reshape(shape)
        return carry

    for index in range(side // rows):
        step(index, 0)
    ring = Ring(slots, ext_ref.shape[2], table_ref[...], info)
    extend_and_send(ring, side, ext_ref, send_ref)


def second_kernel(
    side, slots, ext_in, near_ref, far_ref, table_ref, cot_ref, weight_ref, back_ref,
    pad_ref, grad_ref, pooled_ref, ext_ref, send_ref,
    wide_ref, shifted_ref, mean_ref, west_ref, east_ref,
):
    info = place_of(slots)
    channels, width = ext_in.shape[2], side * slots
    ring = Ring(slots, channels, table_ref[...], info)
    pad_columns(ring, side, ext_in, near_ref, far_ref, pad_ref)
    clear_edges(wide_ref, side, slots)
    rows = ROWS_PER_STEP
    half = side // 2
    step_cells = (rows // 2) * half * slots

    def step(index, carry):
        start = index * rows
        z = convolved(pad_ref, ext_in, weight_ref, start, rows, width, slots, channels)
        cdf, pdf = normal_parts(z)
        paired = (rows // 2, 2, half, 2, slots, channels)
        value = (z * cdf).reshape(paired)
        cells = pl.ds(index * step_cells, step_cells)
        mean = (value[:, 0, :, 0] + value[:, 0, :, 1]) + (value[:, 1, :, 0] + value[:, 1, :, 1])
        mean = mean.reshape(step_cells, channels) * 0.25
        for block in range(channels // 128):
            mean_ref[block, cells, :] = mean[:, block * 128 : (block + 1) * 128]
        cot = cot_ref[cells, :].astype(F32) * 0.25
        cot = cot.reshape(rows // 2, 1, half, 1, slots, channels)
        slope = (cdf + z * pdf).reshape(paired)
        grad = (jnp.broadcast_to(cot, paired) * slope).reshape(rows, width, channels)
        grad_ref[pl.ds(start, rows)] = grad.astype(BF)
        for row in range(rows):
            put_gradient(wide_ref, shifted_ref, start + row, grad[row], slots)
        return carry

    for index in range(side // rows):
        step(index, 0)
    for block in range(channels // 128):
        pooled_ref[:, block * 128 : (block + 1) * 128] = mean_ref[
            block, pl.ds(info[0], half * half, stride=slots), :
        ].astype(BF)
    convolved_back(
        ring, side, wide_ref, shifted_ref, back_ref, ext_ref, send_ref, west_ref, east_ref
    )


def third_kernel(
    side, slots, ext_in, near_ref, far_ref, table_ref, slope_ref, pad_ref, features_ref,
    grad_ref, low_ref, high_ref,
    field_ref,
):
    info = place_of(slots)
    ring = Ring(slots, ext_in.shape[2], table_ref[...], info)
    halo_back(ring, side, ext_in, near_ref, far_ref, field_ref)
    for i in range(side):
        grad_ref[i] = (field_ref[i] * slope_ref[i].astype(F32)).astype(BF)
    columns = low_ref.shape[2]
    start = pl.multiple_of(info[4] * columns, columns)
    grad = grad_ref[:, :, pl.ds(start, columns)].reshape(side * side * slots, columns)

    weight_products(side, slots, pad_ref, features_ref, grad, 0, low_ref, high_ref)


def fourth_kernel(
    side, slots, grad_ref, table_ref, back_ref,
    ext_ref, send_ref,
    wide_ref, shifted_ref, west_ref, east_ref,
):
    info = place_of(slots)
    clear_edges(wide_ref, side, slots)
    for i in range(side):
        put_gradient(wide_ref, shifted_ref, i, grad_ref[i].astype(F32), slots)
    ring = Ring(slots, ext_ref.shape[2], table_ref[...], info)
    convolved_back(
        ring, side, wide_ref, shifted_ref, back_ref, ext_ref, send_ref, west_ref, east_ref
    )


def last_kernel(
    side, slots, ext_in, near_ref, far_ref, table_ref, out_ref, field_ref, flat_ref
):
    info = place_of(slots)
    width = side * slots
    ring = Ring(slots, ext_in.shape[2], table_ref[...], info)
    halo_back(ring, side, ext_in, near_ref, far_ref, field_ref)
    for i in range(side):
        flat_ref[i * width : (i + 1) * width] = field_ref[i]
    out_ref[...] = flat_ref[pl.ds(info[0], side * side, stride=slots), :].astype(BF)


def weight_products(side, slots, pad_ref, ext_ref, grad, first, low_ref, high_ref):
    width, half = side * slots, low_ref.shape[1]
    channels = 2 * half
    lanes = pl.ds(first, channels)

    def step(dh, carry):
        rows = pl.ds(dh, side)
        window = jnp.concatenate(
            [
                pad_ref[rows, 0:width, lanes],
                ext_ref[rows, :, lanes],
                pad_ref[rows, 2 * slots : 2 * slots + width, lanes],
            ],
            axis=-1,
        ).reshape(side * width, 3 * channels)
        product = lax.dot_general(
            window, grad, (((0,), (0,)), ((), ())), preferred_element_type=F32
        ).astype(BF)
        for dw in range(3):
            at = dw * channels
            low_ref[dh * 3 + dw] = product[at : at + half]
            high_ref[dh * 3 + dw] = product[at + half : at + channels]
        return carry

    lax.fori_loop(0, 3, step, 0)


def weight_kernel(side, slots, pad_ref, ext_ref, grad_ref, low_ref, high_ref):
    info = place_of(slots)
    rows, columns = 2 * low_ref.shape[1], low_ref.shape[2]
    start = pl.multiple_of(info[4] * columns, columns)
    grad = grad_ref[:, :, pl.ds(start, columns)].reshape(side * side * slots, columns)
    first = pl.multiple_of(info[5] * rows, rows)
    weight_products(side, slots, pad_ref, ext_ref, grad, first, low_ref, high_ref)


def join_kernel(low_ref, low_other, high_ref, high_other, out_ref):
    rows = low_ref.shape[1]
    out_ref[:, 0:rows] = (low_ref[...].astype(F32) + low_other[...].astype(F32)).astype(BF)
    out_ref[:, rows:] = (high_ref[...].astype(F32) + high_other[...].astype(F32)).astype(BF)


def scale_kernel(slots, target, *refs):
    info = place_of(slots)
    blocks, (first_out, second_out) = refs[:-2], refs[-2:]
    squared = jnp.zeros((1, 1), F32)
    for ref in blocks:
        value = ref[...].astype(F32)
        lanes = jnp.sum(jnp.sum(value * value, axis=0), axis=0, keepdims=True)
        squared = squared + jnp.sum(lanes, axis=1, keepdims=True)
    scale = target / jnp.sqrt(squared + 1e-06)
    for index, ref in enumerate(blocks):
        core = info[4] if index % 2 == 0 else 1 - info[4]
        rows, columns = ref.shape[1:]
        lanes = pl.ds(pl.multiple_of(core * columns, columns), columns)
        value = (ref[...].astype(F32) * scale).astype(BF)
        if index < 2:
            first_out[:, :, lanes] = value
        else:
            block = info[5] if index < 4 else 1 - info[5]
            second_out[:, pl.ds(pl.multiple_of(block * rows, rows), rows), lanes] = value


class RingSums:
    def __init__(self, rings, swap, values):
        self.values, self.swap, self.at, self.arriving = list(values), swap, 0, []
        steps = [1 << k for k in range(rings.bit_length() - 1)]
        self.even = rings == 1 << len(steps)
        self.rounds = len(steps) if self.even else 1
        self.orders = (steps, steps[::-1])

    def send(self):
        if self.even:
            self.arriving = [
                self.swap(value, order[self.at]) for value, order in zip(self.values, self.orders)
            ]
        else:
            totals = [0.5 * lax.psum(value.astype(F32), "lon") for value in self.values]
            self.arriving = [total - value for total, value in zip(totals, self.values)]
        self.at += 1

    def joined(self):
        (low, high), (low_other, high_other) = self.values, self.arriving
        taps, rows, columns = low.shape
        out = jax.ShapeDtypeStruct((taps, 2 * rows, columns), BF)
        return run(join_kernel, [out], [low, low_other, high, high_other])[0]

    def add(self):
        self.values = [
            (value.astype(F32) + other.astype(F32)).astype(BF)
            for value, other in zip(self.values, self.arriving)
        ]


def run(kernel, outs, args, scratch=(), flops=0, vmem_mib=8):
    vmem = pl.BlockSpec(memory_space=pltpu.VMEM)
    moved = sum(math.prod(x.shape) * x.dtype.itemsize for x in list(args) + list(outs))
    return pl.pallas_call(
        kernel,
        out_shape=tuple(outs),
        in_specs=[vmem] * len(args),
        out_specs=tuple(vmem for _ in outs),
        scratch_shapes=list(scratch),
        compiler_params=pltpu.CompilerParams(vmem_limit_bytes=vmem_mib * 1024 * 1024),
        cost_estimate=pl.CostEstimate(flops=flops, bytes_accessed=moved, transcendentals=0),
    )(*args)


def on_device(lon, lat, features, conv_first, conv_second, cotangent, edge_pick, edge_flip, corner_rule):
    side, c_in = features.shape[2], features.shape[4]
    half, c_out = cotangent.shape[2], cotangent.shape[4]
    slots, rings = 2 * lat, lon // 2
    width, padded = side * slots, (side + 2) * slots
    axes = ("lon", "lat")

    def spec(shape, dtype=BF):
        return jax.ShapeDtypeStruct(shape, dtype)

    def vmem(shape, dtype):
        return pltpu.VMEM(shape, dtype)

    def permuted(value, partner):
        pairs = []
        for place in range(lon):
            for band in range(lat):
                there = partner(place, band)
                pairs.append((place * lat + band, there[0] * lat + there[1]))
        return lax.ppermute(value, axes, pairs)

    def core_swap(value):
        return permuted(value, lambda place, band: (place, band ^ 1))

    def x_swap(value):
        return permuted(value, lambda place, band: (place, band ^ 2))

    def ring_swap(value, step):
        return permuted(
            value, lambda place, band: (((place % rings) ^ step) + place // rings * rings, band)
        )

    def beside(place, band):
        ring, upper = place % rings, place // rings
        east = (ring + band) % 2 == 0
        return ((ring + (1 if east else -1)) % rings + upper * rings, band)

    def exchange(value):
        near = permuted(value, beside)
        return near, core_swap(near)

    cells, quarter = side * side, half * half
    total = cells + 2 * quarter + 16
    cot = cotangent.reshape(quarter, c_out)

    def placed(value, row, lane=0):
        rows, lanes = value.shape
        return jnp.pad(value, ((row, total - row - rows), (lane, c_in - lane - lanes)))

    flags, at = 0, 0
    for values in (edge_pick[0], edge_flip[0], corner_rule[0]):
        flags = flags + placed(values, total - 16, at)
        at += values.shape[1]
    own = placed(features.reshape(cells, c_in), 0) + flags.astype(BF)
    own = own + placed(cot[:, :c_in], cells) + placed(cot[:, c_in:], cells + quarter)
    parts = [None] * slots
    parts[0] = own
    for index in [*range(lat, slots, 2), *range(2, lat, 2)]:
        parts[index] = permuted(
            own,
            lambda place, band, index=index: (
                (place + rings * (index // lat)) % lon,
                band ^ (index % lat),
            ),
        )
    for index in range(0, slots, 2):
        parts[index + 1] = core_swap(parts[index])

    first_weight = conv_first.reshape(3, 3 * c_in, c_out)
    second_weight = conv_second.reshape(3, 3 * c_out, c_out)

    features_ext, cot_ring, table, columns = run(
        functools.partial(collect_kernel, side, half, slots),
        [
            spec((side + 2, width, c_in)),
            spec((half * half * slots, c_out)),
            spec((slots, c_in), F32),
            spec((padded, c_in)),
        ],
        parts,
        [
            vmem((side * width, c_in), F32),
            vmem((half * half * slots, c_in), F32),
            vmem((half * half * slots, c_in), F32),
        ],
        flops=4_000_000_000,
    )
    near, far = exchange(columns)
    work = 2 * side * width * 9 * c_in * c_out
    features_pad, act_ext, slope, columns = run(
        functools.partial(first_kernel, side, slots),
        [
            spec((side + 2, padded, c_in)),
            spec((side + 2, width, c_out)),
            spec((side, width, c_out)),
            spec((padded, c_out)),
        ],
        [features_ext, near, far, table, first_weight],
        flops=work,
    )
    near, far = exchange(columns)
    back_scratch = [
        vmem((side, (side + 4) * slots, c_out), BF),
        vmem((side, padded, c_out), BF),
    ]
    act_pad, second_grad, pooled, act_grad, columns = run(
        functools.partial(second_kernel, side, slots),
        [
            spec((side + 2, padded, c_out)),
            spec((side, width, c_out)),
            spec((half * half, c_out)),
            spec((side + 2, width, c_out)),
            spec((padded, c_out)),
        ],
        [act_ext, near, far, table, cot_ring, second_weight, conv_second],
        back_scratch
        + [
            vmem((c_out // 128, half * half * slots, 128), F32),
            vmem((side + 2, slots, c_out), F32),
            vmem((side + 2, slots, c_out), F32),
        ],
        flops=4 * work,
    )
    near = permuted(columns, beside)
    part = c_out // 2
    second_low, second_high = run(
        functools.partial(weight_kernel, side, slots),
        [spec((9, c_out // 4, part)), spec((9, c_out // 4, part))],
        [act_pad, act_ext, second_grad],
        flops=work,
    )
    near, second_low, second_high = lax.optimization_barrier((near, second_low, second_high))
    far = core_swap(near)
    second_sums = RingSums(rings, ring_swap, (second_low, second_high))
    second_sums.send()
    pre_grad, first_low, first_high = run(
        functools.partial(third_kernel, side, slots),
        [
            spec((side, width, c_out)),
            spec((9, c_in // 2, part)),
            spec((9, c_in // 2, part)),
        ],
        [act_grad, near, far, table, slope, features_pad, features_ext],
        [vmem((side, width, c_out), F32)],
        flops=work,
    )
    features_grad, columns = run(
        functools.partial(fourth_kernel, side, slots),
        [spec((side + 2, width, c_in)), spec((padded, c_in))],
        [pre_grad, table, conv_first],
        back_scratch + [vmem((side + 2, slots, c_in), F32), vmem((side + 2, slots, c_in), F32)],
        flops=work,
    )
    *second_sums.arriving, first_low, first_high, columns = lax.optimization_barrier(
        (*second_sums.arriving, first_low, first_high, columns)
    )
    first_sums = RingSums(rings, ring_swap, (first_low, first_high))
    first_sums.send()
    near = permuted(columns, beside)
    for _ in range(second_sums.rounds - 1):
        second_sums.add()
        second_sums.send()
        first_sums.add()
        *first_sums.values, near = lax.optimization_barrier((*first_sums.values, near))
        first_sums.send()
    far = core_swap(near)
    input_grad = run(
        functools.partial(last_kernel, side, slots),
        [spec((side * side, c_in))],
        [features_grad, near, far, table],
        [vmem((side, width, c_in), F32), vmem((side * width, c_in), F32)],
    )[0]
    second_total = second_sums.joined()
    *first_sums.arriving, input_grad = lax.optimization_barrier((*first_sums.arriving, input_grad))
    blocks = []
    for block in (first_sums.joined(), second_total, x_swap(second_total)):
        blocks += [block, core_swap(block)]
    target = math.sqrt(9.0 * (c_in + c_out) * c_out)
    scaled_first, scaled_second = run(
        functools.partial(scale_kernel, slots, target),
        [spec((9, c_in, c_out)), spec((9, c_out, c_out))],
        blocks,
    )
    return (
        pooled.reshape(1, 1, half, half, c_out),
        input_grad.reshape(1, 1, side, side, c_in),
        scaled_first.reshape(3, 3, c_in, c_out),
        scaled_second.reshape(3, 3, c_out, c_out),
    )


def solution(mesh):
    return jax.shard_map(
        functools.partial(on_device, mesh.shape["lon"], mesh.shape["lat"]),
        mesh=mesh,
        in_specs=(
            P("lon", "lat", None, None, None),
            P(),
            P(),
            P("lon", "lat", None, None, None),
            P("lon", "lat", None),
            P("lon", "lat", None),
            P("lon", "lat", None),
        ),
        out_specs=(P("lon", "lat", None, None, None), P("lon", "lat", None, None, None), P(), P()),
        check_vma=False,
    )
```

```python
import functools
import math

import jax
import jax.numpy as jnp
from jax import lax
from jax.experimental import pallas as pl
from jax.experimental.pallas import tpu as pltpu
from jax.sharding import PartitionSpec as P


BF = jnp.bfloat16
F32 = jnp.float32
ROWS_PER_STEP = 4


def normal_parts(z):
    cdf = 0.5 * (1.0 + lax.erf(z * (1.0 / math.sqrt(2.0))))
    pdf = jnp.exp(-0.5 * z * z) * (1.0 / math.sqrt(2.0 * math.pi))
    return cdf, pdf


class Ring:
    def __init__(self, slots, channels, table, info):
        self.slots, self.band = slots, slots // 2
        self.channels, self.info = channels, info
        place = lax.broadcasted_iota(jnp.int32, (slots, channels), 0)
        self.top = lax.rem(place, self.band) == self.band - 1
        self.bottom = lax.rem(place, self.band) == 0
        self.table = table

    def flag(self, column):
        return jnp.broadcast_to(self.table[:, column : column + 1], (self.slots, self.channels))

    def up(self, x):
        return pltpu.roll(x, self.slots - 1, 0)

    def down(self, x):
        return pltpu.roll(x, 1, 0)

    def across(self, x):
        return pltpu.roll(x, self.band, 0)

    def take(self, edges, side, to_source, to_slot):
        pick, flip = to_source(self.flag(side)), to_source(self.flag(2 + side))
        count = len(edges[0])
        chosen = [
            jnp.where(
                pick == 0.0,
                edges[0][j],
                jnp.where(
                    pick == 1.0, edges[1][j], jnp.where(pick == 2.0, edges[2][j], edges[3][j])
                ),
            )
            for j in range(count)
        ]
        return [
            to_slot(jnp.where(flip == 1.0, chosen[count - 1 - j], chosen[j])) for j in range(count)
        ]

    def halo_rows(self, edges):
        same = self.take(edges, 0, self.up, self.down)
        pole = self.take(edges, 0, self.across, self.across)
        south = [jnp.where(self.bottom, b, a) for a, b in zip(same, pole)]
        same = self.take(edges, 1, self.down, self.up)
        pole = self.take(edges, 1, self.across, self.across)
        north = [jnp.where(self.top, b, a) for a, b in zip(same, pole)]
        return south, north

    def give(self, totals, rows, side, to_source):
        pick, flip = to_source(self.flag(side)), to_source(self.flag(2 + side))
        count = len(rows)
        moved = [to_source(row) for row in rows]
        for j in range(count):
            value = jnp.where(flip == 1.0, moved[count - 1 - j], moved[j])
            for edge in range(4):
                share = jnp.where(pick == float(edge), value, 0.0)
                totals[edge][j] = share if totals[edge][j] is None else totals[edge][j] + share

    def halo_rows_back(self, south, north):
        totals = [[None] * len(south) for _ in range(4)]
        self.give(totals, [jnp.where(self.bottom, 0.0, x) for x in south], 0, self.up)
        self.give(totals, [jnp.where(self.bottom, x, 0.0) for x in south], 0, self.across)
        self.give(totals, [jnp.where(self.top, 0.0, x) for x in north], 1, self.down)
        self.give(totals, [jnp.where(self.top, x, 0.0) for x in north], 1, self.across)
        return totals

    def arrived(self, near_ref, far_ref):
        slots = self.slots
        near, far = near_ref[...].astype(F32), far_ref[...].astype(F32)
        to_east = self.info[3] == 1
        east, west = jnp.where(to_east, near, far), jnp.where(to_east, far, near)
        count = near.shape[0] // slots
        east = [east[i * slots : (i + 1) * slots] for i in range(count)]
        west = [west[i * slots : (i + 1) * slots] for i in range(count)]
        east = [jnp.where(self.info[1] == 1, self.across(x), x) for x in east]
        west = [jnp.where(self.info[2] == 1, self.across(x), x) for x in west]
        return east, west

    def packed(self, east_list, west_list, out_ref):
        east, west = jnp.concatenate(east_list, axis=0), jnp.concatenate(west_list, axis=0)
        out_ref[...] = jnp.where(self.info[3] == 1, east, west).astype(BF)


def place_of(slots):
    lat, rings = slots // 2, lax.axis_size("lon") // 2
    lon_at, lat_at = lax.axis_index("lon"), lax.axis_index("lat")
    ring_at, hemisphere = lax.rem(lon_at, rings), lax.div(lon_at, rings)
    core = lax.rem(lat_at, 2)
    return (
        hemisphere * lat + lat_at,
        (ring_at == rings - 1).astype(jnp.int32),
        (ring_at == 0).astype(jnp.int32),
        1 - lax.rem(ring_at + core, 2),
        core,
        lax.rem(lax.div(lat_at, 2), 2),
    )


def split_cells(row, slots):
    return [row[j * slots : (j + 1) * slots] for j in range(row.shape[0] // slots)]


def extend_and_send(ring, side, ext_ref, send_ref):
    slots = ring.slots
    width = side * slots
    pair = 2 * slots
    first_col, last_col = [], []
    for i in range(side):
        first_col.append(ext_ref[1 + i, 0:pair].astype(F32)[:slots])
        last_col.append(ext_ref[1 + i, width - pair : width].astype(F32)[slots:])
    edges = [
        split_cells(ext_ref[1].astype(F32), slots),
        split_cells(ext_ref[side].astype(F32), slots),
        first_col,
        last_col,
    ]
    south, north = ring.halo_rows(edges)
    ext_ref[0] = jnp.concatenate(south, axis=0).astype(BF)
    ext_ref[side + 1] = jnp.concatenate(north, axis=0).astype(BF)
    ring.packed(
        [south[-1]] + last_col + [north[-1]], [south[0]] + first_col + [north[0]], send_ref
    )


def pad_columns(ring, side, ext_ref, near_ref, far_ref, pad_ref):
    slots = ring.slots
    width = side * slots
    east, west = ring.arrived(near_ref, far_ref)
    low, high = ext_ref[0].astype(F32), ext_ref[side + 1].astype(F32)
    blends = (
        (0, west, 0, 1, low[:slots]),
        (1, east, 0, 1, low[width - slots :]),
        (2, west, side + 1, side, high[:slots]),
        (3, east, side + 1, side, high[width - slots :]),
    )
    for corner, column, at, beside, along in blends:
        blended = (0.5 * (along + column[beside])).astype(BF).astype(F32)
        column[at] = jnp.where(ring.flag(4 + corner) == 1.0, blended, column[at])
    for i in range(side + 2):
        pad_ref[i] = jnp.concatenate([west[i], ext_ref[i].astype(F32), east[i]], axis=0).astype(BF)


def windows(pad_ref, ext_ref, start, rows, width, slots, channels):
    left = pad_ref[pl.ds(start, rows), 0:width, :]
    middle = ext_ref[pl.ds(start, rows), :, :]
    right = pad_ref[pl.ds(start, rows), 2 * slots : 2 * slots + width, :]
    return jnp.concatenate([left, middle, right], axis=-1).reshape(rows * width, 3 * channels)


def convolved(pad_ref, ext_ref, weight_ref, start, rows, width, slots, channels):
    total = None
    for dh in range(3):
        window = windows(pad_ref, ext_ref, start + dh, rows, width, slots, channels)
        part = jnp.dot(window, weight_ref[dh], preferred_element_type=F32)
        total = part if total is None else total + part
    return total


def clear_edges(wide_ref, side, slots):
    width = side * slots
    blank = jnp.zeros((side, 2 * slots, wide_ref.shape[2]), BF)
    wide_ref[:, 0 : 2 * slots] = blank
    wide_ref[:, width + 2 * slots :] = blank


def put_gradient(wide_ref, shifted_ref, row, value, slots):
    width = value.shape[0]
    wide_ref[row, 2 * slots : 2 * slots + width] = value.astype(BF)
    blank = jnp.zeros((slots, value.shape[1]), F32)
    shifted_ref[row] = jnp.concatenate([blank, value, blank], axis=0).astype(BF)


def convolved_back(
    ring, side, wide_ref, shifted_ref, weight_ref, out_ref, send_ref, west_ref, east_ref
):
    slots, channels = ring.slots, ring.channels
    width, padded = side * slots, (side + 2) * slots
    depth = wide_ref.shape[2]
    rows = ROWS_PER_STEP

    def finish(row, total):
        out_ref[row] = total[slots : slots + width].astype(BF)
        west_ref[row] = total[:slots].astype(BF).astype(F32)
        east_ref[row] = total[slots + width :].astype(BF).astype(F32)

    waiting = {}
    for start in range(0, side, rows):
        windows_back = (
            wide_ref[start : start + rows, 2 * slots : 2 * slots + padded, :],
            shifted_ref[start : start + rows, :, :],
            wide_ref[start : start + rows, 0:padded, :],
        )
        product = None
        for dw, window in enumerate(windows_back):
            part = lax.dot_general(
                window.reshape(rows * padded, depth),
                weight_ref[:, dw].reshape(3 * channels, depth),
                (((1,), (1,)), ((), ())),
                preferred_element_type=F32,
            )
            product = part if product is None else product + part
        for row in range(rows):
            for dh in range(3):
                part = product[
                    row * padded : (row + 1) * padded, dh * channels : (dh + 1) * channels
                ]
                at = start + row + dh
                waiting[at] = waiting[at] + part if at in waiting else part
        for at in sorted(waiting):
            if at < start + rows or start + rows == side:
                finish(at, waiting.pop(at))
    pair = 2 * slots
    for corner, column_ref, at, beside, is_east in (
        (0, west_ref, 0, 1, False),
        (1, east_ref, 0, 1, True),
        (2, west_ref, side + 1, side, False),
        (3, east_ref, side + 1, side, True),
    ):
        value = column_ref[at]
        blended = ring.flag(4 + corner) == 1.0
        half = jnp.where(blended, 0.5 * value, 0.0)
        column_ref[beside] = column_ref[beside] + half
        column_ref[at] = jnp.where(blended, 0.0, value)
        if is_east:
            old = out_ref[at, width - pair : width].astype(F32)
            new = jnp.concatenate([old[:slots], old[slots:] + half], axis=0)
            out_ref[at, width - pair : width] = new.astype(BF)
        else:
            old = out_ref[at, 0:pair].astype(F32)
            new = jnp.concatenate([old[:slots] + half, old[slots:]], axis=0)
            out_ref[at, 0:pair] = new.astype(BF)
    ring.packed(
        [east_ref[i] for i in range(side + 2)], [west_ref[i] for i in range(side + 2)], send_ref
    )


def halo_back(ring, side, ext_ref, near_ref, far_ref, field_ref):
    slots = ring.slots
    width = side * slots
    east, west = ring.arrived(near_ref, far_ref)
    for i in range(side):
        field_ref[i] = ext_ref[1 + i].astype(F32)
    south = split_cells(ext_ref[0].astype(F32), slots)
    north = split_cells(ext_ref[side + 1].astype(F32), slots)
    south[0], south[-1] = south[0] + west[0], south[-1] + east[0]
    north[0], north[-1] = north[0] + west[-1], north[-1] + east[-1]
    low, high, first, last = ring.halo_rows_back(south, north)
    field_ref[0] += jnp.concatenate(low, axis=0)
    field_ref[side - 1] += jnp.concatenate(high, axis=0)
    for i in range(side):
        field_ref[i, 0:slots] += first[i] + west[1 + i]
        field_ref[i, width - slots : width] += last[i] + east[1 + i]


def collect_kernel(side, half, slots, *refs):
    info = place_of(slots)
    parts, (ext_ref, cot_ref, table_ref, send_ref), scratch = (
        refs[:slots],
        refs[slots : slots + 4],
        refs[slots + 4 :],
    )
    cells, cot_cells = side * side, half * half
    channels = ext_ref.shape[2]
    field_ref, low_ref, high_ref = scratch
    for index, part in enumerate(parts):
        slot = info[0] ^ index
        field_ref[pl.ds(slot, cells, stride=slots), :] = part[0:cells].astype(F32)
        low_ref[pl.ds(slot, cot_cells, stride=slots), :] = part[
            cells : cells + cot_cells
        ].astype(F32)
        high_ref[pl.ds(slot, cot_cells, stride=slots), :] = part[
            cells + cot_cells : cells + 2 * cot_cells
        ].astype(F32)
        flags = part[cells + 2 * cot_cells : cells + 2 * cot_cells + 16].astype(F32)
        table_ref[pl.ds(slot, 1), :] = flags[0:1]
    width = side * slots
    for i in range(side):
        ext_ref[1 + i] = field_ref[i * width : (i + 1) * width].astype(BF)
    cot_ref[:, 0:channels] = low_ref[...].astype(BF)
    cot_ref[:, channels : 2 * channels] = high_ref[...].astype(BF)
    ring = Ring(slots, channels, table_ref[...], info)
    extend_and_send(ring, side, ext_ref, send_ref)


def first_kernel(
    side, slots, ext_in, near_ref, far_ref, table_ref, weight_ref,
    pad_ref, ext_ref, slope_ref, send_ref,
):
    info = place_of(slots)
    channels, width = ext_in.shape[2], side * slots
    ring = Ring(slots, channels, table_ref[...], info)
    pad_columns(ring, side, ext_in, near_ref, far_ref, pad_ref)
    rows = ROWS_PER_STEP

    def step(index, carry):
        start = index * rows
        z = convolved(pad_ref, ext_in, weight_ref, start, rows, width, slots, channels)
        cdf, pdf = normal_parts(z)
        shape = (rows, width, z.shape[1])
        ext_ref[pl.ds(start + 1, rows)] = (z * cdf).astype(BF).reshape(shape)
        slope_ref[pl.ds(start, rows)] = (cdf + z * pdf).astype(BF).reshape(shape)
        return carry

    for index in range(side // rows):
        step(index, 0)
    ring = Ring(slots, ext_ref.shape[2], table_ref[...], info)
    extend_and_send(ring, side, ext_ref, send_ref)


def second_kernel(
    side, slots, ext_in, near_ref, far_ref, table_ref, cot_ref, weight_ref, back_ref,
    pad_ref, grad_ref, pooled_ref, ext_ref, send_ref,
    wide_ref, shifted_ref, mean_ref, west_ref, east_ref,
):
    info = place_of(slots)
    channels, width = ext_in.shape[2], side * slots
    ring = Ring(slots, channels, table_ref[...], info)
    pad_columns(ring, side, ext_in, near_ref, far_ref, pad_ref)
    clear_edges(wide_ref, side, slots)
    rows = ROWS_PER_STEP
    half = side // 2
    step_cells = (rows // 2) * half * slots

    def step(index, carry):
        start = index * rows
        z = convolved(pad_ref, ext_in, weight_ref, start, rows, width, slots, channels)
        cdf, pdf = normal_parts(z)
        paired = (rows // 2, 2, half, 2, slots, channels)
        value = (z * cdf).reshape(paired)
        cells = pl.ds(index * step_cells, step_cells)
        mean = (value[:, 0, :, 0] + value[:, 0, :, 1]) + (value[:, 1, :, 0] + value[:, 1, :, 1])
        mean = mean.reshape(step_cells, channels) * 0.25
        for block in range(channels // 128):
            mean_ref[block, cells, :] = mean[:, block * 128 : (block + 1) * 128]
        cot = cot_ref[cells, :].astype(F32) * 0.25
        cot = cot.reshape(rows // 2, 1, half, 1, slots, channels)
        slope = (cdf + z * pdf).reshape(paired)
        grad = (jnp.broadcast_to(cot, paired) * slope).reshape(rows, width, channels)
        grad_ref[pl.ds(start, rows)] = grad.astype(BF)
        for row in range(rows):
            put_gradient(wide_ref, shifted_ref, start + row, grad[row], slots)
        return carry

    for index in range(side // rows):
        step(index, 0)
    for block in range(channels // 128):
        pooled_ref[:, block * 128 : (block + 1) * 128] = mean_ref[
            block, pl.ds(info[0], half * half, stride=slots), :
        ].astype(BF)
    convolved_back(
        ring, side, wide_ref, shifted_ref, back_ref, ext_ref, send_ref, west_ref, east_ref
    )


def third_kernel(
    side, slots, ext_in, near_ref, far_ref, table_ref, slope_ref, pad_ref, features_ref,
    grad_ref, out_ref,
    field_ref,
):
    info = place_of(slots)
    ring = Ring(slots, ext_in.shape[2], table_ref[...], info)
    halo_back(ring, side, ext_in, near_ref, far_ref, field_ref)
    for i in range(side):
        grad_ref[i] = (field_ref[i] * slope_ref[i].astype(F32)).astype(BF)
    columns = out_ref.shape[2]
    start = pl.multiple_of(info[4] * columns, columns)
    grad = grad_ref[:, :, pl.ds(start, columns)].reshape(side * side * slots, columns)

    weight_products(side, slots, pad_ref, features_ref, grad, 0, out_ref)


def fourth_kernel(
    side, slots, grad_ref, table_ref, back_ref,
    ext_ref, send_ref,
    wide_ref, shifted_ref, west_ref, east_ref,
):
    info = place_of(slots)
    clear_edges(wide_ref, side, slots)
    for i in range(side):
        put_gradient(wide_ref, shifted_ref, i, grad_ref[i].astype(F32), slots)
    ring = Ring(slots, ext_ref.shape[2], table_ref[...], info)
    convolved_back(
        ring, side, wide_ref, shifted_ref, back_ref, ext_ref, send_ref, west_ref, east_ref
    )


def last_kernel(
    side, slots, ext_in, near_ref, far_ref, table_ref, out_ref, field_ref, flat_ref
):
    info = place_of(slots)
    width = side * slots
    ring = Ring(slots, ext_in.shape[2], table_ref[...], info)
    halo_back(ring, side, ext_in, near_ref, far_ref, field_ref)
    for i in range(side):
        flat_ref[i * width : (i + 1) * width] = field_ref[i]
    out_ref[...] = flat_ref[pl.ds(info[0], side * side, stride=slots), :].astype(BF)


def weight_products(side, slots, pad_ref, ext_ref, grad, first, out_ref):
    width, channels = side * slots, out_ref.shape[1]
    lanes = pl.ds(first, channels)

    def step(dh, carry):
        rows = pl.ds(dh, side)
        window = jnp.concatenate(
            [
                pad_ref[rows, 0:width, lanes],
                ext_ref[rows, :, lanes],
                pad_ref[rows, 2 * slots : 2 * slots + width, lanes],
            ],
            axis=-1,
        ).reshape(side * width, 3 * channels)
        product = lax.dot_general(
            window, grad, (((0,), (0,)), ((), ())), preferred_element_type=F32
        ).astype(BF)
        for dw in range(3):
            out_ref[dh * 3 + dw] = product[dw * channels : (dw + 1) * channels]
        return carry

    lax.fori_loop(0, 3, step, 0)


def weight_kernel(side, slots, pad_ref, ext_ref, grad_ref, out_ref):
    info = place_of(slots)
    rows, columns = out_ref.shape[1:]
    start = pl.multiple_of(info[4] * columns, columns)
    grad = grad_ref[:, :, pl.ds(start, columns)].reshape(side * side * slots, columns)
    first = pl.multiple_of(info[5] * rows, rows)
    weight_products(side, slots, pad_ref, ext_ref, grad, first, out_ref)


def scale_kernel(slots, target, *refs):
    info = place_of(slots)
    blocks, (first_out, second_out) = refs[:-2], refs[-2:]
    squared = jnp.zeros((1, 1), F32)
    for ref in blocks:
        value = ref[...].astype(F32)
        lanes = jnp.sum(jnp.sum(value * value, axis=0), axis=0, keepdims=True)
        squared = squared + jnp.sum(lanes, axis=1, keepdims=True)
    scale = target / jnp.sqrt(squared + 1e-06)
    for index, ref in enumerate(blocks):
        core = info[4] if index % 2 == 0 else 1 - info[4]
        rows, columns = ref.shape[1:]
        lanes = pl.ds(pl.multiple_of(core * columns, columns), columns)
        value = (ref[...].astype(F32) * scale).astype(BF)
        if index < 2:
            first_out[:, :, lanes] = value
        else:
            block = info[5] if index < 4 else 1 - info[5]
            second_out[:, pl.ds(pl.multiple_of(block * rows, rows), rows), lanes] = value


def run(kernel, outs, args, scratch=(), flops=0, vmem_mib=8):
    vmem = pl.BlockSpec(memory_space=pltpu.VMEM)
    moved = sum(math.prod(x.shape) * x.dtype.itemsize for x in list(args) + list(outs))
    return pl.pallas_call(
        kernel,
        out_shape=tuple(outs),
        in_specs=[vmem] * len(args),
        out_specs=tuple(vmem for _ in outs),
        scratch_shapes=list(scratch),
        compiler_params=pltpu.CompilerParams(vmem_limit_bytes=vmem_mib * 1024 * 1024),
        cost_estimate=pl.CostEstimate(flops=flops, bytes_accessed=moved, transcendentals=0),
    )(*args)


def on_device(lon, lat, features, conv_first, conv_second, cotangent, edge_pick, edge_flip, corner_rule):
    side, c_in = features.shape[2], features.shape[4]
    half, c_out = cotangent.shape[2], cotangent.shape[4]
    slots, rings = 2 * lat, lon // 2
    width, padded = side * slots, (side + 2) * slots
    axes = ("lon", "lat")

    def spec(shape, dtype=BF):
        return jax.ShapeDtypeStruct(shape, dtype)

    def vmem(shape, dtype):
        return pltpu.VMEM(shape, dtype)

    def permuted(value, partner):
        pairs = []
        for place in range(lon):
            for band in range(lat):
                there = partner(place, band)
                pairs.append((place * lat + band, there[0] * lat + there[1]))
        return lax.ppermute(value, axes, pairs)

    def core_swap(value):
        return permuted(value, lambda place, band: (place, band ^ 1))

    def x_swap(value):
        return permuted(value, lambda place, band: (place, band ^ 2))

    ring_turns = rings.bit_length() - 1
    ring_pairs = rings == 1 << ring_turns
    ring_turns = ring_turns if ring_pairs else 1

    def ring_swap(value, turn):
        if not ring_pairs:
            total = 0.5 * lax.psum(value.astype(F32), "lon")
            return total - value.astype(F32)

        def partner(place, band):
            step = 1 << (turn if band % 2 == 0 else ring_turns - 1 - turn)
            return ((place % rings) ^ step) + place // rings * rings, band

        return permuted(value, partner)

    def summed(value, other):
        return (value.astype(F32) + other.astype(F32)).astype(BF)

    def beside(place, band):
        ring, upper = place % rings, place // rings
        east = (ring + band) % 2 == 0
        return ((ring + (1 if east else -1)) % rings + upper * rings, band)

    def exchange(value):
        near = permuted(value, beside)
        return near, core_swap(near)

    cells, quarter = side * side, half * half
    total = cells + 2 * quarter + 16
    cot = cotangent.reshape(quarter, c_out)

    def placed(value, row, lane=0):
        rows, lanes = value.shape
        return jnp.pad(value, ((row, total - row - rows), (lane, c_in - lane - lanes)))

    flags, at = 0, 0
    for values in (edge_pick[0], edge_flip[0], corner_rule[0]):
        flags = flags + placed(values, total - 16, at)
        at += values.shape[1]
    own = placed(features.reshape(cells, c_in), 0) + flags.astype(BF)
    own = own + placed(cot[:, :c_in], cells) + placed(cot[:, c_in:], cells + quarter)
    parts = [None] * slots
    parts[0] = own
    for index in [*range(lat, slots, 2), *range(2, lat, 2)]:
        parts[index] = permuted(
            own,
            lambda place, band, index=index: (
                (place + rings * (index // lat)) % lon,
                band ^ (index % lat),
            ),
        )
    for index in range(0, slots, 2):
        parts[index + 1] = core_swap(parts[index])

    first_weight = conv_first.reshape(3, 3 * c_in, c_out)
    second_weight = conv_second.reshape(3, 3 * c_out, c_out)

    features_ext, cot_ring, table, columns = run(
        functools.partial(collect_kernel, side, half, slots),
        [
            spec((side + 2, width, c_in)),
            spec((half * half * slots, c_out)),
            spec((slots, c_in), F32),
            spec((padded, c_in)),
        ],
        parts,
        [
            vmem((side * width, c_in), F32),
            vmem((half * half * slots, c_in), F32),
            vmem((half * half * slots, c_in), F32),
        ],
        flops=4_000_000_000,
    )
    near, far = exchange(columns)
    work = 2 * side * width * 9 * c_in * c_out
    features_pad, act_ext, slope, columns = run(
        functools.partial(first_kernel, side, slots),
        [
            spec((side + 2, padded, c_in)),
            spec((side + 2, width, c_out)),
            spec((side, width, c_out)),
            spec((padded, c_out)),
        ],
        [features_ext, near, far, table, first_weight],
        flops=work,
    )
    near, far = exchange(columns)
    back_scratch = [
        vmem((side, (side + 4) * slots, c_out), BF),
        vmem((side, padded, c_out), BF),
    ]
    act_pad, second_grad, pooled, act_grad, columns = run(
        functools.partial(second_kernel, side, slots),
        [
            spec((side + 2, padded, c_out)),
            spec((side, width, c_out)),
            spec((half * half, c_out)),
            spec((side + 2, width, c_out)),
            spec((padded, c_out)),
        ],
        [act_ext, near, far, table, cot_ring, second_weight, conv_second],
        back_scratch
        + [
            vmem((c_out // 128, half * half * slots, 128), F32),
            vmem((side + 2, slots, c_out), F32),
            vmem((side + 2, slots, c_out), F32),
        ],
        flops=4 * work,
    )
    near = permuted(columns, beside)
    part = c_out // 2
    second_sum = run(
        functools.partial(weight_kernel, side, slots),
        [spec((9, c_out // 2, part))],
        [act_pad, act_ext, second_grad],
        flops=work,
    )[0]
    near, second_sum = lax.optimization_barrier((near, second_sum))
    far = core_swap(near)
    second_other = ring_swap(second_sum, 0)
    pre_grad, first_sum = run(
        functools.partial(third_kernel, side, slots),
        [
            spec((side, width, c_out)),
            spec((9, c_in, part)),
        ],
        [act_grad, near, far, table, slope, features_pad, features_ext],
        [vmem((side, width, c_out), F32)],
        flops=work,
    )
    features_grad, columns = run(
        functools.partial(fourth_kernel, side, slots),
        [spec((side + 2, width, c_in)), spec((padded, c_in))],
        [pre_grad, table, conv_first],
        back_scratch + [vmem((side + 2, slots, c_in), F32), vmem((side + 2, slots, c_in), F32)],
        flops=work,
    )
    second_other, columns = lax.optimization_barrier((second_other, columns))
    first_other = ring_swap(first_sum, 0)
    near = permuted(columns, beside)
    for turn in range(1, ring_turns):
        second_sum = summed(second_sum, second_other)
        second_other = ring_swap(second_sum, turn)
        first_sum = summed(first_sum, first_other)
        first_other = ring_swap(first_sum, turn)
    far = core_swap(near)
    input_grad = run(
        functools.partial(last_kernel, side, slots),
        [spec((side * side, c_in))],
        [features_grad, near, far, table],
        [vmem((side, width, c_in), F32), vmem((side * width, c_in), F32)],
    )[0]
    second_sum = summed(second_sum, second_other)
    first_other, input_grad = lax.optimization_barrier((first_other, input_grad))
    first_sum = summed(first_sum, first_other)
    blocks = []
    for block in (first_sum, second_sum, x_swap(second_sum)):
        blocks += [block, core_swap(block)]
    target = math.sqrt(9.0 * (c_in + c_out) * c_out)
    scaled_first, scaled_second = run(
        functools.partial(scale_kernel, slots, target),
        [spec((9, c_in, c_out)), spec((9, c_out, c_out))],
        blocks,
    )
    return (
        pooled.reshape(1, 1, half, half, c_out),
        input_grad.reshape(1, 1, side, side, c_in),
        scaled_first.reshape(3, 3, c_in, c_out),
        scaled_second.reshape(3, 3, c_out, c_out),
    )


def solution(mesh):
    return jax.shard_map(
        functools.partial(on_device, mesh.shape["lon"], mesh.shape["lat"]),
        mesh=mesh,
        in_specs=(
            P("lon", "lat", None, None, None),
            P(),
            P(),
            P("lon", "lat", None, None, None),
            P("lon", "lat", None),
            P("lon", "lat", None),
            P("lon", "lat", None),
        ),
        out_specs=(P("lon", "lat", None, None, None), P("lon", "lat", None, None, None), P(), P()),
        check_vma=False,
    )
```

```python
import functools
import math

import jax
import jax.numpy as jnp
from jax import lax
from jax.experimental import pallas as pl
from jax.experimental.pallas import tpu as pltpu
from jax.sharding import PartitionSpec as P


BF = jnp.bfloat16
F32 = jnp.float32
ROWS_PER_STEP = 4


def normal_parts(z):
    cdf = 0.5 * (1.0 + lax.erf(z * (1.0 / math.sqrt(2.0))))
    pdf = jnp.exp(-0.5 * z * z) * (1.0 / math.sqrt(2.0 * math.pi))
    return cdf, pdf


class Ring:
    def __init__(self, slots, channels, table, info):
        self.slots, self.band = slots, slots // 2
        self.channels, self.info = channels, info
        place = lax.broadcasted_iota(jnp.int32, (slots, channels), 0)
        self.top = lax.rem(place, self.band) == self.band - 1
        self.bottom = lax.rem(place, self.band) == 0
        self.table = table

    def flag(self, column):
        return jnp.broadcast_to(self.table[:, column : column + 1], (self.slots, self.channels))

    def up(self, x):
        return pltpu.roll(x, self.slots - 1, 0)

    def down(self, x):
        return pltpu.roll(x, 1, 0)

    def across(self, x):
        return pltpu.roll(x, self.band, 0)

    def take(self, edges, side, to_source, to_slot):
        pick, flip = to_source(self.flag(side)), to_source(self.flag(2 + side))
        count = len(edges[0])
        chosen = [
            jnp.where(
                pick == 0.0,
                edges[0][j],
                jnp.where(
                    pick == 1.0, edges[1][j], jnp.where(pick == 2.0, edges[2][j], edges[3][j])
                ),
            )
            for j in range(count)
        ]
        return [
            to_slot(jnp.where(flip == 1.0, chosen[count - 1 - j], chosen[j])) for j in range(count)
        ]

    def halo_rows(self, edges):
        same = self.take(edges, 0, self.up, self.down)
        pole = self.take(edges, 0, self.across, self.across)
        south = [jnp.where(self.bottom, b, a) for a, b in zip(same, pole)]
        same = self.take(edges, 1, self.down, self.up)
        pole = self.take(edges, 1, self.across, self.across)
        north = [jnp.where(self.top, b, a) for a, b in zip(same, pole)]
        return south, north

    def give(self, totals, rows, side, to_source):
        pick, flip = to_source(self.flag(side)), to_source(self.flag(2 + side))
        count = len(rows)
        moved = [to_source(row) for row in rows]
        for j in range(count):
            value = jnp.where(flip == 1.0, moved[count - 1 - j], moved[j])
            for edge in range(4):
                share = jnp.where(pick == float(edge), value, 0.0)
                totals[edge][j] = share if totals[edge][j] is None else totals[edge][j] + share

    def halo_rows_back(self, south, north):
        totals = [[None] * len(south) for _ in range(4)]
        self.give(totals, [jnp.where(self.bottom, 0.0, x) for x in south], 0, self.up)
        self.give(totals, [jnp.where(self.bottom, x, 0.0) for x in south], 0, self.across)
        self.give(totals, [jnp.where(self.top, 0.0, x) for x in north], 1, self.down)
        self.give(totals, [jnp.where(self.top, x, 0.0) for x in north], 1, self.across)
        return totals

    def arrived(self, near_ref, far_ref):
        slots = self.slots
        near, far = near_ref[...].astype(F32), far_ref[...].astype(F32)
        to_east = self.info[3] == 1
        east, west = jnp.where(to_east, near, far), jnp.where(to_east, far, near)
        count = near.shape[0] // slots
        east = [east[i * slots : (i + 1) * slots] for i in range(count)]
        west = [west[i * slots : (i + 1) * slots] for i in range(count)]
        east = [jnp.where(self.info[1] == 1, self.across(x), x) for x in east]
        west = [jnp.where(self.info[2] == 1, self.across(x), x) for x in west]
        return east, west

    def packed(self, east_list, west_list, out_ref):
        east, west = jnp.concatenate(east_list, axis=0), jnp.concatenate(west_list, axis=0)
        out_ref[...] = jnp.where(self.info[3] == 1, east, west).astype(BF)


def place_of(slots):
    lat, rings = slots // 2, lax.axis_size("lon") // 2
    lon_at, lat_at = lax.axis_index("lon"), lax.axis_index("lat")
    ring_at, hemisphere = lax.rem(lon_at, rings), lax.div(lon_at, rings)
    core = lax.rem(lat_at, 2)
    return (
        hemisphere * lat + lat_at,
        (ring_at == rings - 1).astype(jnp.int32),
        (ring_at == 0).astype(jnp.int32),
        1 - lax.rem(ring_at + core, 2),
        core,
        lax.rem(lax.div(lat_at, 2), 2),
    )


def split_cells(row, slots):
    return [row[j * slots : (j + 1) * slots] for j in range(row.shape[0] // slots)]


def extend(ring, side, ext_ref):
    slots = ring.slots
    width = side * slots
    pair = 2 * slots
    first_col, last_col = [], []
    for i in range(side):
        first_col.append(ext_ref[1 + i, 0:pair].astype(F32)[:slots])
        last_col.append(ext_ref[1 + i, width - pair : width].astype(F32)[slots:])
    edges = [
        split_cells(ext_ref[1].astype(F32), slots),
        split_cells(ext_ref[side].astype(F32), slots),
        first_col,
        last_col,
    ]
    south, north = ring.halo_rows(edges)
    ext_ref[0] = jnp.concatenate(south, axis=0).astype(BF)
    ext_ref[side + 1] = jnp.concatenate(north, axis=0).astype(BF)
    return [south[-1]] + last_col + [north[-1]], [south[0]] + first_col + [north[0]]


def pad_columns(ring, side, ext_ref, near_ref, far_ref, pad_ref):
    slots = ring.slots
    width = side * slots
    east, west = ring.arrived(near_ref, far_ref)
    low, high = ext_ref[0].astype(F32), ext_ref[side + 1].astype(F32)
    blends = (
        (0, west, 0, 1, low[:slots]),
        (1, east, 0, 1, low[width - slots :]),
        (2, west, side + 1, side, high[:slots]),
        (3, east, side + 1, side, high[width - slots :]),
    )
    for corner, column, at, beside, along in blends:
        blended = (0.5 * (along + column[beside])).astype(BF).astype(F32)
        column[at] = jnp.where(ring.flag(4 + corner) == 1.0, blended, column[at])
    for i in range(side + 2):
        pad_ref[i] = jnp.concatenate([west[i], ext_ref[i].astype(F32), east[i]], axis=0).astype(BF)


def windows(pad_ref, ext_ref, start, rows, width, slots, channels):
    left = pad_ref[pl.ds(start, rows), 0:width, :]
    middle = ext_ref[pl.ds(start, rows), :, :]
    right = pad_ref[pl.ds(start, rows), 2 * slots : 2 * slots + width, :]
    return jnp.concatenate([left, middle, right], axis=-1).reshape(rows * width, 3 * channels)


def convolved(pad_ref, ext_ref, weight_ref, start, rows, width, slots, channels):
    total = None
    for dh in range(3):
        window = windows(pad_ref, ext_ref, start + dh, rows, width, slots, channels)
        part = jnp.dot(window, weight_ref[dh], preferred_element_type=F32)
        total = part if total is None else total + part
    return total


def clear_edges(wide_ref, side, slots):
    width = side * slots
    blank = jnp.zeros((side, 2 * slots, wide_ref.shape[2]), BF)
    wide_ref[:, 0 : 2 * slots] = blank
    wide_ref[:, width + 2 * slots :] = blank


def put_gradient(wide_ref, shifted_ref, row, value, slots):
    width = value.shape[0]
    wide_ref[row, 2 * slots : 2 * slots + width] = value.astype(BF)
    blank = jnp.zeros((slots, value.shape[1]), F32)
    shifted_ref[row] = jnp.concatenate([blank, value, blank], axis=0).astype(BF)


def convolved_back(
    ring, side, wide_ref, shifted_ref, weight_ref, out_ref, send_ref, west_ref, east_ref
):
    slots, channels = ring.slots, ring.channels
    width, padded = side * slots, (side + 2) * slots
    depth = wide_ref.shape[2]
    rows = ROWS_PER_STEP

    def finish(row, total):
        out_ref[row] = total[slots : slots + width].astype(BF)
        west_ref[row] = total[:slots].astype(BF).astype(F32)
        east_ref[row] = total[slots + width :].astype(BF).astype(F32)

    waiting = {}
    for start in range(0, side, rows):
        windows_back = (
            wide_ref[start : start + rows, 2 * slots : 2 * slots + padded, :],
            shifted_ref[start : start + rows, :, :],
            wide_ref[start : start + rows, 0:padded, :],
        )
        product = None
        for dw, window in enumerate(windows_back):
            part = lax.dot_general(
                window.reshape(rows * padded, depth),
                weight_ref[:, dw].reshape(3 * channels, depth),
                (((1,), (1,)), ((), ())),
                preferred_element_type=F32,
            )
            product = part if product is None else product + part
        for row in range(rows):
            for dh in range(3):
                part = product[
                    row * padded : (row + 1) * padded, dh * channels : (dh + 1) * channels
                ]
                at = start + row + dh
                waiting[at] = waiting[at] + part if at in waiting else part
        for at in sorted(waiting):
            if at < start + rows or start + rows == side:
                finish(at, waiting.pop(at))
    pair = 2 * slots
    for corner, column_ref, at, beside, is_east in (
        (0, west_ref, 0, 1, False),
        (1, east_ref, 0, 1, True),
        (2, west_ref, side + 1, side, False),
        (3, east_ref, side + 1, side, True),
    ):
        value = column_ref[at]
        blended = ring.flag(4 + corner) == 1.0
        half = jnp.where(blended, 0.5 * value, 0.0)
        column_ref[beside] = column_ref[beside] + half
        column_ref[at] = jnp.where(blended, 0.0, value)
        if is_east:
            old = out_ref[at, width - pair : width].astype(F32)
            new = jnp.concatenate([old[:slots], old[slots:] + half], axis=0)
            out_ref[at, width - pair : width] = new.astype(BF)
        else:
            old = out_ref[at, 0:pair].astype(F32)
            new = jnp.concatenate([old[:slots] + half, old[slots:]], axis=0)
            out_ref[at, 0:pair] = new.astype(BF)
    ring.packed(
        [east_ref[i] for i in range(side + 2)], [west_ref[i] for i in range(side + 2)], send_ref
    )


def halo_back(ring, side, ext_ref, near_ref, far_ref, field_ref):
    slots = ring.slots
    width = side * slots
    east, west = ring.arrived(near_ref, far_ref)
    for i in range(side):
        field_ref[i] = ext_ref[1 + i].astype(F32)
    south = split_cells(ext_ref[0].astype(F32), slots)
    north = split_cells(ext_ref[side + 1].astype(F32), slots)
    south[0], south[-1] = south[0] + west[0], south[-1] + east[0]
    north[0], north[-1] = north[0] + west[-1], north[-1] + east[-1]
    low, high, first, last = ring.halo_rows_back(south, north)
    field_ref[0] += jnp.concatenate(low, axis=0)
    field_ref[side - 1] += jnp.concatenate(high, axis=0)
    for i in range(side):
        field_ref[i, 0:slots] += first[i] + west[1 + i]
        field_ref[i, width - slots : width] += last[i] + east[1 + i]


def collect_kernel(side, half, slots, *refs):
    info = place_of(slots)
    parts, (ext_ref, cot_ref, table_ref, send_ref), scratch = (
        refs[:slots],
        refs[slots : slots + 4],
        refs[slots + 4 :],
    )
    cells, cot_cells = side * side, half * half
    channels = ext_ref.shape[2]
    field_ref, low_ref, high_ref = scratch
    for index, part in enumerate(parts):
        slot = info[0] ^ index
        field_ref[pl.ds(slot, cells, stride=slots), :] = part[0:cells].astype(F32)
        low_ref[pl.ds(slot, cot_cells, stride=slots), :] = part[
            cells : cells + cot_cells
        ].astype(F32)
        high_ref[pl.ds(slot, cot_cells, stride=slots), :] = part[
            cells + cot_cells : cells + 2 * cot_cells
        ].astype(F32)
        flags = part[cells + 2 * cot_cells : cells + 2 * cot_cells + 16].astype(F32)
        table_ref[pl.ds(slot, 1), :] = flags[0:1]
    width = side * slots
    for i in range(side):
        ext_ref[1 + i] = field_ref[i * width : (i + 1) * width].astype(BF)
    cot_ref[:, 0:channels] = low_ref[...].astype(BF)
    cot_ref[:, channels : 2 * channels] = high_ref[...].astype(BF)
    ring = Ring(slots, channels, table_ref[...], info)
    ring.packed(*extend(ring, side, ext_ref), send_ref)


def edge_kernel(
    side, slots, ext_in, near_ref, far_ref, table_ref, weight_ref,
    pad_ref, send_ref,
):
    info = place_of(slots)
    channels, width = ext_in.shape[2], side * slots
    ring = Ring(slots, channels, table_ref[...], info)
    pad_columns(ring, side, ext_in, near_ref, far_ref, pad_ref)
    left = pad_ref[:, 0 : 4 * slots].astype(F32)
    right = pad_ref[:, width - 2 * slots : width + 2 * slots].astype(F32)
    z = None
    for dh in range(3):
        taps = []
        for dw in range(3):
            at = dw * slots
            taps.append(
                jnp.concatenate(
                    [
                        left[dh : dh + side, at : at + slots],
                        right[dh : dh + side, at + slots : at + 2 * slots],
                    ],
                    axis=1,
                ).astype(BF)
            )
        window = jnp.concatenate(taps, axis=-1).reshape(side * 2 * slots, 3 * channels)
        part = jnp.dot(window, weight_ref[dh], preferred_element_type=F32)
        z = part if z is None else z + part
    cdf, _ = normal_parts(z)
    act = (z * cdf).astype(BF).astype(F32)
    cells = split_cells(act, slots)
    first, last = cells[0::2], cells[1::2]
    ring = Ring(slots, act.shape[1], table_ref[...], info)
    south, north = ring.halo_rows(
        [
            [first[0], last[0]],
            [first[-1], last[-1]],
            [first[0], first[-1]],
            [last[0], last[-1]],
        ]
    )
    ring.packed(
        [south[1]] + last + [north[1]], [south[0]] + first + [north[0]], send_ref
    )


def first_kernel(
    side, slots, ext_in, pad_ref, table_ref, weight_ref,
    ext_ref, slope_ref,
):
    channels, width = ext_in.shape[2], side * slots
    rows = ROWS_PER_STEP

    def step(index, carry):
        start = index * rows
        z = convolved(pad_ref, ext_in, weight_ref, start, rows, width, slots, channels)
        cdf, pdf = normal_parts(z)
        shape = (rows, width, z.shape[1])
        ext_ref[pl.ds(start + 1, rows)] = (z * cdf).astype(BF).reshape(shape)
        slope_ref[pl.ds(start, rows)] = (cdf + z * pdf).astype(BF).reshape(shape)
        return carry

    for index in range(side // rows):
        step(index, 0)
    extend(Ring(slots, ext_ref.shape[2], table_ref[...], None), side, ext_ref)


def second_kernel(
    side, slots, ext_in, near_ref, far_ref, table_ref, cot_ref, weight_ref, back_ref,
    pad_ref, grad_ref, pooled_ref, ext_ref, send_ref,
    wide_ref, shifted_ref, mean_ref, west_ref, east_ref,
):
    info = place_of(slots)
    channels, width = ext_in.shape[2], side * slots
    ring = Ring(slots, channels, table_ref[...], info)
    pad_columns(ring, side, ext_in, near_ref, far_ref, pad_ref)
    clear_edges(wide_ref, side, slots)
    rows = ROWS_PER_STEP
    half = side // 2
    step_cells = (rows // 2) * half * slots

    def step(index, carry):
        start = index * rows
        z = convolved(pad_ref, ext_in, weight_ref, start, rows, width, slots, channels)
        cdf, pdf = normal_parts(z)
        paired = (rows // 2, 2, half, 2, slots, channels)
        value = (z * cdf).reshape(paired)
        cells = pl.ds(index * step_cells, step_cells)
        mean = (value[:, 0, :, 0] + value[:, 0, :, 1]) + (value[:, 1, :, 0] + value[:, 1, :, 1])
        mean = mean.reshape(step_cells, channels) * 0.25
        for block in range(channels // 128):
            mean_ref[block, cells, :] = mean[:, block * 128 : (block + 1) * 128]
        cot = cot_ref[cells, :].astype(F32) * 0.25
        cot = cot.reshape(rows // 2, 1, half, 1, slots, channels)
        slope = (cdf + z * pdf).reshape(paired)
        grad = (jnp.broadcast_to(cot, paired) * slope).reshape(rows, width, channels)
        grad_ref[pl.ds(start, rows)] = grad.astype(BF)
        for row in range(rows):
            put_gradient(wide_ref, shifted_ref, start + row, grad[row], slots)
        return carry

    for index in range(side // rows):
        step(index, 0)
    for block in range(channels // 128):
        pooled_ref[:, block * 128 : (block + 1) * 128] = mean_ref[
            block, pl.ds(info[0], half * half, stride=slots), :
        ].astype(BF)
    convolved_back(
        ring, side, wide_ref, shifted_ref, back_ref, ext_ref, send_ref, west_ref, east_ref
    )


def third_kernel(
    side, slots, ext_in, near_ref, far_ref, table_ref, slope_ref, pad_ref, features_ref,
    grad_ref, out_ref,
    field_ref,
):
    info = place_of(slots)
    ring = Ring(slots, ext_in.shape[2], table_ref[...], info)
    halo_back(ring, side, ext_in, near_ref, far_ref, field_ref)
    for i in range(side):
        grad_ref[i] = (field_ref[i] * slope_ref[i].astype(F32)).astype(BF)
    columns = out_ref.shape[2]
    start = pl.multiple_of(info[4] * columns, columns)
    grad = grad_ref[:, :, pl.ds(start, columns)].reshape(side * side * slots, columns)

    weight_products(side, slots, pad_ref, features_ref, grad, 0, out_ref)


def fourth_kernel(
    side, slots, grad_ref, table_ref, back_ref,
    ext_ref, send_ref,
    wide_ref, shifted_ref, west_ref, east_ref,
):
    info = place_of(slots)
    clear_edges(wide_ref, side, slots)
    for i in range(side):
        put_gradient(wide_ref, shifted_ref, i, grad_ref[i].astype(F32), slots)
    ring = Ring(slots, ext_ref.shape[2], table_ref[...], info)
    convolved_back(
        ring, side, wide_ref, shifted_ref, back_ref, ext_ref, send_ref, west_ref, east_ref
    )


def last_kernel(
    side, slots, ext_in, near_ref, far_ref, table_ref, out_ref, field_ref, flat_ref
):
    info = place_of(slots)
    width = side * slots
    ring = Ring(slots, ext_in.shape[2], table_ref[...], info)
    halo_back(ring, side, ext_in, near_ref, far_ref, field_ref)
    for i in range(side):
        flat_ref[i * width : (i + 1) * width] = field_ref[i]
    out_ref[...] = flat_ref[pl.ds(info[0], side * side, stride=slots), :].astype(BF)


def weight_products(side, slots, pad_ref, ext_ref, grad, first, out_ref):
    width, channels = side * slots, out_ref.shape[1]
    lanes = pl.ds(first, channels)

    def step(dh, carry):
        rows = pl.ds(dh, side)
        window = jnp.concatenate(
            [
                pad_ref[rows, 0:width, lanes],
                ext_ref[rows, :, lanes],
                pad_ref[rows, 2 * slots : 2 * slots + width, lanes],
            ],
            axis=-1,
        ).reshape(side * width, 3 * channels)
        product = lax.dot_general(
            window, grad, (((0,), (0,)), ((), ())), preferred_element_type=F32
        ).astype(BF)
        for dw in range(3):
            out_ref[dh * 3 + dw] = product[dw * channels : (dw + 1) * channels]
        return carry

    lax.fori_loop(0, 3, step, 0)


def weight_kernel(side, slots, pad_ref, ext_ref, grad_ref, out_ref):
    info = place_of(slots)
    rows, columns = out_ref.shape[1:]
    start = pl.multiple_of(info[4] * columns, columns)
    grad = grad_ref[:, :, pl.ds(start, columns)].reshape(side * side * slots, columns)
    first = pl.multiple_of(info[5] * rows, rows)
    weight_products(side, slots, pad_ref, ext_ref, grad, first, out_ref)


def scale_kernel(slots, target, *refs):
    info = place_of(slots)
    blocks, (first_out, second_out, first_ref, second_ref, sems) = refs[:-5], refs[-5:]
    squared = jnp.zeros((1, 1), F32)
    for ref in blocks:
        value = ref[...].astype(F32)
        lanes = jnp.sum(jnp.sum(value * value, axis=0), axis=0, keepdims=True)
        squared = squared + jnp.sum(lanes, axis=1, keepdims=True)
    scale = target / jnp.sqrt(squared + 1e-06)

    def put(pair, to):
        for index, ref in enumerate(pair):
            core = info[4] if index == 0 else 1 - info[4]
            columns = ref.shape[2]
            lanes = pl.ds(pl.multiple_of(core * columns, columns), columns)
            to[:, :, lanes] = (ref[...].astype(F32) * scale).astype(BF)

    rows = blocks[2].shape[1]
    copies = []
    for index in range(3):
        if index == 0:
            source, to = first_ref, first_out
        else:
            half = info[5] if index == 1 else 1 - info[5]
            at = pl.ds(pl.multiple_of(half * rows, rows), rows)
            source, to = second_ref.at[index - 1], second_out.at[:, at, :]
        put(blocks[2 * index : 2 * index + 2], source)
        copies.append(pltpu.make_async_copy(source, to, sems.at[index]))
        copies[-1].start()
    for copy in copies:
        copy.wait()


def run(kernel, outs, args, scratch=(), flops=0, vmem_mib=8, to=pltpu.VMEM):
    vmem = pl.BlockSpec(memory_space=pltpu.VMEM)
    moved = sum(math.prod(x.shape) * x.dtype.itemsize for x in list(args) + list(outs))
    return pl.pallas_call(
        kernel,
        out_shape=tuple(outs),
        in_specs=[vmem] * len(args),
        out_specs=tuple(pl.BlockSpec(memory_space=to) for _ in outs),
        scratch_shapes=list(scratch),
        compiler_params=pltpu.CompilerParams(vmem_limit_bytes=vmem_mib * 1024 * 1024),
        cost_estimate=pl.CostEstimate(flops=flops, bytes_accessed=moved, transcendentals=0),
    )(*args)


def on_device(lon, lat, features, conv_first, conv_second, cotangent, edge_pick, edge_flip, corner_rule):
    side, c_in = features.shape[2], features.shape[4]
    half, c_out = cotangent.shape[2], cotangent.shape[4]
    slots, rings = 2 * lat, lon // 2
    width, padded = side * slots, (side + 2) * slots
    axes = ("lon", "lat")

    def spec(shape, dtype=BF):
        return jax.ShapeDtypeStruct(shape, dtype)

    def vmem(shape, dtype):
        return pltpu.VMEM(shape, dtype)

    def permuted(value, partner):
        pairs = []
        for place in range(lon):
            for band in range(lat):
                there = partner(place, band)
                pairs.append((place * lat + band, there[0] * lat + there[1]))
        return lax.ppermute(value, axes, pairs)

    def core_swap(value):
        return permuted(value, lambda place, band: (place, band ^ 1))

    def x_swap(value):
        return permuted(value, lambda place, band: (place, band ^ 2))

    ring_turns = rings.bit_length() - 1
    ring_pairs = rings == 1 << ring_turns
    ring_turns = ring_turns if ring_pairs else 1

    def ring_swap(value, turn):
        if not ring_pairs:
            total = 0.5 * lax.psum(value.astype(F32), "lon")
            return total - value.astype(F32)

        def partner(place, band):
            step = 1 << (turn if band % 2 == 0 else ring_turns - 1 - turn)
            return ((place % rings) ^ step) + place // rings * rings, band

        return permuted(value, partner)

    def summed(value, other):
        return (value.astype(F32) + other.astype(F32)).astype(BF)

    def beside(place, band):
        ring, upper = place % rings, place // rings
        east = (ring + band) % 2 == 0
        return ((ring + (1 if east else -1)) % rings + upper * rings, band)

    def exchange(value):
        near = permuted(value, beside)
        return near, core_swap(near)

    cells, quarter = side * side, half * half
    total = cells + 2 * quarter + 16
    cot = cotangent.reshape(quarter, c_out)

    def placed(value, row, lane=0):
        rows, lanes = value.shape
        return jnp.pad(value, ((row, total - row - rows), (lane, c_in - lane - lanes)))

    flags, at = 0, 0
    for values in (edge_pick[0], edge_flip[0], corner_rule[0]):
        flags = flags + placed(values, total - 16, at)
        at += values.shape[1]
    own = placed(features.reshape(cells, c_in), 0) + flags.astype(BF)
    own = own + placed(cot[:, :c_in], cells) + placed(cot[:, c_in:], cells + quarter)
    parts = [None] * slots
    parts[0] = own
    for index in [*range(lat, slots, 2), *range(2, lat, 2)]:
        parts[index] = permuted(
            own,
            lambda place, band, index=index: (
                (place + rings * (index // lat)) % lon,
                band ^ (index % lat),
            ),
        )
    for index in range(0, slots, 2):
        parts[index + 1] = core_swap(parts[index])

    first_weight = conv_first.reshape(3, 3 * c_in, c_out)
    second_weight = conv_second.reshape(3, 3 * c_out, c_out)

    features_ext, cot_ring, table, columns = run(
        functools.partial(collect_kernel, side, half, slots),
        [
            spec((side + 2, width, c_in)),
            spec((half * half * slots, c_out)),
            spec((slots, c_in), F32),
            spec((padded, c_in)),
        ],
        parts,
        [
            vmem((side * width, c_in), F32),
            vmem((half * half * slots, c_in), F32),
            vmem((half * half * slots, c_in), F32),
        ],
        flops=4_000_000_000,
    )
    near, far = exchange(columns)
    work = 2 * side * width * 9 * c_in * c_out
    features_pad, columns = run(
        functools.partial(edge_kernel, side, slots),
        [spec((side + 2, padded, c_in)), spec((padded, c_out))],
        [features_ext, near, far, table, first_weight],
        flops=work // 8,
    )
    near = permuted(columns, beside)
    act_ext, slope = run(
        functools.partial(first_kernel, side, slots),
        [spec((side + 2, width, c_out)), spec((side, width, c_out))],
        [features_ext, features_pad, table, first_weight],
        flops=work,
    )
    near, act_ext = lax.optimization_barrier((near, act_ext))
    far = core_swap(near)
    back_scratch = [
        vmem((side, (side + 4) * slots, c_out), BF),
        vmem((side, padded, c_out), BF),
    ]
    act_pad, second_grad, pooled, act_grad, columns = run(
        functools.partial(second_kernel, side, slots),
        [
            spec((side + 2, padded, c_out)),
            spec((side, width, c_out)),
            spec((half * half, c_out)),
            spec((side + 2, width, c_out)),
            spec((padded, c_out)),
        ],
        [act_ext, near, far, table, cot_ring, second_weight, conv_second],
        back_scratch
        + [
            vmem((c_out // 128, half * half * slots, 128), F32),
            vmem((side + 2, slots, c_out), F32),
            vmem((side + 2, slots, c_out), F32),
        ],
        flops=4 * work,
    )
    near = permuted(columns, beside)
    part = c_out // 2
    second_sum = run(
        functools.partial(weight_kernel, side, slots),
        [spec((9, c_out // 2, part))],
        [act_pad, act_ext, second_grad],
        flops=work,
    )[0]
    near, second_sum = lax.optimization_barrier((near, second_sum))
    far = core_swap(near)
    second_other = ring_swap(second_sum, 0)
    pre_grad, first_sum = run(
        functools.partial(third_kernel, side, slots),
        [
            spec((side, width, c_out)),
            spec((9, c_in, part)),
        ],
        [act_grad, near, far, table, slope, features_pad, features_ext],
        [vmem((side, width, c_out), F32)],
        flops=work,
    )
    features_grad, columns = run(
        functools.partial(fourth_kernel, side, slots),
        [spec((side + 2, width, c_in)), spec((padded, c_in))],
        [pre_grad, table, conv_first],
        back_scratch + [vmem((side + 2, slots, c_in), F32), vmem((side + 2, slots, c_in), F32)],
        flops=work,
    )
    second_other, columns = lax.optimization_barrier((second_other, columns))
    first_other = ring_swap(first_sum, 0)
    near = permuted(columns, beside)
    for turn in range(1, ring_turns):
        second_sum = summed(second_sum, second_other)
        second_other = ring_swap(second_sum, turn)
        first_sum = summed(first_sum, first_other)
        first_other = ring_swap(first_sum, turn)
    far = core_swap(near)
    input_grad = run(
        functools.partial(last_kernel, side, slots),
        [spec((side * side, c_in))],
        [features_grad, near, far, table],
        [vmem((side, width, c_in), F32), vmem((side * width, c_in), F32)],
    )[0]
    second_sum = summed(second_sum, second_other)
    first_other, input_grad = lax.optimization_barrier((first_other, input_grad))
    first_sum = summed(first_sum, first_other)
    blocks = []
    for block in (first_sum, second_sum, x_swap(second_sum)):
        blocks += [block, core_swap(block)]
    target = math.sqrt(9.0 * (c_in + c_out) * c_out)
    scaled_first, scaled_second = run(
        functools.partial(scale_kernel, slots, target),
        [spec((9, c_in, c_out)), spec((9, c_out, c_out))],
        blocks,
        [
            vmem((9, c_in, c_out), BF),
            vmem((2, 9, c_out // 2, c_out), BF),
            pltpu.SemaphoreType.DMA((3,)),
        ],
        to=pl.ANY,
    )
    return (
        pooled.reshape(1, 1, half, half, c_out),
        input_grad.reshape(1, 1, side, side, c_in),
        scaled_first.reshape(3, 3, c_in, c_out),
        scaled_second.reshape(3, 3, c_out, c_out),
    )


def solution(mesh):
    return jax.shard_map(
        functools.partial(on_device, mesh.shape["lon"], mesh.shape["lat"]),
        mesh=mesh,
        in_specs=(
            P("lon", "lat", None, None, None),
            P(),
            P(),
            P("lon", "lat", None, None, None),
            P("lon", "lat", None),
            P("lon", "lat", None),
            P("lon", "lat", None),
        ),
        out_specs=(P("lon", "lat", None, None, None), P("lon", "lat", None, None, None), P(), P()),
        check_vma=False,
    )
```

```python
import functools
import math

import jax
import jax.numpy as jnp
from jax import lax
from jax.experimental import pallas as pl
from jax.experimental.pallas import tpu as pltpu
from jax.sharding import PartitionSpec as P


BF = jnp.bfloat16
F32 = jnp.float32
ROWS_PER_STEP = 4


def normal_parts(z):
    cdf = 0.5 * (1.0 + lax.erf(z * (1.0 / math.sqrt(2.0))))
    pdf = jnp.exp(-0.5 * z * z) * (1.0 / math.sqrt(2.0 * math.pi))
    return cdf, pdf


class Ring:
    def __init__(self, slots, channels, table, info):
        self.slots, self.band = slots, slots // 2
        self.channels, self.info = channels, info
        place = lax.broadcasted_iota(jnp.int32, (slots, channels), 0)
        self.top = lax.rem(place, self.band) == self.band - 1
        self.bottom = lax.rem(place, self.band) == 0
        self.table = table

    def flag(self, column):
        return jnp.broadcast_to(self.table[:, column : column + 1], (self.slots, self.channels))

    def up(self, x):
        return pltpu.roll(x, self.slots - 1, 0)

    def down(self, x):
        return pltpu.roll(x, 1, 0)

    def across(self, x):
        return pltpu.roll(x, self.band, 0)

    def take(self, edges, side, to_source, to_slot):
        pick, flip = to_source(self.flag(side)), to_source(self.flag(2 + side))
        count = len(edges[0])
        chosen = [
            jnp.where(
                pick == 0.0,
                edges[0][j],
                jnp.where(
                    pick == 1.0, edges[1][j], jnp.where(pick == 2.0, edges[2][j], edges[3][j])
                ),
            )
            for j in range(count)
        ]
        return [
            to_slot(jnp.where(flip == 1.0, chosen[count - 1 - j], chosen[j])) for j in range(count)
        ]

    def halo_rows(self, edges):
        same = self.take(edges, 0, self.up, self.down)
        pole = self.take(edges, 0, self.across, self.across)
        south = [jnp.where(self.bottom, b, a) for a, b in zip(same, pole)]
        same = self.take(edges, 1, self.down, self.up)
        pole = self.take(edges, 1, self.across, self.across)
        north = [jnp.where(self.top, b, a) for a, b in zip(same, pole)]
        return south, north

    def give(self, totals, rows, side, to_source):
        pick, flip = to_source(self.flag(side)), to_source(self.flag(2 + side))
        count = len(rows)
        moved = [to_source(row) for row in rows]
        for j in range(count):
            value = jnp.where(flip == 1.0, moved[count - 1 - j], moved[j])
            for edge in range(4):
                share = jnp.where(pick == float(edge), value, 0.0)
                totals[edge][j] = share if totals[edge][j] is None else totals[edge][j] + share

    def halo_rows_back(self, south, north):
        totals = [[None] * len(south) for _ in range(4)]
        self.give(totals, [jnp.where(self.bottom, 0.0, x) for x in south], 0, self.up)
        self.give(totals, [jnp.where(self.bottom, x, 0.0) for x in south], 0, self.across)
        self.give(totals, [jnp.where(self.top, 0.0, x) for x in north], 1, self.down)
        self.give(totals, [jnp.where(self.top, x, 0.0) for x in north], 1, self.across)
        return totals

    def arrived(self, near_ref, far_ref):
        slots = self.slots
        near, far = near_ref[...].astype(F32), far_ref[...].astype(F32)
        to_east = self.info[3] == 1
        east, west = jnp.where(to_east, near, far), jnp.where(to_east, far, near)
        count = near.shape[0] // slots
        east = [east[i * slots : (i + 1) * slots] for i in range(count)]
        west = [west[i * slots : (i + 1) * slots] for i in range(count)]
        east = [jnp.where(self.info[1] == 1, self.across(x), x) for x in east]
        west = [jnp.where(self.info[2] == 1, self.across(x), x) for x in west]
        return east, west

    def packed(self, east_list, west_list, out_ref):
        east, west = jnp.concatenate(east_list, axis=0), jnp.concatenate(west_list, axis=0)
        out_ref[...] = jnp.where(self.info[3] == 1, east, west).astype(BF)


def place_of(slots):
    lat, rings = slots // 2, lax.axis_size("lon") // 2
    lon_at, lat_at = lax.axis_index("lon"), lax.axis_index("lat")
    ring_at, hemisphere = lax.rem(lon_at, rings), lax.div(lon_at, rings)
    core = lax.rem(lat_at, 2)
    return (
        hemisphere * lat + lat_at,
        (ring_at == rings - 1).astype(jnp.int32),
        (ring_at == 0).astype(jnp.int32),
        1 - lax.rem(ring_at + core, 2),
        core,
        lax.rem(lax.div(lat_at, 2), 2),
    )


def split_cells(row, slots):
    return [row[j * slots : (j + 1) * slots] for j in range(row.shape[0] // slots)]


def extend(ring, side, ext_ref):
    slots = ring.slots
    width = side * slots
    pair = 2 * slots
    first_col, last_col = [], []
    for i in range(side):
        first_col.append(ext_ref[1 + i, 0:pair].astype(F32)[:slots])
        last_col.append(ext_ref[1 + i, width - pair : width].astype(F32)[slots:])
    edges = [
        split_cells(ext_ref[1].astype(F32), slots),
        split_cells(ext_ref[side].astype(F32), slots),
        first_col,
        last_col,
    ]
    south, north = ring.halo_rows(edges)
    ext_ref[0] = jnp.concatenate(south, axis=0).astype(BF)
    ext_ref[side + 1] = jnp.concatenate(north, axis=0).astype(BF)
    return [south[-1]] + last_col + [north[-1]], [south[0]] + first_col + [north[0]]


def pad_columns(ring, side, ext_ref, near_ref, far_ref, pad_ref):
    slots = ring.slots
    width = side * slots
    east, west = ring.arrived(near_ref, far_ref)
    low, high = ext_ref[0].astype(F32), ext_ref[side + 1].astype(F32)
    blends = (
        (0, west, 0, 1, low[:slots]),
        (1, east, 0, 1, low[width - slots :]),
        (2, west, side + 1, side, high[:slots]),
        (3, east, side + 1, side, high[width - slots :]),
    )
    for corner, column, at, beside, along in blends:
        blended = (0.5 * (along + column[beside])).astype(BF).astype(F32)
        column[at] = jnp.where(ring.flag(4 + corner) == 1.0, blended, column[at])
    for i in range(side + 2):
        pad_ref[i] = jnp.concatenate([west[i], ext_ref[i].astype(F32), east[i]], axis=0).astype(BF)


def windows(pad_ref, ext_ref, start, rows, width, slots, channels):
    left = pad_ref[pl.ds(start, rows), 0:width, :]
    middle = ext_ref[pl.ds(start, rows), :, :]
    right = pad_ref[pl.ds(start, rows), 2 * slots : 2 * slots + width, :]
    return jnp.concatenate([left, middle, right], axis=-1).reshape(rows * width, 3 * channels)


def convolved(pad_ref, ext_ref, weight_ref, start, rows, width, slots, channels):
    total = None
    for dh in range(3):
        window = windows(pad_ref, ext_ref, start + dh, rows, width, slots, channels)
        part = jnp.dot(window, weight_ref[dh], preferred_element_type=F32)
        total = part if total is None else total + part
    return total


def clear_edges(wide_ref, side, slots):
    width = side * slots
    blank = jnp.zeros((side, 2 * slots, wide_ref.shape[2]), BF)
    wide_ref[:, 0 : 2 * slots] = blank
    wide_ref[:, width + 2 * slots :] = blank


def put_gradient(wide_ref, shifted_ref, row, value, slots):
    width = value.shape[0]
    wide_ref[row, 2 * slots : 2 * slots + width] = value.astype(BF)
    blank = jnp.zeros((slots, value.shape[1]), F32)
    shifted_ref[row] = jnp.concatenate([blank, value, blank], axis=0).astype(BF)


def convolved_back(
    ring, side, wide_ref, shifted_ref, weight_ref, out_ref, send_ref, west_ref, east_ref
):
    slots, channels = ring.slots, ring.channels
    width, padded = side * slots, (side + 2) * slots
    depth = wide_ref.shape[2]
    rows = ROWS_PER_STEP

    def finish(row, total):
        out_ref[row] = total[slots : slots + width].astype(BF)
        west_ref[row] = total[:slots].astype(BF).astype(F32)
        east_ref[row] = total[slots + width :].astype(BF).astype(F32)

    waiting = {}
    for start in range(0, side, rows):
        windows_back = (
            wide_ref[start : start + rows, 2 * slots : 2 * slots + padded, :],
            shifted_ref[start : start + rows, :, :],
            wide_ref[start : start + rows, 0:padded, :],
        )
        product = None
        for dw, window in enumerate(windows_back):
            part = lax.dot_general(
                window.reshape(rows * padded, depth),
                weight_ref[:, dw].reshape(3 * channels, depth),
                (((1,), (1,)), ((), ())),
                preferred_element_type=F32,
            )
            product = part if product is None else product + part
        for row in range(rows):
            for dh in range(3):
                part = product[
                    row * padded : (row + 1) * padded, dh * channels : (dh + 1) * channels
                ]
                at = start + row + dh
                waiting[at] = waiting[at] + part if at in waiting else part
        for at in sorted(waiting):
            if at < start + rows or start + rows == side:
                finish(at, waiting.pop(at))
    pair = 2 * slots
    for corner, column_ref, at, beside, is_east in (
        (0, west_ref, 0, 1, False),
        (1, east_ref, 0, 1, True),
        (2, west_ref, side + 1, side, False),
        (3, east_ref, side + 1, side, True),
    ):
        value = column_ref[at]
        blended = ring.flag(4 + corner) == 1.0
        half = jnp.where(blended, 0.5 * value, 0.0)
        column_ref[beside] = column_ref[beside] + half
        column_ref[at] = jnp.where(blended, 0.0, value)
        if is_east:
            old = out_ref[at, width - pair : width].astype(F32)
            new = jnp.concatenate([old[:slots], old[slots:] + half], axis=0)
            out_ref[at, width - pair : width] = new.astype(BF)
        else:
            old = out_ref[at, 0:pair].astype(F32)
            new = jnp.concatenate([old[:slots] + half, old[slots:]], axis=0)
            out_ref[at, 0:pair] = new.astype(BF)
    if send_ref is not None:
        ring.packed(
            [east_ref[i] for i in range(side + 2)], [west_ref[i] for i in range(side + 2)], send_ref
        )


def halo_back(ring, side, ext_ref, near_ref, far_ref, field_ref):
    slots = ring.slots
    width = side * slots
    east, west = ring.arrived(near_ref, far_ref)
    for i in range(side):
        field_ref[i] = ext_ref[1 + i].astype(F32)
    south = split_cells(ext_ref[0].astype(F32), slots)
    north = split_cells(ext_ref[side + 1].astype(F32), slots)
    south[0], south[-1] = south[0] + west[0], south[-1] + east[0]
    north[0], north[-1] = north[0] + west[-1], north[-1] + east[-1]
    low, high, first, last = ring.halo_rows_back(south, north)
    field_ref[0] += jnp.concatenate(low, axis=0)
    field_ref[side - 1] += jnp.concatenate(high, axis=0)
    for i in range(side):
        field_ref[i, 0:slots] += first[i] + west[1 + i]
        field_ref[i, width - slots : width] += last[i] + east[1 + i]


def collect_kernel(side, half, slots, *refs):
    info = place_of(slots)
    parts, (ext_ref, cot_ref, table_ref, send_ref), scratch = (
        refs[:slots],
        refs[slots : slots + 4],
        refs[slots + 4 :],
    )
    cells, cot_cells = side * side, half * half
    channels = ext_ref.shape[2]
    field_ref, low_ref, high_ref = scratch
    for index, part in enumerate(parts):
        slot = info[0] ^ index
        field_ref[pl.ds(slot, cells, stride=slots), :] = part[0:cells].astype(F32)
        low_ref[pl.ds(slot, cot_cells, stride=slots), :] = part[
            cells : cells + cot_cells
        ].astype(F32)
        high_ref[pl.ds(slot, cot_cells, stride=slots), :] = part[
            cells + cot_cells : cells + 2 * cot_cells
        ].astype(F32)
        flags = part[cells + 2 * cot_cells : cells + 2 * cot_cells + 16].astype(F32)
        table_ref[pl.ds(slot, 1), :] = flags[0:1]
    width = side * slots
    for i in range(side):
        ext_ref[1 + i] = field_ref[i * width : (i + 1) * width].astype(BF)
    cot_ref[:, 0:channels] = low_ref[...].astype(BF)
    cot_ref[:, channels : 2 * channels] = high_ref[...].astype(BF)
    ring = Ring(slots, channels, table_ref[...], info)
    ring.packed(*extend(ring, side, ext_ref), send_ref)


def edge_convolved(side, slots, pad_ref, weight_ref):
    channels, width = pad_ref.shape[2], side * slots
    left = pad_ref[:, 0 : 4 * slots].astype(F32)
    right = pad_ref[:, width - 2 * slots : width + 2 * slots].astype(F32)
    total = None
    for dh in range(3):
        taps = []
        for dw in range(3):
            at = dw * slots
            taps.append(
                jnp.concatenate(
                    [
                        left[dh : dh + side, at : at + slots],
                        right[dh : dh + side, at + slots : at + 2 * slots],
                    ],
                    axis=1,
                ).astype(BF)
            )
        window = jnp.concatenate(taps, axis=-1).reshape(side * 2 * slots, 3 * channels)
        part = jnp.dot(window, weight_ref[dh], preferred_element_type=F32)
        total = part if total is None else total + part
    return total


def edge_kernel(
    side, slots, ext_in, near_ref, far_ref, table_ref, weight_ref,
    pad_ref, send_ref,
):
    info = place_of(slots)
    ring = Ring(slots, ext_in.shape[2], table_ref[...], info)
    pad_columns(ring, side, ext_in, near_ref, far_ref, pad_ref)
    z = edge_convolved(side, slots, pad_ref, weight_ref)
    cdf, _ = normal_parts(z)
    act = (z * cdf).astype(BF).astype(F32)
    cells = split_cells(act, slots)
    first, last = cells[0::2], cells[1::2]
    ring = Ring(slots, act.shape[1], table_ref[...], info)
    south, north = ring.halo_rows(
        [
            [first[0], last[0]],
            [first[-1], last[-1]],
            [first[0], first[-1]],
            [last[0], last[-1]],
        ]
    )
    ring.packed([south[1]] + last + [north[1]], [south[0]] + first + [north[0]], send_ref)


def edge_back_kernel(
    side, slots, ext_in, near_ref, far_ref, table_ref, cot_ref, weight_ref, back_ref,
    pad_ref, send_ref,
):
    info = place_of(slots)
    channels, half = ext_in.shape[2], side // 2
    ring = Ring(slots, channels, table_ref[...], info)
    pad_columns(ring, side, ext_in, near_ref, far_ref, pad_ref)
    z = edge_convolved(side, slots, pad_ref, weight_ref)
    cdf, pdf = normal_parts(z)
    slope = split_cells(cdf + z * pdf, slots)
    line = half * slots
    columns = []
    for which in range(2):
        grads = []
        for row in range(half):
            if which == 0:
                cot = cot_ref[row * line : row * line + 2 * slots].astype(F32)[:slots]
            else:
                cot = cot_ref[(row + 1) * line - 2 * slots : (row + 1) * line].astype(F32)[slots:]
            for i in (2 * row, 2 * row + 1):
                grads.append(cot * 0.25 * slope[2 * i + which])
        product = lax.dot_general(
            jnp.concatenate(grads, axis=0).astype(BF),
            back_ref[:, 2 * which].reshape(3 * channels, channels),
            (((1,), (1,)), ((), ())),
            preferred_element_type=F32,
        )
        column = []
        for at in range(side + 2):
            total = None
            for dh in range(3):
                row = at - dh
                if 0 <= row < side:
                    part = product[
                        row * slots : (row + 1) * slots, dh * channels : (dh + 1) * channels
                    ]
                    total = part if total is None else total + part
            column.append(total.astype(BF).astype(F32))
        for corner, at, beside in ((which, 0, 1), (2 + which, side + 1, side)):
            blended = ring.flag(4 + corner) == 1.0
            value = column[at]
            column[beside] = column[beside] + jnp.where(blended, 0.5 * value, 0.0)
            column[at] = jnp.where(blended, 0.0, value)
        columns.append(column)
    ring.packed(columns[1], columns[0], send_ref)


def first_kernel(
    side, slots, ext_in, pad_ref, table_ref, weight_ref,
    ext_ref, slope_ref,
):
    channels, width = ext_in.shape[2], side * slots
    rows = ROWS_PER_STEP

    def step(index, carry):
        start = index * rows
        z = convolved(pad_ref, ext_in, weight_ref, start, rows, width, slots, channels)
        cdf, pdf = normal_parts(z)
        shape = (rows, width, z.shape[1])
        ext_ref[pl.ds(start + 1, rows)] = (z * cdf).astype(BF).reshape(shape)
        slope_ref[pl.ds(start, rows)] = (cdf + z * pdf).astype(BF).reshape(shape)
        return carry

    for index in range(side // rows):
        step(index, 0)
    extend(Ring(slots, ext_ref.shape[2], table_ref[...], None), side, ext_ref)


def second_kernel(
    side, slots, ext_in, pad_ref, cot_ref, weight_ref,
    grad_ref, pooled_ref,
    mean_ref,
):
    info = place_of(slots)
    channels, width = ext_in.shape[2], side * slots
    rows = ROWS_PER_STEP
    half = side // 2
    step_cells = (rows // 2) * half * slots

    def step(index, carry):
        start = index * rows
        z = convolved(pad_ref, ext_in, weight_ref, start, rows, width, slots, channels)
        cdf, pdf = normal_parts(z)
        paired = (rows // 2, 2, half, 2, slots, channels)
        value = (z * cdf).reshape(paired)
        cells = pl.ds(index * step_cells, step_cells)
        mean = (value[:, 0, :, 0] + value[:, 0, :, 1]) + (value[:, 1, :, 0] + value[:, 1, :, 1])
        mean = mean.reshape(step_cells, channels) * 0.25
        for block in range(channels // 128):
            mean_ref[block, cells, :] = mean[:, block * 128 : (block + 1) * 128]
        cot = cot_ref[cells, :].astype(F32) * 0.25
        cot = cot.reshape(rows // 2, 1, half, 1, slots, channels)
        slope = (cdf + z * pdf).reshape(paired)
        grad = (jnp.broadcast_to(cot, paired) * slope).reshape(rows, width, channels)
        grad_ref[pl.ds(start, rows)] = grad.astype(BF)
        return carry

    for index in range(side // rows):
        step(index, 0)
    for block in range(channels // 128):
        pooled_ref[:, block * 128 : (block + 1) * 128] = mean_ref[
            block, pl.ds(info[0], half * half, stride=slots), :
        ].astype(BF)


def third_kernel(
    side, slots, ext_in, near_ref, far_ref, table_ref, slope_ref, pad_ref, features_ref,
    grad_ref, out_ref,
    field_ref,
):
    info = place_of(slots)
    ring = Ring(slots, ext_in.shape[2], table_ref[...], info)
    halo_back(ring, side, ext_in, near_ref, far_ref, field_ref)
    for i in range(side):
        grad_ref[i] = (field_ref[i] * slope_ref[i].astype(F32)).astype(BF)
    columns = out_ref.shape[2]
    start = pl.multiple_of(info[4] * columns, columns)
    grad = grad_ref[:, :, pl.ds(start, columns)].reshape(side * side * slots, columns)

    weight_products(side, slots, pad_ref, features_ref, grad, 0, out_ref)


def back_kernel(side, slots, sends, grad_ref, table_ref, back_ref, ext_ref, *refs):
    send_ref = refs[0] if sends else None
    wide_ref, shifted_ref, west_ref, east_ref = refs[sends:]
    info = place_of(slots)
    clear_edges(wide_ref, side, slots)
    for i in range(side):
        put_gradient(wide_ref, shifted_ref, i, grad_ref[i].astype(F32), slots)
    ring = Ring(slots, ext_ref.shape[2], table_ref[...], info)
    convolved_back(
        ring, side, wide_ref, shifted_ref, back_ref, ext_ref, send_ref, west_ref, east_ref
    )


def last_kernel(
    side, slots, ext_in, near_ref, far_ref, table_ref, out_ref, field_ref, flat_ref
):
    info = place_of(slots)
    width = side * slots
    ring = Ring(slots, ext_in.shape[2], table_ref[...], info)
    halo_back(ring, side, ext_in, near_ref, far_ref, field_ref)
    for i in range(side):
        flat_ref[i * width : (i + 1) * width] = field_ref[i]
    out_ref[...] = flat_ref[pl.ds(info[0], side * side, stride=slots), :].astype(BF)


def weight_products(side, slots, pad_ref, ext_ref, grad, first, out_ref):
    width, channels = side * slots, out_ref.shape[1]
    lanes = pl.ds(first, channels)

    def step(dh, carry):
        rows = pl.ds(dh, side)
        window = jnp.concatenate(
            [
                pad_ref[rows, 0:width, lanes],
                ext_ref[rows, :, lanes],
                pad_ref[rows, 2 * slots : 2 * slots + width, lanes],
            ],
            axis=-1,
        ).reshape(side * width, 3 * channels)
        product = lax.dot_general(
            window, grad, (((0,), (0,)), ((), ())), preferred_element_type=F32
        ).astype(BF)
        for dw in range(3):
            out_ref[dh * 3 + dw] = product[dw * channels : (dw + 1) * channels]
        return carry

    lax.fori_loop(0, 3, step, 0)


def weight_kernel(side, slots, pad_ref, ext_ref, grad_ref, out_ref):
    info = place_of(slots)
    rows, columns = out_ref.shape[1:]
    start = pl.multiple_of(info[4] * columns, columns)
    grad = grad_ref[:, :, pl.ds(start, columns)].reshape(side * side * slots, columns)
    first = pl.multiple_of(info[5] * rows, rows)
    weight_products(side, slots, pad_ref, ext_ref, grad, first, out_ref)


def scale_kernel(slots, target, *refs):
    info = place_of(slots)
    blocks, (first_out, second_out, first_ref, second_ref, sems) = refs[:-5], refs[-5:]
    squared = jnp.zeros((1, 1), F32)
    for ref in blocks:
        value = ref[...].astype(F32)
        lanes = jnp.sum(jnp.sum(value * value, axis=0), axis=0, keepdims=True)
        squared = squared + jnp.sum(lanes, axis=1, keepdims=True)
    scale = target / jnp.sqrt(squared + 1e-06)

    def put(pair, to):
        for index, ref in enumerate(pair):
            core = info[4] if index == 0 else 1 - info[4]
            columns = ref.shape[2]
            lanes = pl.ds(pl.multiple_of(core * columns, columns), columns)
            to[:, :, lanes] = (ref[...].astype(F32) * scale).astype(BF)

    rows = blocks[2].shape[1]
    copies = []
    for index in range(3):
        if index == 0:
            source, to = first_ref, first_out
        else:
            half = info[5] if index == 1 else 1 - info[5]
            at = pl.ds(pl.multiple_of(half * rows, rows), rows)
            source, to = second_ref.at[index - 1], second_out.at[:, at, :]
        put(blocks[2 * index : 2 * index + 2], source)
        copies.append(pltpu.make_async_copy(source, to, sems.at[index]))
        copies[-1].start()
    for copy in copies:
        copy.wait()


def run(kernel, outs, args, scratch=(), flops=0, vmem_mib=8, to=pltpu.VMEM):
    vmem = pl.BlockSpec(memory_space=pltpu.VMEM)
    moved = sum(math.prod(x.shape) * x.dtype.itemsize for x in list(args) + list(outs))
    return pl.pallas_call(
        kernel,
        out_shape=tuple(outs),
        in_specs=[vmem] * len(args),
        out_specs=tuple(pl.BlockSpec(memory_space=to) for _ in outs),
        scratch_shapes=list(scratch),
        compiler_params=pltpu.CompilerParams(vmem_limit_bytes=vmem_mib * 1024 * 1024),
        cost_estimate=pl.CostEstimate(flops=flops, bytes_accessed=moved, transcendentals=0),
    )(*args)


def on_device(lon, lat, features, conv_first, conv_second, cotangent, edge_pick, edge_flip, corner_rule):
    side, c_in = features.shape[2], features.shape[4]
    half, c_out = cotangent.shape[2], cotangent.shape[4]
    slots, rings = 2 * lat, lon // 2
    width, padded = side * slots, (side + 2) * slots
    axes = ("lon", "lat")

    def spec(shape, dtype=BF):
        return jax.ShapeDtypeStruct(shape, dtype)

    def vmem(shape, dtype):
        return pltpu.VMEM(shape, dtype)

    def permuted(value, partner):
        pairs = []
        for place in range(lon):
            for band in range(lat):
                there = partner(place, band)
                pairs.append((place * lat + band, there[0] * lat + there[1]))
        return lax.ppermute(value, axes, pairs)

    def core_swap(value):
        return permuted(value, lambda place, band: (place, band ^ 1))

    def x_swap(value):
        return permuted(value, lambda place, band: (place, band ^ 2))

    ring_turns = rings.bit_length() - 1
    ring_pairs = rings == 1 << ring_turns
    ring_turns = ring_turns if ring_pairs else 1

    def ring_swap(value, turn):
        if not ring_pairs:
            total = 0.5 * lax.psum(value.astype(F32), "lon")
            return total - value.astype(F32)

        def partner(place, band):
            step = 1 << (turn if band % 2 == 0 else ring_turns - 1 - turn)
            return ((place % rings) ^ step) + place // rings * rings, band

        return permuted(value, partner)

    def summed(value, other):
        return (value.astype(F32) + other.astype(F32)).astype(BF)

    def beside(place, band):
        ring, upper = place % rings, place // rings
        east = (ring + band) % 2 == 0
        return ((ring + (1 if east else -1)) % rings + upper * rings, band)

    def exchange(value):
        near = permuted(value, beside)
        return near, core_swap(near)

    cells, quarter = side * side, half * half
    total = cells + 2 * quarter + 16
    cot = cotangent.reshape(quarter, c_out)

    def placed(value, row, lane=0):
        rows, lanes = value.shape
        edges = ((row, total - row - rows, 0), (lane, c_in - lane - lanes, 0))
        return lax.pad(value, jnp.zeros((), value.dtype), edges)

    flags, at = 0, 0
    for values in (edge_pick[0], edge_flip[0], corner_rule[0]):
        flags = flags + placed(values, total - 16, at)
        at += values.shape[1]
    own = placed(features.reshape(cells, c_in), 0) + flags.astype(BF)
    own = own + placed(cot, cells) + placed(cot, cells + quarter, -c_in)
    parts = [None] * slots
    parts[0] = own
    for index in [*range(lat, slots, 2), *range(2, lat, 2)]:
        parts[index] = permuted(
            own,
            lambda place, band, index=index: (
                (place + rings * (index // lat)) % lon,
                band ^ (index % lat),
            ),
        )
    for index in range(0, slots, 2):
        parts[index + 1] = core_swap(parts[index])

    first_weight = conv_first.reshape(3, 3 * c_in, c_out)
    second_weight = conv_second.reshape(3, 3 * c_out, c_out)

    features_ext, cot_ring, table, columns = run(
        functools.partial(collect_kernel, side, half, slots),
        [
            spec((side + 2, width, c_in)),
            spec((half * half * slots, c_out)),
            spec((slots, c_in), F32),
            spec((padded, c_in)),
        ],
        parts,
        [
            vmem((side * width, c_in), F32),
            vmem((half * half * slots, c_in), F32),
            vmem((half * half * slots, c_in), F32),
        ],
        flops=4_000_000_000,
    )
    near, far = exchange(columns)
    work = 2 * side * width * 9 * c_in * c_out
    features_pad, columns = run(
        functools.partial(edge_kernel, side, slots),
        [spec((side + 2, padded, c_in)), spec((padded, c_out))],
        [features_ext, near, far, table, first_weight],
        flops=work // 8,
    )
    near = permuted(columns, beside)
    act_ext, slope = run(
        functools.partial(first_kernel, side, slots),
        [spec((side + 2, width, c_out)), spec((side, width, c_out))],
        [features_ext, features_pad, table, first_weight],
        flops=work,
    )
    near, act_ext = lax.optimization_barrier((near, act_ext))
    far = core_swap(near)
    back_scratch = [
        vmem((side, (side + 4) * slots, c_out), BF),
        vmem((side, padded, c_out), BF),
    ]
    act_pad, columns = run(
        functools.partial(edge_back_kernel, side, slots),
        [spec((side + 2, padded, c_out)), spec((padded, c_out))],
        [act_ext, near, far, table, cot_ring, second_weight, conv_second],
        flops=work // 2,
    )
    near = permuted(columns, beside)
    second_grad, pooled = run(
        functools.partial(second_kernel, side, slots),
        [spec((side, width, c_out)), spec((half * half, c_out))],
        [act_ext, act_pad, cot_ring, second_weight],
        [vmem((c_out // 128, half * half * slots, 128), F32)],
        flops=2 * work,
    )
    part = c_out // 2
    second_sum = run(
        functools.partial(weight_kernel, side, slots),
        [spec((9, c_out // 2, part))],
        [act_pad, act_ext, second_grad],
        flops=work,
    )[0]
    near, second_sum, second_grad = lax.optimization_barrier((near, second_sum, second_grad))
    far = core_swap(near)
    second_other = ring_swap(second_sum, 0)
    act_grad = run(
        functools.partial(back_kernel, side, slots, 0),
        [spec((side + 2, width, c_out))],
        [second_grad, table, conv_second],
        back_scratch + [vmem((side + 2, slots, c_out), F32), vmem((side + 2, slots, c_out), F32)],
        flops=2 * work,
    )[0]
    pre_grad, first_sum = run(
        functools.partial(third_kernel, side, slots),
        [
            spec((side, width, c_out)),
            spec((9, c_in, part)),
        ],
        [act_grad, near, far, table, slope, features_pad, features_ext],
        [vmem((side, width, c_out), F32)],
        flops=work,
    )
    features_grad, columns = run(
        functools.partial(back_kernel, side, slots, 1),
        [spec((side + 2, width, c_in)), spec((padded, c_in))],
        [pre_grad, table, conv_first],
        back_scratch + [vmem((side + 2, slots, c_in), F32), vmem((side + 2, slots, c_in), F32)],
        flops=work,
    )
    second_other, columns = lax.optimization_barrier((second_other, columns))
    first_other = ring_swap(first_sum, 0)
    near = permuted(columns, beside)
    for turn in range(1, ring_turns):
        second_sum = summed(second_sum, second_other)
        second_other = ring_swap(second_sum, turn)
        first_sum = summed(first_sum, first_other)
        first_other = ring_swap(first_sum, turn)
    far = core_swap(near)
    input_grad = run(
        functools.partial(last_kernel, side, slots),
        [spec((side * side, c_in))],
        [features_grad, near, far, table],
        [vmem((side, width, c_in), F32), vmem((side * width, c_in), F32)],
    )[0]
    second_sum = summed(second_sum, second_other)
    first_other, input_grad = lax.optimization_barrier((first_other, input_grad))
    first_sum = summed(first_sum, first_other)
    blocks = []
    for block in (first_sum, second_sum, x_swap(second_sum)):
        blocks += [block, core_swap(block)]
    target = math.sqrt(9.0 * (c_in + c_out) * c_out)
    scaled_first, scaled_second = run(
        functools.partial(scale_kernel, slots, target),
        [spec((9, c_in, c_out)), spec((9, c_out, c_out))],
        blocks,
        [
            vmem((9, c_in, c_out), BF),
            vmem((2, 9, c_out // 2, c_out), BF),
            pltpu.SemaphoreType.DMA((3,)),
        ],
        to=pl.ANY,
    )
    return (
        pooled.reshape(1, 1, half, half, c_out),
        input_grad.reshape(1, 1, side, side, c_in),
        scaled_first.reshape(3, 3, c_in, c_out),
        scaled_second.reshape(3, 3, c_out, c_out),
    )


def solution(mesh):
    return jax.shard_map(
        functools.partial(on_device, mesh.shape["lon"], mesh.shape["lat"]),
        mesh=mesh,
        in_specs=(
            P("lon", "lat", None, None, None),
            P(),
            P(),
            P("lon", "lat", None, None, None),
            P("lon", "lat", None),
            P("lon", "lat", None),
            P("lon", "lat", None),
        ),
        out_specs=(P("lon", "lat", None, None, None), P("lon", "lat", None, None, None), P(), P()),
        check_vma=False,
    )
```

```python
import functools
import math

import jax
import jax.numpy as jnp
from jax import lax
from jax.experimental import pallas as pl
from jax.experimental.pallas import tpu as pltpu
from jax.sharding import PartitionSpec as P


BF = jnp.bfloat16
F32 = jnp.float32
ROWS_PER_STEP = 4


def normal_parts(z):
    cdf = 0.5 * (1.0 + lax.erf(z * (1.0 / math.sqrt(2.0))))
    pdf = jnp.exp(-0.5 * z * z) * (1.0 / math.sqrt(2.0 * math.pi))
    return cdf, pdf


class Ring:
    def __init__(self, slots, channels, table, info):
        self.slots, self.band = slots, slots // 2
        self.channels, self.info = channels, info
        place = lax.broadcasted_iota(jnp.int32, (slots, channels), 0)
        self.top = lax.rem(place, self.band) == self.band - 1
        self.bottom = lax.rem(place, self.band) == 0
        self.table = table

    def flag(self, column):
        return jnp.broadcast_to(self.table[:, column : column + 1], (self.slots, self.channels))

    def up(self, x):
        return pltpu.roll(x, self.slots - 1, 0)

    def down(self, x):
        return pltpu.roll(x, 1, 0)

    def across(self, x):
        return pltpu.roll(x, self.band, 0)

    def take(self, edges, side, to_source, to_slot):
        pick, flip = to_source(self.flag(side)), to_source(self.flag(2 + side))
        count = len(edges[0])
        chosen = [
            jnp.where(
                pick == 0.0,
                edges[0][j],
                jnp.where(
                    pick == 1.0, edges[1][j], jnp.where(pick == 2.0, edges[2][j], edges[3][j])
                ),
            )
            for j in range(count)
        ]
        return [
            to_slot(jnp.where(flip == 1.0, chosen[count - 1 - j], chosen[j])) for j in range(count)
        ]

    def halo_rows(self, edges):
        same = self.take(edges, 0, self.up, self.down)
        pole = self.take(edges, 0, self.across, self.across)
        south = [jnp.where(self.bottom, b, a) for a, b in zip(same, pole)]
        same = self.take(edges, 1, self.down, self.up)
        pole = self.take(edges, 1, self.across, self.across)
        north = [jnp.where(self.top, b, a) for a, b in zip(same, pole)]
        return south, north

    def give(self, totals, rows, side, to_source):
        pick, flip = to_source(self.flag(side)), to_source(self.flag(2 + side))
        count = len(rows)
        moved = [to_source(row) for row in rows]
        for j in range(count):
            value = jnp.where(flip == 1.0, moved[count - 1 - j], moved[j])
            for edge in range(4):
                share = jnp.where(pick == float(edge), value, 0.0)
                totals[edge][j] = share if totals[edge][j] is None else totals[edge][j] + share

    def halo_rows_back(self, south, north):
        totals = [[None] * len(south) for _ in range(4)]
        self.give(totals, [jnp.where(self.bottom, 0.0, x) for x in south], 0, self.up)
        self.give(totals, [jnp.where(self.bottom, x, 0.0) for x in south], 0, self.across)
        self.give(totals, [jnp.where(self.top, 0.0, x) for x in north], 1, self.down)
        self.give(totals, [jnp.where(self.top, x, 0.0) for x in north], 1, self.across)
        return totals

    def arrived(self, near_ref, far_ref):
        slots = self.slots
        near, far = near_ref[...].astype(F32), far_ref[...].astype(F32)
        to_east = self.info[3] == 1
        east, west = jnp.where(to_east, near, far), jnp.where(to_east, far, near)
        count = near.shape[0] // slots
        east = [east[i * slots : (i + 1) * slots] for i in range(count)]
        west = [west[i * slots : (i + 1) * slots] for i in range(count)]
        east = [jnp.where(self.info[1] == 1, self.across(x), x) for x in east]
        west = [jnp.where(self.info[2] == 1, self.across(x), x) for x in west]
        return east, west

    def packed(self, east_list, west_list, out_ref):
        east, west = jnp.concatenate(east_list, axis=0), jnp.concatenate(west_list, axis=0)
        out_ref[...] = jnp.where(self.info[3] == 1, east, west).astype(BF)


def place_of(slots):
    lat, rings = slots // 2, lax.axis_size("lon") // 2
    lon_at, lat_at = lax.axis_index("lon"), lax.axis_index("lat")
    ring_at, hemisphere = lax.rem(lon_at, rings), lax.div(lon_at, rings)
    core = lax.rem(lat_at, 2)
    return (
        hemisphere * lat + lat_at,
        (ring_at == rings - 1).astype(jnp.int32),
        (ring_at == 0).astype(jnp.int32),
        1 - lax.rem(ring_at + core, 2),
        core,
        lax.rem(lax.div(lat_at, 2), 2),
    )


def split_cells(row, slots):
    return [row[j * slots : (j + 1) * slots] for j in range(row.shape[0] // slots)]


def extend(ring, side, ext_ref):
    slots = ring.slots
    width = side * slots
    pair = 2 * slots
    first_col, last_col = [], []
    for i in range(side):
        first_col.append(ext_ref[1 + i, 0:pair].astype(F32)[:slots])
        last_col.append(ext_ref[1 + i, width - pair : width].astype(F32)[slots:])
    edges = [
        split_cells(ext_ref[1].astype(F32), slots),
        split_cells(ext_ref[side].astype(F32), slots),
        first_col,
        last_col,
    ]
    south, north = ring.halo_rows(edges)
    ext_ref[0] = jnp.concatenate(south, axis=0).astype(BF)
    ext_ref[side + 1] = jnp.concatenate(north, axis=0).astype(BF)
    return [south[-1]] + last_col + [north[-1]], [south[0]] + first_col + [north[0]]


def pad_columns(ring, side, ext_ref, near_ref, far_ref, pad_ref):
    slots = ring.slots
    width = side * slots
    east, west = ring.arrived(near_ref, far_ref)
    low, high = ext_ref[0].astype(F32), ext_ref[side + 1].astype(F32)
    blends = (
        (0, west, 0, 1, low[:slots]),
        (1, east, 0, 1, low[width - slots :]),
        (2, west, side + 1, side, high[:slots]),
        (3, east, side + 1, side, high[width - slots :]),
    )
    for corner, column, at, beside, along in blends:
        blended = (0.5 * (along + column[beside])).astype(BF).astype(F32)
        column[at] = jnp.where(ring.flag(4 + corner) == 1.0, blended, column[at])
    for i in range(side + 2):
        pad_ref[i] = jnp.concatenate([west[i], ext_ref[i].astype(F32), east[i]], axis=0).astype(BF)


def windows(pad_ref, ext_ref, start, rows, width, slots, channels):
    left = pad_ref[pl.ds(start, rows), 0:width, :]
    middle = ext_ref[pl.ds(start, rows), :, :]
    right = pad_ref[pl.ds(start, rows), 2 * slots : 2 * slots + width, :]
    return jnp.concatenate([left, middle, right], axis=-1).reshape(rows * width, 3 * channels)


def convolved(pad_ref, ext_ref, weight_ref, start, rows, width, slots, channels):
    total = None
    for dh in range(3):
        window = windows(pad_ref, ext_ref, start + dh, rows, width, slots, channels)
        part = jnp.dot(window, weight_ref[dh], preferred_element_type=F32)
        total = part if total is None else total + part
    return total


def clear_edges(wide_ref, side, slots):
    width = side * slots
    blank = jnp.zeros((side, 2 * slots, wide_ref.shape[2]), BF)
    wide_ref[:, 0 : 2 * slots] = blank
    wide_ref[:, width + 2 * slots :] = blank


def put_gradient(wide_ref, shifted_ref, row, value, slots):
    width = value.shape[0]
    wide_ref[row, 2 * slots : 2 * slots + width] = value.astype(BF)
    blank = jnp.zeros((slots, value.shape[1]), F32)
    shifted_ref[row] = jnp.concatenate([blank, value, blank], axis=0).astype(BF)


def convolved_back(
    ring, side, wide_ref, shifted_ref, weight_ref, out_ref, send_ref, west_ref, east_ref
):
    slots, channels = ring.slots, ring.channels
    width, padded = side * slots, (side + 2) * slots
    depth = wide_ref.shape[2]
    rows = ROWS_PER_STEP

    def finish(row, total):
        out_ref[row] = total[slots : slots + width].astype(BF)
        west_ref[row] = total[:slots].astype(BF).astype(F32)
        east_ref[row] = total[slots + width :].astype(BF).astype(F32)

    waiting = {}
    for start in range(0, side, rows):
        windows_back = (
            wide_ref[start : start + rows, 2 * slots : 2 * slots + padded, :],
            shifted_ref[start : start + rows, :, :],
            wide_ref[start : start + rows, 0:padded, :],
        )
        product = None
        for dw, window in enumerate(windows_back):
            part = lax.dot_general(
                window.reshape(rows * padded, depth),
                weight_ref[:, dw].reshape(3 * channels, depth),
                (((1,), (1,)), ((), ())),
                preferred_element_type=F32,
            )
            product = part if product is None else product + part
        for row in range(rows):
            for dh in range(3):
                part = product[
                    row * padded : (row + 1) * padded, dh * channels : (dh + 1) * channels
                ]
                at = start + row + dh
                waiting[at] = waiting[at] + part if at in waiting else part
        for at in sorted(waiting):
            if at < start + rows or start + rows == side:
                finish(at, waiting.pop(at))
    pair = 2 * slots
    for corner, column_ref, at, beside, is_east in (
        (0, west_ref, 0, 1, False),
        (1, east_ref, 0, 1, True),
        (2, west_ref, side + 1, side, False),
        (3, east_ref, side + 1, side, True),
    ):
        value = column_ref[at]
        blended = ring.flag(4 + corner) == 1.0
        half = jnp.where(blended, 0.5 * value, 0.0)
        column_ref[beside] = column_ref[beside] + half
        column_ref[at] = jnp.where(blended, 0.0, value)
        if is_east:
            old = out_ref[at, width - pair : width].astype(F32)
            new = jnp.concatenate([old[:slots], old[slots:] + half], axis=0)
            out_ref[at, width - pair : width] = new.astype(BF)
        else:
            old = out_ref[at, 0:pair].astype(F32)
            new = jnp.concatenate([old[:slots] + half, old[slots:]], axis=0)
            out_ref[at, 0:pair] = new.astype(BF)
    if send_ref is not None:
        ring.packed(
            [east_ref[i] for i in range(side + 2)], [west_ref[i] for i in range(side + 2)], send_ref
        )


def halo_back(ring, side, ext_ref, near_ref, far_ref, field_ref):
    slots = ring.slots
    width = side * slots
    east, west = ring.arrived(near_ref, far_ref)
    for i in range(side):
        field_ref[i] = ext_ref[1 + i].astype(F32)
    south = split_cells(ext_ref[0].astype(F32), slots)
    north = split_cells(ext_ref[side + 1].astype(F32), slots)
    south[0], south[-1] = south[0] + west[0], south[-1] + east[0]
    north[0], north[-1] = north[0] + west[-1], north[-1] + east[-1]
    low, high, first, last = ring.halo_rows_back(south, north)
    field_ref[0] += jnp.concatenate(low, axis=0)
    field_ref[side - 1] += jnp.concatenate(high, axis=0)
    for i in range(side):
        field_ref[i, 0:slots] += first[i] + west[1 + i]
        field_ref[i, width - slots : width] += last[i] + east[1 + i]


def collect_kernel(side, half, slots, *refs):
    info = place_of(slots)
    parts, (ext_ref, cot_ref, table_ref, send_ref), scratch = (
        refs[:slots],
        refs[slots : slots + 4],
        refs[slots + 4 :],
    )
    cells, cot_cells = side * side, half * half
    channels = ext_ref.shape[2]
    field_ref, low_ref, high_ref = scratch
    for index, part in enumerate(parts):
        slot = info[0] ^ index
        field_ref[pl.ds(slot, cells, stride=slots), :] = part[0:cells].astype(F32)
        low_ref[pl.ds(slot, cot_cells, stride=slots), :] = part[
            cells : cells + cot_cells
        ].astype(F32)
        high_ref[pl.ds(slot, cot_cells, stride=slots), :] = part[
            cells + cot_cells : cells + 2 * cot_cells
        ].astype(F32)
        flags = part[cells + 2 * cot_cells : cells + 2 * cot_cells + 16].astype(F32)
        table_ref[pl.ds(slot, 1), :] = flags[0:1]
    width = side * slots
    for i in range(side):
        ext_ref[1 + i] = field_ref[i * width : (i + 1) * width].astype(BF)
    cot_ref[:, 0:channels] = low_ref[0 : cot_cells * slots].astype(BF)
    cot_ref[:, channels : 2 * channels] = high_ref[0 : cot_cells * slots].astype(BF)
    ring = Ring(slots, channels, table_ref[...], info)
    ring.packed(*extend(ring, side, ext_ref), send_ref)


def edge_convolved(side, slots, pad_ref, weight_ref):
    channels, width = pad_ref.shape[2], side * slots
    left = pad_ref[:, 0 : 4 * slots].astype(F32)
    right = pad_ref[:, width - 2 * slots : width + 2 * slots].astype(F32)
    total = None
    for dh in range(3):
        taps = []
        for dw in range(3):
            at = dw * slots
            taps.append(
                jnp.concatenate(
                    [
                        left[dh : dh + side, at : at + slots],
                        right[dh : dh + side, at + slots : at + 2 * slots],
                    ],
                    axis=1,
                ).astype(BF)
            )
        window = jnp.concatenate(taps, axis=-1).reshape(side * 2 * slots, 3 * channels)
        part = jnp.dot(window, weight_ref[dh], preferred_element_type=F32)
        total = part if total is None else total + part
    return total


def edge_kernel(
    side, slots, ext_in, near_ref, far_ref, table_ref, weight_ref,
    pad_ref, send_ref,
):
    info = place_of(slots)
    ring = Ring(slots, ext_in.shape[2], table_ref[...], info)
    pad_columns(ring, side, ext_in, near_ref, far_ref, pad_ref)
    z = edge_convolved(side, slots, pad_ref, weight_ref)
    cdf, _ = normal_parts(z)
    act = (z * cdf).astype(BF).astype(F32)
    cells = split_cells(act, slots)
    first, last = cells[0::2], cells[1::2]
    ring = Ring(slots, act.shape[1], table_ref[...], info)
    south, north = ring.halo_rows(
        [
            [first[0], last[0]],
            [first[-1], last[-1]],
            [first[0], first[-1]],
            [last[0], last[-1]],
        ]
    )
    ring.packed([south[1]] + last + [north[1]], [south[0]] + first + [north[0]], send_ref)


def edge_back_kernel(
    side, slots, ext_in, near_ref, far_ref, table_ref, cot_ref, weight_ref, back_ref,
    pad_ref, send_ref,
):
    info = place_of(slots)
    channels, half = ext_in.shape[2], side // 2
    ring = Ring(slots, channels, table_ref[...], info)
    pad_columns(ring, side, ext_in, near_ref, far_ref, pad_ref)
    z = edge_convolved(side, slots, pad_ref, weight_ref)
    cdf, pdf = normal_parts(z)
    slope = split_cells(cdf + z * pdf, slots)
    line = half * slots
    columns = []
    for which in range(2):
        grads = []
        for row in range(half):
            if which == 0:
                cot = cot_ref[row * line : row * line + 2 * slots].astype(F32)[:slots]
            else:
                cot = cot_ref[(row + 1) * line - 2 * slots : (row + 1) * line].astype(F32)[slots:]
            for i in (2 * row, 2 * row + 1):
                grads.append(cot * 0.25 * slope[2 * i + which])
        product = lax.dot_general(
            jnp.concatenate(grads, axis=0).astype(BF),
            back_ref[:, 2 * which].reshape(3 * channels, channels),
            (((1,), (1,)), ((), ())),
            preferred_element_type=F32,
        )
        column = []
        for at in range(side + 2):
            total = None
            for dh in range(3):
                row = at - dh
                if 0 <= row < side:
                    part = product[
                        row * slots : (row + 1) * slots, dh * channels : (dh + 1) * channels
                    ]
                    total = part if total is None else total + part
            column.append(total.astype(BF).astype(F32))
        for corner, at, beside in ((which, 0, 1), (2 + which, side + 1, side)):
            blended = ring.flag(4 + corner) == 1.0
            value = column[at]
            column[beside] = column[beside] + jnp.where(blended, 0.5 * value, 0.0)
            column[at] = jnp.where(blended, 0.0, value)
        columns.append(column)
    ring.packed(columns[1], columns[0], send_ref)


def first_kernel(
    side, slots, ext_in, pad_ref, table_ref, weight_ref,
    ext_ref, slope_ref,
):
    channels, width = ext_in.shape[2], side * slots
    rows = ROWS_PER_STEP

    def step(index, carry):
        start = index * rows
        z = convolved(pad_ref, ext_in, weight_ref, start, rows, width, slots, channels)
        cdf, pdf = normal_parts(z)
        shape = (rows, width, z.shape[1])
        ext_ref[pl.ds(start + 1, rows)] = (z * cdf).astype(BF).reshape(shape)
        slope_ref[pl.ds(start, rows)] = (cdf + z * pdf).astype(BF).reshape(shape)
        return carry

    for index in range(side // rows):
        step(index, 0)
    extend(Ring(slots, ext_ref.shape[2], table_ref[...], None), side, ext_ref)


def second_kernel(
    side, slots, ext_in, pad_ref, cot_ref, weight_ref,
    grad_ref, pooled_ref,
    mean_ref,
):
    info = place_of(slots)
    channels, width = ext_in.shape[2], side * slots
    rows = ROWS_PER_STEP
    half = side // 2
    step_cells = (rows // 2) * half * slots

    def step(index, carry):
        start = index * rows
        z = convolved(pad_ref, ext_in, weight_ref, start, rows, width, slots, channels)
        cdf, pdf = normal_parts(z)
        paired = (rows // 2, 2, half, 2, slots, channels)
        value = (z * cdf).reshape(paired)
        cells = pl.ds(index * step_cells, step_cells)
        mean = (value[:, 0, :, 0] + value[:, 0, :, 1]) + (value[:, 1, :, 0] + value[:, 1, :, 1])
        mean = mean.reshape(step_cells, channels) * 0.25
        for block in range(channels // 128):
            mean_ref[block, cells, :] = mean[:, block * 128 : (block + 1) * 128]
        cot = cot_ref[cells, :].astype(F32) * 0.25
        cot = cot.reshape(rows // 2, 1, half, 1, slots, channels)
        slope = (cdf + z * pdf).reshape(paired)
        grad = (jnp.broadcast_to(cot, paired) * slope).reshape(rows, width, channels)
        grad_ref[pl.ds(start, rows)] = grad.astype(BF)
        return carry

    for index in range(side // rows):
        step(index, 0)
    for block in range(channels // 128):
        pooled_ref[:, block * 128 : (block + 1) * 128] = mean_ref[
            block, pl.ds(info[0], half * half, stride=slots), :
        ].astype(BF)


def third_kernel(
    side, slots, ext_in, near_ref, far_ref, table_ref, slope_ref, pad_ref, features_ref,
    grad_ref, out_ref,
    field_ref,
):
    info = place_of(slots)
    ring = Ring(slots, ext_in.shape[2], table_ref[...], info)
    halo_back(ring, side, ext_in, near_ref, far_ref, field_ref)
    for i in range(side):
        grad_ref[i] = (field_ref[i] * slope_ref[i].astype(F32)).astype(BF)
    columns = out_ref.shape[2]
    start = pl.multiple_of(info[4] * columns, columns)
    grad = grad_ref[:, :, pl.ds(start, columns)].reshape(side * side * slots, columns)

    weight_products(side, slots, pad_ref, features_ref, grad, 0, out_ref)


def back_kernel(side, slots, sends, grad_ref, table_ref, back_ref, ext_ref, *refs):
    send_ref = refs[0] if sends else None
    wide_ref, shifted_ref, west_ref, east_ref = refs[sends:]
    info = place_of(slots)
    clear_edges(wide_ref, side, slots)
    for i in range(side):
        put_gradient(wide_ref, shifted_ref, i, grad_ref[i].astype(F32), slots)
    ring = Ring(slots, ext_ref.shape[2], table_ref[...], info)
    convolved_back(
        ring, side, wide_ref, shifted_ref, back_ref, ext_ref, send_ref, west_ref, east_ref
    )


def last_kernel(
    side, slots, ext_in, near_ref, far_ref, table_ref, out_ref, field_ref, flat_ref
):
    info = place_of(slots)
    width = side * slots
    ring = Ring(slots, ext_in.shape[2], table_ref[...], info)
    halo_back(ring, side, ext_in, near_ref, far_ref, field_ref)
    for i in range(side):
        flat_ref[i * width : (i + 1) * width] = field_ref[i]
    out_ref[...] = flat_ref[pl.ds(info[0], side * side, stride=slots), :].astype(BF)


def weight_products(side, slots, pad_ref, ext_ref, grad, first, out_ref):
    width, channels = side * slots, out_ref.shape[1]
    lanes = pl.ds(first, channels)

    def step(dh, carry):
        rows = pl.ds(dh, side)
        window = jnp.concatenate(
            [
                pad_ref[rows, 0:width, lanes],
                ext_ref[rows, :, lanes],
                pad_ref[rows, 2 * slots : 2 * slots + width, lanes],
            ],
            axis=-1,
        ).reshape(side * width, 3 * channels)
        product = lax.dot_general(
            window, grad, (((0,), (0,)), ((), ())), preferred_element_type=F32
        ).astype(BF)
        for dw in range(3):
            out_ref[dh * 3 + dw] = product[dw * channels : (dw + 1) * channels]
        return carry

    lax.fori_loop(0, 3, step, 0)


def weight_kernel(side, slots, pad_ref, ext_ref, grad_ref, out_ref):
    info = place_of(slots)
    rows, columns = out_ref.shape[1:]
    start = pl.multiple_of(info[4] * columns, columns)
    grad = grad_ref[:, :, pl.ds(start, columns)].reshape(side * side * slots, columns)
    first = pl.multiple_of(info[5] * rows, rows)
    weight_products(side, slots, pad_ref, ext_ref, grad, first, out_ref)


def scale_kernel(slots, target, *refs):
    info = place_of(slots)
    blocks, (first_out, second_out, first_ref, second_ref, sems) = refs[:-5], refs[-5:]
    squared = jnp.zeros((1, 1), F32)
    for ref in blocks:
        value = ref[...].astype(F32)
        lanes = jnp.sum(jnp.sum(value * value, axis=0), axis=0, keepdims=True)
        squared = squared + jnp.sum(lanes, axis=1, keepdims=True)
    scale = target / jnp.sqrt(squared + 1e-06)

    def put(pair, to):
        for index, ref in enumerate(pair):
            core = info[4] if index == 0 else 1 - info[4]
            columns = ref.shape[2]
            lanes = pl.ds(pl.multiple_of(core * columns, columns), columns)
            to[:, :, lanes] = (ref[...].astype(F32) * scale).astype(BF)

    rows = blocks[2].shape[1]
    copies = []
    for index in range(3):
        if index == 0:
            source, to = first_ref, first_out
        else:
            half = info[5] if index == 1 else 1 - info[5]
            at = pl.ds(pl.multiple_of(half * rows, rows), rows)
            source, to = second_ref.at[index - 1], second_out.at[:, at, :]
        put(blocks[2 * index : 2 * index + 2], source)
        copies.append(pltpu.make_async_copy(source, to, sems.at[index]))
        copies[-1].start()
    for copy in copies:
        copy.wait()


def run(kernel, outs, args, scratch=(), flops=0, vmem_mib=8, to=pltpu.VMEM):
    vmem = pl.BlockSpec(memory_space=pltpu.VMEM)
    moved = sum(math.prod(x.shape) * x.dtype.itemsize for x in list(args) + list(outs))
    return pl.pallas_call(
        kernel,
        out_shape=tuple(outs),
        in_specs=[vmem] * len(args),
        out_specs=tuple(pl.BlockSpec(memory_space=to) for _ in outs),
        scratch_shapes=list(scratch),
        compiler_params=pltpu.CompilerParams(vmem_limit_bytes=vmem_mib * 1024 * 1024),
        cost_estimate=pl.CostEstimate(flops=flops, bytes_accessed=moved, transcendentals=0),
    )(*args)


def on_device(lon, lat, features, conv_first, conv_second, cotangent, edge_pick, edge_flip, corner_rule):
    side, c_in = features.shape[2], features.shape[4]
    half, c_out = cotangent.shape[2], cotangent.shape[4]
    slots, rings = 2 * lat, lon // 2
    width, padded = side * slots, (side + 2) * slots
    axes = ("lon", "lat")

    def spec(shape, dtype=BF):
        return jax.ShapeDtypeStruct(shape, dtype)

    def vmem(shape, dtype):
        return pltpu.VMEM(shape, dtype)

    def permuted(value, partner):
        pairs = []
        for place in range(lon):
            for band in range(lat):
                there = partner(place, band)
                pairs.append((place * lat + band, there[0] * lat + there[1]))
        return lax.ppermute(value, axes, pairs)

    def core_swap(value):
        return permuted(value, lambda place, band: (place, band ^ 1))

    def x_swap(value):
        return permuted(value, lambda place, band: (place, band ^ 2))

    ring_turns = rings.bit_length() - 1
    ring_pairs = rings == 1 << ring_turns
    ring_turns = ring_turns if ring_pairs else 1

    def ring_swap(value, turn):
        if not ring_pairs:
            total = 0.5 * lax.psum(value.astype(F32), "lon")
            return total - value.astype(F32)

        def partner(place, band):
            step = 1 << (turn if band % 2 == 0 else ring_turns - 1 - turn)
            return ((place % rings) ^ step) + place // rings * rings, band

        return permuted(value, partner)

    def summed(value, other):
        return (value.astype(F32) + other.astype(F32)).astype(BF)

    def beside(place, band):
        ring, upper = place % rings, place // rings
        east = (ring + band) % 2 == 0
        return ((ring + (1 if east else -1)) % rings + upper * rings, band)

    def exchange(value):
        near = permuted(value, beside)
        return near, core_swap(near)

    cells, quarter = side * side, half * half
    total = cells + 2 * quarter + 16
    cot = cotangent.reshape(quarter, c_out)

    def placed(value, row, lane=0):
        rows, lanes = value.shape
        edges = ((row, total - row - rows, 0), (lane, c_in - lane - lanes, 0))
        return lax.pad(value, jnp.zeros((), value.dtype), edges)

    flags, at = 0, 0
    for values in (edge_pick[0], edge_flip[0], corner_rule[0]):
        flags = flags + placed(values, total - 16, at)
        at += values.shape[1]
    own = placed(features.reshape(cells, c_in), 0) + flags.astype(BF)
    own = own + placed(cot, cells) + placed(cot, cells + quarter, -c_in)
    parts = [None] * slots
    parts[0] = own
    for index in [*range(lat, slots, 2), *range(2, lat, 2)]:
        parts[index] = permuted(
            own,
            lambda place, band, index=index: (
                (place + rings * (index // lat)) % lon,
                band ^ (index % lat),
            ),
        )
    for index in range(0, slots, 2):
        parts[index + 1] = core_swap(parts[index])

    first_weight = conv_first.reshape(3, 3 * c_in, c_out)
    second_weight = conv_second.reshape(3, 3 * c_out, c_out)

    features_ext, cot_ring, table, columns = run(
        functools.partial(collect_kernel, side, half, slots),
        [
            spec((side + 2, width, c_in)),
            spec((half * half * slots, c_out)),
            spec((slots, c_in), F32),
            spec((padded, c_in)),
        ],
        parts,
        [
            vmem(((side * side + 1) * slots, c_in), F32),
            vmem(((half * half + 1) * slots, c_in), F32),
            vmem(((half * half + 1) * slots, c_in), F32),
        ],
        flops=4_000_000_000,
    )
    near, far = exchange(columns)
    work = 2 * side * width * 9 * c_in * c_out
    features_pad, columns = run(
        functools.partial(edge_kernel, side, slots),
        [spec((side + 2, padded, c_in)), spec((padded, c_out))],
        [features_ext, near, far, table, first_weight],
        flops=work // 8,
    )
    near = permuted(columns, beside)
    act_ext, slope = run(
        functools.partial(first_kernel, side, slots),
        [spec((side + 2, width, c_out)), spec((side, width, c_out))],
        [features_ext, features_pad, table, first_weight],
        flops=work,
    )
    near, act_ext = lax.optimization_barrier((near, act_ext))
    far = core_swap(near)
    back_scratch = [
        vmem((side, (side + 4) * slots, c_out), BF),
        vmem((side, padded, c_out), BF),
    ]
    act_pad, columns = run(
        functools.partial(edge_back_kernel, side, slots),
        [spec((side + 2, padded, c_out)), spec((padded, c_out))],
        [act_ext, near, far, table, cot_ring, second_weight, conv_second],
        flops=work // 2,
    )
    near = permuted(columns, beside)
    second_grad, pooled = run(
        functools.partial(second_kernel, side, slots),
        [spec((side, width, c_out)), spec((half * half, c_out))],
        [act_ext, act_pad, cot_ring, second_weight],
        [vmem((c_out // 128, (half * half + 1) * slots, 128), F32)],
        flops=2 * work,
    )
    part = c_out // 2
    second_sum = run(
        functools.partial(weight_kernel, side, slots),
        [spec((9, c_out // 2, part))],
        [act_pad, act_ext, second_grad],
        flops=work,
    )[0]
    near, second_sum, second_grad = lax.optimization_barrier((near, second_sum, second_grad))
    far = core_swap(near)
    second_other = ring_swap(second_sum, 0)
    act_grad = run(
        functools.partial(back_kernel, side, slots, 0),
        [spec((side + 2, width, c_out))],
        [second_grad, table, conv_second],
        back_scratch + [vmem((side + 2, slots, c_out), F32), vmem((side + 2, slots, c_out), F32)],
        flops=2 * work,
    )[0]
    pre_grad, first_sum = run(
        functools.partial(third_kernel, side, slots),
        [
            spec((side, width, c_out)),
            spec((9, c_in, part)),
        ],
        [act_grad, near, far, table, slope, features_pad, features_ext],
        [vmem((side, width, c_out), F32)],
        flops=work,
    )
    features_grad, columns = run(
        functools.partial(back_kernel, side, slots, 1),
        [spec((side + 2, width, c_in)), spec((padded, c_in))],
        [pre_grad, table, conv_first],
        back_scratch + [vmem((side + 2, slots, c_in), F32), vmem((side + 2, slots, c_in), F32)],
        flops=work,
    )
    second_other, columns = lax.optimization_barrier((second_other, columns))
    first_other = ring_swap(first_sum, 0)
    near = permuted(columns, beside)
    for turn in range(1, ring_turns):
        second_sum = summed(second_sum, second_other)
        second_other = ring_swap(second_sum, turn)
        first_sum = summed(first_sum, first_other)
        first_other = ring_swap(first_sum, turn)
    far = core_swap(near)
    input_grad = run(
        functools.partial(last_kernel, side, slots),
        [spec((side * side, c_in))],
        [features_grad, near, far, table],
        [vmem((side, width, c_in), F32), vmem(((side * side + 1) * slots, c_in), F32)],
    )[0]
    second_sum = summed(second_sum, second_other)
    first_other, input_grad = lax.optimization_barrier((first_other, input_grad))
    first_sum = summed(first_sum, first_other)
    blocks = []
    for block in (first_sum, second_sum, x_swap(second_sum)):
        blocks += [block, core_swap(block)]
    target = math.sqrt(9.0 * (c_in + c_out) * c_out)
    scaled_first, scaled_second = run(
        functools.partial(scale_kernel, slots, target),
        [spec((9, c_in, c_out)), spec((9, c_out, c_out))],
        blocks,
        [
            vmem((9, c_in, c_out), BF),
            vmem((2, 9, c_out // 2, c_out), BF),
            pltpu.SemaphoreType.DMA((3,)),
        ],
        to=pl.ANY,
    )
    return (
        pooled.reshape(1, 1, half, half, c_out),
        input_grad.reshape(1, 1, side, side, c_in),
        scaled_first.reshape(3, 3, c_in, c_out),
        scaled_second.reshape(3, 3, c_out, c_out),
    )


def solution(mesh):
    return jax.shard_map(
        functools.partial(on_device, mesh.shape["lon"], mesh.shape["lat"]),
        mesh=mesh,
        in_specs=(
            P("lon", "lat", None, None, None),
            P(),
            P(),
            P("lon", "lat", None, None, None),
            P("lon", "lat", None),
            P("lon", "lat", None),
            P("lon", "lat", None),
        ),
        out_specs=(P("lon", "lat", None, None, None), P("lon", "lat", None, None, None), P(), P()),
        check_vma=False,
    )
```
